32 devices in a mesh: dp: 8 (over y, x, core), tensor: 4 (over z).
Axes of the slice: x: 2, y: 2, z: 4, core: 2. Of those that a mesh axis runs over, the one named last changes fastest.
Arguments:
- block_input: float32 [16, 680, 1024], P('dp', 'tensor'), may hold values from -6 to 6
- cotangent: float32 [16, 680, 1024], P('dp', 'tensor'), may hold values from -6 to 6
- class_ids: int32 [16], replicated, may hold values from 0 to 1023
- scale_ids: int32 [16, 680], P('dp'), may hold values from 0 to 9, never falling along the last dimension, each value on 1 to 256 neighbouring positions
- class_table: bfloat16 [1024, 1024], P('dp', 'tensor'), may hold values from -6 to 6
- w_ada: bfloat16 [1024, 6, 1024], P('tensor', None, 'dp'), may hold values from -0.1875 to 0.1875
- b_ada: bfloat16 [6, 1024], P(None, 'dp'), may hold values from -4 to 4
- query_key_value_weight: bfloat16 [3, 1024, 1024], P(None, 'dp', 'tensor'), may hold values from -0.1875 to 0.1875
- qv_bias: bfloat16 [2, 16, 64], P(None, 'tensor', 'dp'), may hold values from -6 to 6
- q_gain: bfloat16 [16, 64], P('tensor', 'dp'), may hold values from 8 to 24
- output_projection: bfloat16 [1024, 1024], P('tensor', 'dp'), may hold values from -0.75 to 0.75
- up_weight: bfloat16 [1024, 4096], P('dp', 'tensor'), may hold values from -0.1875 to 0.1875
- hidden_bias: bfloat16 [64, 64], P('tensor', 'dp'), may hold values from -6 to 6
- down_weight: bfloat16 [4096, 1024], P('tensor', 'dp'), may hold values from -0.09375 to 0.09375
- projection_bias: bfloat16 [2, 1024], P(None, 'dp'), may hold values from -6 to 6
Outputs:
- block_output: float32 [16, 680, 1024], P('dp', 'tensor')
- input_grad: float32 [16, 680, 1024], P('dp', 'tensor')
- table_grad: float32 [1024, 1024], P('dp', 'tensor')
- w_ada_grad: float32 [1024, 6, 1024], P('tensor', None, 'dp')
- b_ada_grad: float32 [6, 1024], P(None, 'dp')
- w_qkv_grad: float32 [3, 1024, 1024], P(None, 'dp', 'tensor')
- qv_bias_grad: float32 [2, 16, 64], P(None, 'tensor', 'dp')
- q_gain_grad: float32 [16, 64], P('tensor', 'dp')
- w_proj_grad: float32 [1024, 1024], P('tensor', 'dp')
- w_fc1_grad: float32 [1024, 4096], P('dp', 'tensor')
- b_fc1_grad: float32 [64, 64], P('tensor', 'dp')
- w_fc2_grad: float32 [4096, 1024], P('tensor', 'dp')
- b_out_grad: float32 [2, 1024], P(None, 'dp')
The draws below stay inside these ranges and needn't reach their ends.
Inputs may be any that keep to these rules, and one draw needn't show every extreme that they name: `scale_ids`: in each sequence the scale ids never fall, every one of the 10 scales holds 1 to 256 tokens, and some scale holds exactly 256.
All inputs are finite; a program needn't handle non-finite values.
Results may differ from the reference program's by a relative error of at most 0.015.
Values may be sent and summed in bfloat16 or wider, within the bound.
A program may use at most 192 MiB of HBM per device.

```python
import math
import jax
import jax.numpy as jnp
import numpy as np
from jax import lax

D = 1024
H = 16
HD = 64
FF = 4096
CLASSES = 1024
L = 680
SCALES = 10
SCALE_MOST = 256
MICRO = 2
SEQ_DEV = 1
SEQS = 16


def with_ends(array, rng, low, high):
    longest = array.shape.index(max(array.shape))
    spots = []
    for shift in (0, 1):
        where = [jax.random.randint(jax.random.fold_in(rng, axis), (), 0, length) for axis, length in enumerate(array.shape)]
        where[longest] = (where[longest] + shift) % array.shape[longest]
        spots.append(tuple(where))
    return array.at[spots[0]].set(low).at[spots[1]].set(high)


def level_of(rng, extent, split, least, high):
    def one(dim, parts):
        draws = jax.random.uniform(jax.random.fold_in(jax.random.fold_in(rng, 6), dim), (parts,), jnp.float32, least / len(split), high / len(split))
        return jnp.repeat(jnp.exp(draws), extent[dim] // parts).reshape((-1,) + (1,) * (len(extent) - dim - 1))

    gain = one(*split[0])
    for cut in split[1:]:
        gain = gain * one(*cut)
    return gain


def profile(number_of, total, limit, lean):
    weights = [(1 << 20) // math.isqrt(rank ** lean) + 1 for rank in range(2, number_of + 1)]
    surplus, counts = total - limit - (number_of - 1), [1] * (number_of - 1)
    while surplus > 0:
        movable = [i for i in range(number_of - 1) if counts[i] < limit]
        whole, left = sum([weights[i] for i in movable]), surplus
        for i in movable:
            more = min(limit - counts[i], max(1, left * weights[i] // whole), surplus)
            counts[i] = counts[i] + more
            surplus = surplus - more
    return np.array([limit] + counts)


def uneven(own_key, number_of, total, bound, skew):
    if number_of == 2:
        one = jax.random.randint(own_key, (), max(1, total - bound), min(bound, total - 1) + 1)
        return jnp.stack([one, total - one])
    lengths = jnp.asarray(profile(number_of, total, bound, skew), jnp.int32)
    twos = (number_of - 1) // 2
    giver, receiver = lengths[1:1 + 2 * twos:2], lengths[2:2 + 2 * twos:2]
    slack = jnp.minimum(giver - 1, bound - receiver)
    moved = jax.random.randint(jax.random.fold_in(own_key, 1), (twos,), 0, 1 << 20) % (slack + 1)
    lengths = lengths.at[1:1 + 2 * twos:2].set(giver - moved).at[2:2 + 2 * twos:2].set(receiver + moved)
    return lengths[jax.random.permutation(jax.random.fold_in(own_key, 2), number_of)]


def noise(rng, dims, scale, limit, pieces=(), dtype=jnp.bfloat16):
    gain = level_of(rng, dims, pieces, -0.22, 0.18) if pieces else 1.0
    values = jax.random.normal(rng, dims, jnp.float32) * scale * gain
    return jnp.minimum(jnp.maximum(values, -limit), limit).astype(dtype)


def setup_inputs(seed: int = 0) -> dict:
    key_list = jax.random.split(jax.random.key(seed), 16)
    return {
        "block_input": noise(key_list[0], (SEQS, L, D), 1.0, 6.0, ((0, 8), (1, 4)), jnp.float32),
        "cotangent": noise(key_list[1], (SEQS, L, D), 1.0, 6.0, ((0, 8), (1, 4)), jnp.float32),
        "class_ids": with_ends(jax.random.randint(key_list[2], (SEQS,), 0, CLASSES), jax.random.fold_in(key_list[2], 1), 0, CLASSES - 1).astype(jnp.int32),
        "scale_ids": jax.vmap(lambda own: jnp.searchsorted(jnp.cumsum(uneven(own, SCALES, L, SCALE_MOST, 0)), jnp.arange(L), side="right"))(jax.random.split(key_list[3], SEQS)).reshape((SEQS, L)).astype(jnp.int32),
        "class_table": noise(key_list[4], (CLASSES, D), 1.0, 6.0, ((0, 8), (1, 4))),
        "w_ada": noise(key_list[5], (D, 6, D), D ** -0.5, 0.1875, ((0, 4), (2, 8))),
        "b_ada": noise(key_list[6], (6, D), 0.3, 4.0, ((1, 8),)),
        "query_key_value_weight": noise(key_list[7], (3, D, D), D ** -0.5, 0.1875, ((1, 8), (2, 4))),
        "qv_bias": noise(key_list[8], (2, H, HD), 0.5, 6.0, ((1, 4), (2, 8))),
        "q_gain": jnp.clip(jnp.exp(math.log(24.0) - 1.0986123 * jax.random.uniform(key_list[9], (H, HD), jnp.float32) ** level_of(key_list[9], (H, HD), ((0, 4), (1, 8)), -0.2, 0.2)), 8.0, 24.0).astype(jnp.bfloat16),
        "output_projection": noise(key_list[10], (D, D), (D // 16) ** -0.5, 0.75, ((0, 4), (1, 8))),
        "up_weight": noise(key_list[11], (D, FF), D ** -0.5, 0.1875, ((0, 8), (1, 4))),
        "hidden_bias": noise(key_list[12], (FF // HD, HD), 0.5, 6.0, ((0, 4), (1, 8))),
        "down_weight": noise(key_list[13], (FF, D), FF ** -0.5, 0.09375, ((0, 4), (1, 8))),
        "projection_bias": noise(key_list[14], (2, D), 0.5, 6.0, ((1, 8),)),
    }


highest_precision = lax.Precision.HIGHEST

@jax.custom_vjp
def low(v):
    return lax.optimization_barrier(v.astype(jnp.bfloat16)).astype(jnp.float32)

@jax.custom_vjp
def low_back(v):
    return v

def low_keep(v):
    return (low(v), None)

def low_pass(kept, grad):
    return (grad,)

def back_keep(v):
    return (v, None)

def back_low(kept, grad):
    return (low(grad),)
low.defvjp(low_keep, low_pass)
low_back.defvjp(back_keep, back_low)

def modulate(tokens, scale_in, shift_in):
    centred = tokens - lax.optimization_barrier(jnp.mean(tokens, axis=-1, keepdims=True))
    spread = lax.optimization_barrier(jnp.mean(centred * centred, axis=-1, keepdims=True))
    return centred * lax.rsqrt(spread + 1e-06) * (1.0 + scale_in) + shift_in

def gelu_tanh(values):
    return jax.nn.gelu(values, approximate=True)

def forward(params, tokens, labels, scale_rows):
    class_table, w_ada, b_ada, query_key_value_weight, qv_bias, q_gain, output_projection, up_weight, hidden_bias, down_weight, projection_bias = params
    seq_count, length, breadth = tokens.shape
    head_count, head_size = q_gain.shape
    shaped = (seq_count, length, head_count, head_size)
    cond = jnp.take(class_table, labels, axis=0)
    silu_low = low(jax.nn.silu(cond))
    modulation = low_back(jnp.einsum('sc,cjd->sjd', silu_low, w_ada, precision=highest_precision) + b_ada)
    rows_mod = [modulation[:, number][:, None, :] for number in range(6)]
    first_residual = low(modulate(tokens, rows_mod[2], rows_mod[4]))
    query_key_value_rows = jnp.einsum('zug,hgn->hzun', first_residual, query_key_value_weight, precision=highest_precision)
    queries = low_back(query_key_value_rows[0] + qv_bias[0].reshape(-1)).reshape(shaped)
    key_rows = low_back(query_key_value_rows[1]).reshape(shaped)
    value_rows = low_back(query_key_value_rows[2] + qv_bias[1].reshape(-1)).reshape(shaped)
    q_hat = queries * lax.rsqrt(lax.optimization_barrier(jnp.sum(queries * queries, axis=-1, keepdims=True)) + 1e-06)
    k_hat = key_rows * lax.rsqrt(lax.optimization_barrier(jnp.sum(key_rows * key_rows, axis=-1, keepdims=True)) + 1e-06)
    q_low = low(q_hat * q_gain)
    k_low = low(k_hat)
    v_low = low(value_rows)
    scores = low_back(jnp.einsum('sqhd,skhd->shqk', q_low, k_low, precision=highest_precision))
    allowed = (scale_rows[:, :, None] >= scale_rows[:, None, :])[:, None]
    scores = jnp.where(allowed, scores, -1e+30)
    peak = lax.optimization_barrier(jnp.max(scores, axis=-1, keepdims=True))
    expo_vals = jnp.exp(scores - peak)
    weights = expo_vals / lax.optimization_barrier(jnp.sum(expo_vals, axis=-1, keepdims=True))
    mixed = jnp.einsum('shqk,skhd->sqhd', low(weights), v_low, precision=highest_precision)
    attention_result = low(low_back(mixed)).reshape(seq_count, length, breadth)
    branch_output = low_back(jnp.einsum('yxi,it->yxt', attention_result, output_projection, precision=highest_precision) + projection_bias[0])
    middle = tokens + rows_mod[0] * branch_output
    second_residual = low(modulate(middle, rows_mod[3], rows_mod[5]))
    hidden_units = low_back(jnp.einsum('ahi,ir->ahr', second_residual, up_weight, precision=highest_precision) + hidden_bias.reshape(-1))
    activation_lowprec = low(gelu_tanh(hidden_units))
    feedforward_output = low_back(jnp.einsum('xmt,ti->xmi', activation_lowprec, down_weight, precision=highest_precision) + projection_bias[1])
    return middle + rows_mod[1] * feedforward_output

def reference(block_input, cotangent, class_ids, scale_ids, class_table, w_ada, b_ada, query_key_value_weight, qv_bias, q_gain, output_projection, up_weight, hidden_bias, down_weight, projection_bias):
    params = tuple((entry.astype(jnp.float32) for entry in (class_table, w_ada, b_ada, query_key_value_weight, qv_bias, q_gain, output_projection, up_weight, hidden_bias, down_weight, projection_bias)))
    group_size = MICRO * SEQ_DEV
    step_count = SEQS // group_size
    token_groups = block_input.reshape(step_count, group_size, L, D)
    grad_groups = cotangent.reshape(step_count, group_size, L, D)
    label_groups = class_ids.reshape(step_count, group_size)
    scale_groups = scale_ids.reshape(step_count, group_size, L)

    def one_step(totals, inputs):
        tokens, grads_out, labels, scale_rows = inputs
        result, pullback = jax.vjp(lambda weights_in, data_in: forward(weights_in, data_in, labels, scale_rows), params, tokens)
        weight_grads, data_grad = pullback(grads_out)
        return (jax.tree.map(jnp.add, totals, weight_grads), (result, data_grad))
    zeros_init = jax.tree.map(jnp.zeros_like, params)
    totals, (results, data_grads) = lax.scan(one_step, zeros_init, (token_groups, grad_groups, label_groups, scale_groups))
    return (results.reshape(SEQS, L, D), data_grads.reshape(SEQS, L, D), totals[0], totals[1], totals[2], totals[3], totals[4], totals[5], totals[6], totals[7], totals[8], totals[9], totals[10])
```

```python
import functools

import jax
import jax.numpy as jnp
from jax import lax
from jax.experimental import pallas as pl
from jax.experimental.pallas import tpu as pltpu
from jax.sharding import PartitionSpec as P

MESH = pl.DeviceIdType.MESH
F32, B16 = jnp.float32, jnp.bfloat16
GROUPS = 3
CHUNK = 256
EPS = 1e-06
FAR = 256.0


def dot(a, b):
    return lax.dot_general(a, b, (((1,), (0,)), ((), ())), preferred_element_type=F32)


def dot_nt(a, b):
    return lax.dot_general(a, b, (((1,), (1,)), ((), ())), preferred_element_type=F32)


def dot_tn(a, b):
    return lax.dot_general(a, b, (((0,), (0,)), ((), ())), preferred_element_type=F32)


def split_dot(a, b):
    high = a.astype(B16)
    low = (a - high.astype(F32)).astype(B16)
    return dot(high, b) + dot(low, b)


def row_sum(a):
    return jnp.sum(a, axis=0, keepdims=True)


class Dims:
    def __init__(self, dp, tensor, rows, width, head, hidden):
        self.T = tensor
        self.NC = dp // 2
        self.bits = self.NC.bit_length() - 1
        self.Q = rows
        self.M = rows * tensor
        self.D = width
        self.hd = head
        self.hq = width // tensor // 2
        self.fu = hidden // tensor // 2
        self.R = width // dp
        self.C = 4 * self.hq + 2 * self.fu
        self.off = (0, 4 * self.hq, 4 * self.hq + self.fu)
        self.wide = (4 * self.hq, self.fu, self.fu)
        self.NCH = width // CHUNK
        assert 1 << self.bits == self.NC


def block_kernel(
    dm,
    ws, xb, dyb, mods, hp, hb, psi, phi,
    fin, outd, gind, sums, hsum, fsum,
    wall, xs, dys, h1, h2, qs, ks, vs, rq, rk, linv, o, ol, ab, n2, r2, g, gp,
    send, recv, df, xt, do, dqkv, od, rb0, rb1, zb, fbuf,
    c_s, c_r, c_l, z_s, z_r, p_s, p_r, x_s, x_r, x_l, x_f,
    e_s, e_r, rs_s, rs_r, rz_s, rz_r, f_s, f_r, o_s, o_r, o_l,
):
    T, NB, Q, M, D, R, C = dm.T, dm.bits, dm.Q, dm.M, dm.D, dm.R, dm.C
    hq, fu, NCH = dm.hq, dm.fu, dm.NCH
    TH = T // 2
    dpi = lax.axis_index("dp")
    me_z = lax.axis_index("tensor")
    core = lax.rem(dpi, 2)
    chip = dpi // 2
    mybit = [lax.rem(chip // (1 << b), 2) for b in range(NB)]
    partner = (dpi + 1 - 2 * core, me_z)

    def z_dev(off):
        return (dpi, lax.rem(me_z + off, T))

    def bit_dev(b):
        return (dpi + (1 - 2 * mybit[b]) * (2 << b), me_z)

    bar = pltpu.get_barrier_semaphore()
    friends = [partner] + [z_dev(k) for k in range(1, T)] + [bit_dev(b) for b in range(NB)]
    for dev in friends:
        pl.semaphore_signal(bar, inc=1, device_id=dev, device_id_type=MESH)
    pl.semaphore_wait(bar, len(friends))

    def rdma(src, dst, ss, rs, dev):
        return pltpu.make_async_remote_copy(
            src_ref=src, dst_ref=dst, send_sem=ss, recv_sem=rs, device_id=dev, device_id_type=MESH
        )

    every = slice(None)

    def place(fixed):
        return tuple(fixed.get(b, every) for b in reversed(range(NB)))

    mine = place({b: mybit[b] for b in range(NB)})

    def cols(grp):
        return pl.ds(dm.off[grp], dm.wide[grp])

    def core_copy(grp):
        src = ws.at[1 - core, :, cols(grp)]
        dst = wall.at[(me_z,) + mine + (pl.ds(pl.multiple_of(core * R, R), R), cols(grp))]
        return rdma(src, dst, c_s.at[grp], c_r.at[grp], partner)

    def core_local(grp):
        src = ws.at[core, :, cols(grp)]
        dst = wall.at[(me_z,) + mine + (pl.ds(pl.multiple_of(core * R, R), R), cols(grp))]
        return pltpu.make_async_copy(src, dst, c_l.at[grp])

    def core_wait(grp):
        core_local(grp).wait()
        other = wall.at[(me_z,) + mine + (pl.ds(pl.multiple_of((1 - core) * R, R), R), cols(grp))]
        rdma(other, other, c_s.at[grp], c_r.at[grp], partner).wait_recv()

    def z_copy(grp, off):
        part = wall.at[(me_z,) + mine + (every, cols(grp))]
        return rdma(part, part, z_s.at[grp, off - 1], z_r.at[grp, off - 1], z_dev(off))

    def z_start(grp):
        for off in range(1, T):
            z_copy(grp, off).start()

    def z_wait(grp):
        for off in range(1, T):
            part = wall.at[(lax.rem(me_z - off + T, T),) + mine + (every, cols(grp))]
            rdma(part, part, z_s.at[grp, off - 1], z_r.at[grp, off - 1], z_dev(off)).wait_recv()

    order = [list(range(NB)), list(reversed(range(NB)))]

    def half_z(h):
        return pl.ds(h * TH, TH)

    def p_copy(grp, step, h, landing):
        b = order[h][step]
        fixed = {k: mybit[k] for k in order[h][step:]}
        if landing:
            fixed[b] = 1 - mybit[b]
        part = wall.at[(half_z(h),) + place(fixed) + (every, cols(grp))]
        return rdma(part, part, p_s.at[grp, step, h], p_r.at[grp, step, h], bit_dev(b))

    def p_start(grp, step):
        for h in range(2):
            p_copy(grp, step, h, False).start()

    def p_wait(grp, step):
        for h in range(2):
            p_copy(grp, step, h, True).wait_recv()

    def gather_sent(grp):
        core_copy(grp).wait_send()
        for off in range(1, T):
            z_copy(grp, off).wait_send()
        for step in range(NB):
            for h in range(2):
                p_copy(grp, step, h, False).wait_send()

    owner = me_z // 2 == core

    def tok_copy(which, src, dst, i):
        zt = 2 * core + i
        return rdma(src.at[i], dst.at[me_z], x_s.at[which, i], x_r.at[which, me_z], (dpi, zt))

    def tok_start(which, src, dst):
        for i in range(2):
            @pl.when(2 * core + i != me_z)
            def _():
                tok_copy(which, src, dst, i).start()

            @pl.when(2 * core + i == me_z)
            def _():
                pltpu.make_async_copy(src.at[i], dst.at[me_z], x_l.at[which]).start()

    def tok_forward(which, dst):
        return rdma(dst, dst, x_f.at[which, 0], x_f.at[which, 1], partner)

    def tok_wait(which, src, dst):
        @pl.when(owner)
        def _():
            for off in range(1, T):
                zq = lax.rem(me_z + off, T)
                rdma(dst.at[zq], dst.at[zq], x_s.at[which, 0], x_r.at[which, zq], (dpi, zq)).wait_recv()
            pltpu.make_async_copy(src.at[0], dst.at[me_z], x_l.at[which]).wait()
            tok_forward(which, dst).start()

        @pl.when(jnp.logical_not(owner))
        def _():
            tok_forward(which, dst).wait_recv()

    def tok_sent(which, src, dst):
        for i in range(2):
            @pl.when(2 * core + i != me_z)
            def _():
                tok_copy(which, src, dst, i).wait_send()

        @pl.when(owner)
        def _():
            tok_forward(which, dst).wait_send()

    back_from = (od, h2)

    def back_copy(which, dst, zq):
        return rdma(back_from[which].at[zq], dst.at[lax.rem(me_z, 2)], o_s.at[which, zq], o_r.at[which, lax.rem(me_z, 2)], (dpi, zq))

    def back_start(which, dst):
        @pl.when(owner)
        def _():
            for off in range(1, T):
                back_copy(which, dst, lax.rem(me_z + off, T)).start()
            pltpu.make_async_copy(back_from[which].at[me_z], dst.at[lax.rem(me_z, 2)], o_l.at[which]).start()

    def back_wait(which, dst):
        @pl.when(owner)
        def _():
            for off in range(1, T):
                back_copy(which, dst, lax.rem(me_z + off, T)).wait_send()
            pltpu.make_async_copy(back_from[which].at[me_z], dst.at[lax.rem(me_z, 2)], o_l.at[which]).wait()

        for i in range(2):
            @pl.when(2 * core + i != me_z)
            def _():
                rdma(dst.at[i], dst.at[i], o_s.at[which, 0], o_r.at[which, i], (dpi, 2 * core + i)).wait_recv()

    def x_copy(k, n):
        return rdma(send.at[n], recv.at[k % 2, n], e_s.at[k, n], e_r.at[k, n], partner)

    def exchange(k, n, value):
        send[n] = value.astype(B16).reshape(T, Q, CHUNK)
        x_copy(k, n).start()

    def exchange_wait(k):
        for n in range(NCH):
            x_copy(k, n).wait_recv()

    def exchange_sent(k):
        for n in range(NCH):
            x_copy(k, n).wait_send()

    def both(k, t):
        parts = [send[n, t].astype(F32) + recv[k % 2, n, t].astype(F32) for n in range(NCH)]
        return jnp.concatenate(parts, axis=-1)

    def wz(z, lo, n):
        return wall[(z,) + (every,) * NB + (every, pl.ds(lo, n))].reshape(D, n)

    def wrows(z, n, lo, width):
        per = CHUNK // (2 * R)
        low = per.bit_length() - 1
        top = n * per
        fixed = {b: (top >> b) & 1 for b in range(low, NB)}
        return wall[(z,) + place(fixed) + (every, pl.ds(lo, width))].reshape(CHUNK, width)

    def wstore(z, lo, n, value):
        wall[(z,) + (every,) * NB + (every, pl.ds(lo, n))] = value.astype(B16).reshape(
            (2,) * NB + (2 * R, n)
        )

    def all_z(ref):
        return jnp.concatenate([ref[z] for z in range(T)], axis=-1)

    def mod(r):
        return mods[r : r + 1, :]

    def transpose_into(ref):
        for n in range(D // 128):
            block = ref[:, :, n * 128 : (n + 1) * 128].reshape(M, 128)
            xt[n * 128 : (n + 1) * 128, :] = block.T

    def rs_region(grp, step, h, away):
        order_r = order[h][::-1]
        fixed = {k: mybit[k] for k in order_r[: step + 1]}
        b = order_r[step]
        if away:
            fixed[b] = 1 - mybit[b]
        return b, fixed

    slot = {2: 0, 1: 1, 0: 0}

    def rs_buf(grp, step, h):
        return rb0.at[slot[grp], h] if step == 0 else rb1[step - 1].at[grp, h]

    def rs_copy(grp, step, h):
        b, fixed = rs_region(grp, step, h, True)
        part = wall.at[(half_z(h),) + place(fixed) + (every, cols(grp))]
        return rdma(part, rs_buf(grp, step, h), rs_s.at[grp, step, h], rs_r.at[grp, step, h], bit_dev(b))

    def rs_start(grp, step, h):
        rs_copy(grp, step, h).start()

    def rs_add(grp, step, h):
        rs_copy(grp, step, h).wait_recv()
        b, fixed = rs_region(grp, step, h, False)
        rest = [k for k in reversed(range(NB)) if k not in fixed]
        buf = rs_buf(grp, step, h)

        def one(i, carry):
            zz, j = i // (1 << len(rest)), lax.rem(i, 1 << len(rest))
            at = dict(fixed)
            inner = ()
            for pos, k in enumerate(rest):
                v = lax.rem(j // (1 << (len(rest) - 1 - pos)), 2)
                at[k] = v
                inner += (v,)
            where = (h * TH + zz,) + place(at) + (every, cols(grp))
            wall[where] = (wall[where].astype(F32) + buf[(zz,) + inner].astype(F32)).astype(B16)
            return carry

        lax.fori_loop(0, TH << len(rest), one, 0)

    def rz_copy(grp, off):
        part = wall.at[(lax.rem(me_z + off, T),) + mine + (every, cols(grp))]
        return rdma(part, zb.at[off - 1, :, cols(grp)], rz_s.at[grp, off - 1], rz_r.at[grp, off - 1], z_dev(off))

    def rz_start(grp):
        for off in range(1, T):
            rz_copy(grp, off).start()

    def fin_copy(grp):
        rows = pl.ds(pl.multiple_of((1 - core) * R, R), R)
        return rdma(fbuf.at[rows, cols(grp)], fin.at[core, :, cols(grp)], f_s.at[grp], f_r.at[grp], partner)

    def rz_add(grp):
        for off in range(1, T):
            rz_copy(grp, off).wait_recv()
        total = wall[(me_z,) + mine + (every, cols(grp))].astype(F32)
        for off in range(1, T):
            total = total + zb[off - 1, :, cols(grp)].astype(F32)
        fbuf[:, cols(grp)] = total
        fin_copy(grp).start()
        fin[core, :, cols(grp)] = fbuf[pl.ds(pl.multiple_of(core * R, R), R), cols(grp)]

    def rs_end(grp):
        for step in range(NB):
            for h in range(2):
                rs_copy(grp, step, h).wait_send()
        for off in range(1, T):
            rz_copy(grp, off).wait_send()
        fin_copy(grp).wait()

    tok_start(0, xb, xs)
    for grp in range(GROUPS):
        core_copy(grp).start()
        core_local(grp).start()
    for grp in range(GROUPS):
        core_wait(grp)
        if grp == 0:
            z_start(0)
    sums[...] = jnp.zeros_like(sums)
    tok_wait(0, xb, xs)

    def ln(rows):
        centred = rows - jnp.mean(rows, axis=-1, keepdims=True)
        inv = lax.rsqrt(jnp.mean(centred * centred, axis=-1, keepdims=True) + EPS)
        return centred * inv, inv

    def first_norm(t, carry):
        normed, _ = ln(xs[t].astype(F32))
        h1[t] = (normed * (1.0 + mod(2)) + mod(4)).astype(B16)
        return carry

    lax.fori_loop(0, T, first_norm, 0)
    z_wait(0)
    p_start(0, 0)
    z_start(1)
    tok_start(1, dyb, dys)
    for step in range(NB):
        p_wait(0, step)
        if step + 1 < NB:
            p_start(0, step + 1)
    z_wait(1)
    p_start(1, 0)
    z_start(2)

    lane = lax.broadcasted_iota(jnp.int32, (1, hq), 1)
    halves = [(lane // dm.hd) == k for k in range(hq // dm.hd)]
    bi = lax.broadcasted_iota(jnp.int32, (hq, hq), 0) // dm.hd
    bj = lax.broadcasted_iota(jnp.int32, (hq, hq), 1) // dm.hd
    same_head = (bi == bj).astype(B16)

    def qkv(z, carry):
        t = dot(h1[...].reshape(M, D), wz(z, 0, 3 * hq))
        q = t[:, :hq] + hp[z, 0:1, :]
        k = t[:, hq : 2 * hq]
        v = t[:, 2 * hq :] + hp[z, 1:2, :]
        qi = lax.rsqrt(split_dot(q * q, same_head) + EPS)
        ki = lax.rsqrt(split_dot(k * k, same_head) + EPS)
        qs[z] = (q * qi * hp[z, 2:3, :]).astype(B16)
        ks[z] = (k * ki).astype(B16)
        vs[z] = v.astype(B16)
        rq[z] = qi.astype(B16)
        rk[z] = ki.astype(B16)
        return carry

    lax.fori_loop(0, T, qkv, 0)
    zero16 = jnp.zeros((), B16)

    def expo(z, k, q_all, k_all):
        q_one = jnp.where(halves[k], q_all, zero16)
        left = jnp.concatenate([q_one, psi[...]], axis=1)
        right = jnp.concatenate([k_all, phi[...]], axis=1)
        return q_one, jnp.exp(dot_nt(left, right)).astype(B16)

    def attend(z, carry):
        q_all, k_all, v_all = qs[z], ks[z], vs[z]
        v_ones = jnp.concatenate([v_all, jnp.ones((M, hq), B16)], axis=1)
        mixed = inverse = None
        for k in range(hq // dm.hd):
            _, e = expo(z, k, q_all, k_all)
            both_ = dot(e, v_ones)
            inv = 1.0 / both_[:, hq:]
            one = both_[:, :hq] * inv
            mixed = one if mixed is None else jnp.where(halves[k], one, mixed)
            inverse = inv if inverse is None else jnp.where(halves[k], inv, inverse)
        o[z] = mixed.astype(B16)
        ol[z] = (mixed - mixed.astype(B16).astype(F32)).astype(B16)
        linv[z] = inverse
        return carry

    for z0 in range(0, T, 2):
        lax.fori_loop(z0, z0 + 2, attend, 0)
        if z0 == 0:
            p_wait(1, 0)
            if NB > 1:
                p_start(1, 1)
            z_wait(2)
            p_start(2, 0)

    o_all = all_z(o)
    for n in range(NCH):
        w = jnp.concatenate([wrows(z, n, 3 * hq, hq) for z in range(T)], axis=-1)
        exchange(0, n, dot_nt(o_all, w))
    exchange_wait(0)

    def middle(t):
        return xs[t].astype(F32) + mod(0) * ab[t].astype(F32)

    def second_norm(t, carry):
        ab[t] = (both(0, t) + mod(6)).astype(B16)
        normed, inv = ln(middle(t))
        h2[t] = (normed * (1.0 + mod(3)) + mod(5)).astype(B16)
        n2[t] = normed.astype(B16)
        r2[t] = jnp.broadcast_to(inv, (Q, 128))
        return carry

    lax.fori_loop(0, T, second_norm, 0)
    exchange_sent(0)
    for step in range(1, NB):
        p_wait(1, step)
        if step + 1 < NB:
            p_start(1, step + 1)
    p_wait(2, 0)
    if NB > 1:
        p_start(2, 1)

    root = 0.7978845608028654

    def up(z, carry):
        u = dot(h2[...].reshape(M, D), wz(z, dm.off[1], fu)) + hb[z, 0:1, :]
        uu = u * u
        th = jnp.tanh(root * u * (1.0 + 0.044715 * uu))
        g[z] = (0.5 * u * (1.0 + th)).astype(B16)
        gp[z] = (0.5 * (1.0 + th) + (0.5 * root) * u * (1.0 - th * th) * (1.0 + 0.134145 * uu)).astype(B16)
        return carry

    lax.fori_loop(0, T, up, 0)
    for step in range(1, NB):
        p_wait(2, step)
        if step + 1 < NB:
            p_start(2, step + 1)

    g_all = all_z(g)
    for n in range(NCH):
        w = jnp.concatenate([wrows(z, n, dm.off[2], fu) for z in range(T)], axis=-1)
        exchange(1, n, dot_nt(g_all, w))
    tok_wait(1, dyb, dys)
    exchange_wait(1)

    def last(t, carry):
        f = both(1, t) + mod(7)
        dy = dys[t].astype(F32)
        gamma = mod(1)
        od[t] = (mod(0) * ab[t].astype(F32) + gamma * f).astype(B16)
        sums[1:2, :] += row_sum(dy * f)
        d = (gamma * dy).astype(B16)
        df[t] = d
        sums[7:8, :] += row_sum(d.astype(F32))
        return carry

    lax.fori_loop(0, T, last, 0)
    exchange_sent(1)
    back_start(0, outd)
    for grp in range(GROUPS):
        gather_sent(grp)

    transpose_into(df)

    def down_back(z, carry):
        dg = dot(df[...].reshape(M, D), wz(z, dm.off[2], fu))
        du = (dg * gp[z].astype(F32)).astype(B16)
        gp[z] = du
        fsum[z] = jnp.broadcast_to(row_sum(du.astype(F32)), (8, fu))
        wstore(z, dm.off[2], fu, dot(xt[...], g[z]))
        return carry

    for h in range(2):
        lax.fori_loop(h * TH, (h + 1) * TH, down_back, 0)
        rs_start(2, 0, h)

    du_all = all_z(gp)
    for n in range(NCH):
        w = jnp.concatenate([wrows(z, n, dm.off[1], fu) for z in range(T)], axis=-1)
        exchange(2, n, dot_nt(du_all, w))
    transpose_into(h2)

    def up_back(z, carry):
        wstore(z, dm.off[1], fu, dot(xt[...], gp[z]))
        return carry

    lax.fori_loop(0, TH, up_back, 0)
    exchange_wait(2)

    def ln_back(e, normed, inv):
        return (e - jnp.mean(e, axis=-1, keepdims=True) - normed * jnp.mean(e * normed, axis=-1, keepdims=True)) * inv

    def mid_back(t, carry):
        dh = both(2, t)
        normed = n2[t].astype(F32)
        sums[3:4, :] += row_sum(dh * normed)
        sums[5:6, :] += row_sum(dh)
        step_back = ln_back(dh * (1.0 + mod(3)), normed, r2[t, :, 0:1])
        dx1 = dys[t].astype(F32) + step_back
        dys[t] = step_back.astype(B16)
        sums[0:1, :] += row_sum(dx1 * ab[t].astype(F32))
        da = (mod(0) * dx1).astype(B16)
        df[t] = da
        sums[6:7, :] += row_sum(da.astype(F32))
        return carry

    tok_sent(1, dyb, dys)
    lax.fori_loop(0, T, mid_back, 0)
    exchange_sent(2)
    for h in range(2):
        rs_add(2, 0, h)
        if NB > 1:
            rs_start(2, 1, h)
    rs_start(1, 0, 0)
    lax.fori_loop(TH, T, up_back, 0)
    rs_start(1, 0, 1)

    w_proj = jnp.concatenate([wz(z, 3 * hq, hq) for z in range(T)], axis=-1)
    do_all = dot(df[...].reshape(M, D), w_proj).astype(B16)
    for z in range(T):
        do[z] = do_all[:, z * hq : (z + 1) * hq]
    transpose_into(df)
    dw = dot(xt[...], all_z(o))
    for z in range(T):
        wstore(z, 3 * hq, hq, dw[:, z * hq : (z + 1) * hq])

    lane2 = lax.broadcasted_iota(jnp.int32, (1, hq), 1)
    ends = jnp.where(lane2 < 2, -1.0, 0.0).astype(B16)

    def attend_back(z, carry):
        q_all, k_all, v_all = qs[z], ks[z], vs[z]
        scaled = do[z].astype(F32) * linv[z]
        dob = scaled.astype(B16)
        prod = dob.astype(F32) * (o[z].astype(F32) + ol[z].astype(F32))
        v_ends = jnp.concatenate([v_all, jnp.broadcast_to(ends, (M, hq))], axis=1)
        dq = dk = dv = 0.0
        for k in range(hq // dm.hd):
            q_one, e = expo(z, k, q_all, k_all)
            to_all = (bi == k).astype(B16)
            total = split_dot(prod, to_all)
            high = total.astype(B16)
            low = (total - high.astype(F32)).astype(B16)
            extra = jnp.where(lane2 == 0, high, jnp.where(lane2 == 1, low, zero16))
            d_one = jnp.where(halves[k], dob, zero16)
            dp = dot_nt(jnp.concatenate([d_one, extra], axis=1), v_ends)
            ds = (e.astype(F32) * dp).astype(B16)
            dq = dq + dot(ds, jnp.where(halves[k], k_all, zero16))
            dk = dk + dot_tn(ds, q_one)
            dv = dv + dot_tn(e, d_one)
        gain = hp[z, 2:3, :]
        q_hat = q_all.astype(F32) * hp[z, 3:4, :]
        k_hat = k_all.astype(F32)
        hsum[z, 2:3, :] = row_sum(dq * q_hat)
        eq = dq * gain
        dq = ((eq - q_hat * split_dot(eq * q_hat, same_head)) * rq[z].astype(F32)).astype(B16)
        dk = ((dk - k_hat * split_dot(dk * k_hat, same_head)) * rk[z].astype(F32)).astype(B16)
        dv = dv.astype(B16)
        hsum[z, 0:1, :] = row_sum(dq.astype(F32))
        hsum[z, 1:2, :] = row_sum(dv.astype(F32))
        dqkv[z] = jnp.concatenate([dq, dk, dv], axis=1)
        return carry

    hsum[...] = jnp.zeros_like(hsum)
    lax.fori_loop(0, TH, attend_back, 0)
    for h in range(2):
        for step in range(1, NB):
            rs_add(2, step, h)
            if step + 1 < NB:
                rs_start(2, step + 1, h)
    rz_start(2)
    for h in range(2):
        rs_add(1, 0, h)
        if NB > 1:
            rs_start(1, 1, h)
    lax.fori_loop(TH, T, attend_back, 0)

    d_all = all_z(dqkv)
    for n in range(NCH):
        w = jnp.concatenate([wrows(z, n, 0, 3 * hq) for z in range(T)], axis=-1)
        exchange(3, n, dot_nt(d_all, w))
    transpose_into(h1)

    def qkv_back(z, carry):
        wstore(z, 0, 3 * hq, dot(xt[...], dqkv[z]))
        return carry

    for h in range(2):
        lax.fori_loop(h * TH, (h + 1) * TH, qkv_back, 0)
        rs_start(0, 0, h)
    exchange_wait(3)

    def first_back(t, carry):
        dh = both(3, t)
        normed, inv = ln(xs[t].astype(F32))
        sums[2:3, :] += row_sum(dh * normed)
        sums[4:5, :] += row_sum(dh)
        h2[t] = (dys[t].astype(F32) + ln_back(dh * (1.0 + mod(2)), normed, inv)).astype(B16)
        return carry

    lax.fori_loop(0, T, first_back, 0)
    exchange_sent(3)
    back_start(1, gind)
    for h in range(2):
        for step in range(1, NB):
            rs_add(1, step, h)
            if step + 1 < NB:
                rs_start(1, step + 1, h)
    rz_start(1)
    rz_add(2)
    for step in range(NB):
        for h in range(2):
            rs_add(0, step, h)
            if step + 1 < NB:
                rs_start(0, step + 1, h)
    rz_start(0)
    rz_add(1)
    rz_add(0)
    for grp in range(GROUPS):
        rs_end(grp)
    tok_sent(0, xb, xs)
    back_wait(0, outd)
    back_wait(1, gind)


def block_call(dm, ws, xb, dyb, mods, hp, hb, psi, phi):
    T, NB, Q, M, D, R, C = dm.T, dm.bits, dm.Q, dm.M, dm.D, dm.R, dm.C
    hq, fu, NCH, gw = dm.hq, dm.fu, dm.NCH, dm.fu
    TH = T // 2
    two = (2,) * NB
    v = pltpu.VMEM
    dma = pltpu.SemaphoreType.DMA
    any_, vm = pl.BlockSpec(memory_space=pl.ANY), pl.BlockSpec(memory_space=pltpu.VMEM)
    s = jax.ShapeDtypeStruct
    tok = (T, Q, D)
    scratch = [
        v((T,) + two + (2 * R, C), B16),
        v(tok, B16), v(tok, B16), v(tok, B16), v(tok, B16),
        v((T, M, hq), B16), v((T, M, hq), B16), v((T, M, hq), B16),
        v((T, M, hq), B16), v((T, M, hq), B16), v((T, M, hq), F32),
        v((T, M, hq), B16), v((T, M, hq), B16), v(tok, B16), v(tok, B16), v((T, Q, 128), F32),
        v((T, M, fu), B16), v((T, M, fu), B16),
        v((NCH, T, Q, CHUNK), B16), v((2, NCH, T, Q, CHUNK), B16),
        v(tok, B16), v((D, M), B16),
        v((T, M, hq), B16), v((T, M, 3 * hq), B16), v(tok, B16),
        v((2, 2, TH) + (2,) * (NB - 1) + (2 * R, gw), B16),
        [v((GROUPS, 2, TH) + (2,) * (NB - 1 - k) + (2 * R, gw), B16) for k in range(1, NB)],
        v((T - 1, 2 * R, C), B16), v((2 * R, C), F32),
        dma((GROUPS,)), dma((GROUPS,)), dma((GROUPS,)),
        dma((GROUPS, T - 1)), dma((GROUPS, T - 1)),
        dma((GROUPS, NB, 2)), dma((GROUPS, NB, 2)),
        dma((2, 2)), dma((2, T)), dma((2,)), dma((2, 2)),
        dma((4, NCH)), dma((4, NCH)),
        dma((GROUPS, NB, 2)), dma((GROUPS, NB, 2)),
        dma((GROUPS, T - 1)), dma((GROUPS, T - 1)),
        dma((GROUPS,)), dma((GROUPS,)),
        dma((2, T)), dma((2, 2)), dma((2,)),
    ]
    return pl.pallas_call(
        functools.partial(block_kernel, dm),
        out_shape=(
            s((2, R, C), F32), s((2, Q, D), B16), s((2, Q, D), B16),
            s((8, D), F32), s((T, 8, hq), F32), s((T, 8, fu), F32),
        ),
        in_specs=[any_] * 3 + [vm] * 5,
        out_specs=(vm, any_, any_, vm, vm, vm),
        scratch_shapes=scratch,
        compiler_params=pltpu.CompilerParams(
            collective_id=0, has_side_effects=True, vmem_limit_bytes=66 * 1024 * 1024
        ),
        cost_estimate=pl.CostEstimate(flops=30 * 10**9, bytes_accessed=10**7, transcendentals=10**7),
    )(ws, xb, dyb, mods, hp, hb, psi, phi)


def local(
    dp, tensor,
    block_input, cotangent, class_ids, scale_ids, class_table, w_ada, b_ada, query_key_value_weight,
    qv_bias, q_gain, output_projection, up_weight, hidden_bias, down_weight, projection_bias,
):
    seqs, quarter, width = block_input.shape
    length = scale_ids.shape[1]
    assert seqs == 2 and tensor == 4
    rows = -(-quarter // 16) * 16
    head = q_gain.shape[1] * dp
    hidden = up_weight.shape[1] * tensor
    dm = Dims(dp, tensor, rows, width, head, hidden)
    T, R, hq, fu, NC, M = dm.T, dm.R, dm.hq, dm.fu, dm.NC, dm.M
    total = class_ids.shape[0]
    di, zi = lax.axis_index("dp"), lax.axis_index("tensor")
    core = di % 2

    my_rows = class_table.shape[0]
    hot = (class_ids[:, None] == (di * my_rows + jnp.arange(my_rows, dtype=jnp.int32))[None, :]).astype(B16)
    cond = lax.psum(jnp.dot(hot, class_table, preferred_element_type=F32), "dp")
    silu, silu_back = jax.vjp(jax.nn.silu, cond)
    silu_low = silu.astype(B16)
    parts = jnp.einsum("sc,cjd->sjd", silu_low, w_ada, preferred_element_type=F32)
    parts = parts.reshape((NC, T) + parts.shape[1:])
    mine = lax.psum_scatter(parts, "tensor", scatter_dimension=1, tiled=True)[:, 0] + b_ada.astype(F32)
    spread = lax.all_to_all(jnp.repeat(mine, 2, axis=0), "dp", 0, 0, tiled=True)
    modulation = jnp.moveaxis(spread, 0, 1).reshape(6, width)

    pieces = [qv_bias, q_gain, hidden_bias, projection_bias]
    flat = jnp.concatenate([p.reshape(-1) for p in pieces])
    everyone = lax.all_gather(lax.all_gather(flat, "tensor"), "dp")
    cut, at = [], 0
    for p in pieces:
        cut.append(everyone[:, :, at : at + p.size].reshape((dp, T) + p.shape).astype(F32))
        at += p.size
    qv_all = cut[0].transpose(2, 1, 3, 0, 4).reshape(2, T, 2, hq)[:, :, core]
    gain_all = cut[1].transpose(1, 2, 0, 3).reshape(T, 2, hq)[:, core]
    hidden_all = cut[2].transpose(1, 2, 0, 3).reshape(T, 2, fu)[:, core]
    out_bias = cut[3][:, 0].transpose(1, 0, 2).reshape(2, width)
    mods = jnp.concatenate([modulation, out_bias], axis=0)
    hp = jnp.stack([qv_all[0], qv_all[1], gain_all, 1.0 / gain_all], axis=1)
    hp = jnp.concatenate([hp, jnp.zeros_like(hp)], axis=1)
    hb = jnp.broadcast_to(hidden_all[:, None], (T, 8, fu))

    swap = [(d, d + 1 - 2 * (d % 2)) for d in range(dp)]
    other = lax.ppermute(scale_ids, "dp", swap)
    ids = jnp.where(zi // 2 == core, scale_ids, other)
    ids = lax.dynamic_index_in_dim(ids, zi % 2, 0, keepdims=False)
    ids = jnp.pad(ids.reshape(T, quarter), ((0, 0), (0, rows - quarter)), constant_values=127).reshape(M, 1)
    lanes = jnp.arange(128, dtype=jnp.int32)[None, :]
    psi = jnp.where(lanes > ids, FAR, 0.0).astype(B16)
    phi = jnp.where(lanes == ids, -1.0, 0.0).astype(B16)

    def halves(w):
        return jnp.moveaxis(w.reshape(w.shape[:-1] + (2, w.shape[-1] // 2)), -2, 0)

    qkv_half = halves(query_key_value_weight)
    ws = jnp.concatenate(
        [qkv_half[:, 0], qkv_half[:, 1], qkv_half[:, 2], halves(output_projection.T), halves(up_weight), halves(down_weight.T)],
        axis=-1,
    )
    pad = ((0, 0), (0, rows - quarter), (0, 0))
    xb = jnp.pad(block_input.astype(B16), pad)
    dyb = jnp.pad(cotangent.astype(B16), pad)

    fin, outd, gind, sums, hsum, fsum = block_call(dm, ws, xb, dyb, mods, hp, hb, psi, phi)

    block_output = block_input + outd[:, :quarter].astype(F32)
    input_grad = cotangent + gind[:, :quarter].astype(F32)

    def joined(lo, n):
        return jnp.moveaxis(fin[:, :, lo : lo + n], 0, 1).reshape(R, 2 * n)

    w_qkv_grad = jnp.stack([joined(k * hq, hq) for k in range(3)])
    w_proj_grad = joined(3 * hq, hq).T
    w_fc1_grad = joined(dm.off[1], fu)
    w_fc2_grad = joined(dm.off[2], fu).T

    dmod = sums[:6].reshape(6, dp, R).astype(B16)
    dmod = lax.all_to_all(jnp.moveaxis(dmod, 1, 0), "dp", 0, 0, tiled=True)
    dmod = lax.all_gather(dmod[::2], "tensor", axis=1)
    dmod = dmod.reshape((total, 6, R))
    b_ada_grad = jnp.sum(dmod.astype(F32), axis=0)
    w_ada_grad = jnp.einsum("sc,sjd->cjd", silu_low, dmod, preferred_element_type=F32)
    d_silu = lax.psum(jnp.einsum("sjd,cjd->sc", dmod, w_ada, preferred_element_type=F32), "dp")
    (d_cond,) = silu_back(d_silu)
    table_grad = jnp.dot(hot.astype(F32).T, d_cond, precision=lax.Precision.HIGHEST, preferred_element_type=F32)

    vec = jnp.concatenate([hsum[:, :3].reshape(-1), fsum[:, 0].reshape(-1), sums[6:].reshape(-1) * 0.5])
    nh, nf = T * 3 * hq, T * fu
    place_ = jnp.arange(2, dtype=jnp.int32) == core
    by_core = jnp.where(place_[:, None], vec[None, : nh + nf], 0.0).reshape(-1)
    vec = lax.psum(jnp.concatenate([by_core, vec[nh + nf :]]), ("dp", "tensor"))
    by_core = vec[: 2 * (nh + nf)].reshape(2, nh + nf)
    heads = by_core[:, :nh].reshape(2, T, 3, hq)
    heads = lax.dynamic_index_in_dim(heads, zi, 1, keepdims=False)
    heads = jnp.moveaxis(heads, 0, 1).reshape(3, -1, head)
    step = head // dp
    heads = lax.dynamic_slice_in_dim(heads, di * step, step, 2)
    qv_bias_grad, q_gain_grad = heads[:2], heads[2]
    fc1 = lax.dynamic_index_in_dim(by_core[:, nh:].reshape(2, T, fu), zi, 1, keepdims=False)
    fc1 = fc1.reshape(-1, hidden_bias.shape[1] * dp)
    step = hidden_bias.shape[1]
    b_fc1_grad = lax.dynamic_slice_in_dim(fc1, di * step, step, 1)
    b_out_grad = lax.dynamic_slice_in_dim(vec[2 * (nh + nf) :].reshape(2, width), di * R, R, 1)

    return (
        block_output, input_grad, table_grad, w_ada_grad, b_ada_grad, w_qkv_grad, qv_bias_grad, q_gain_grad,
        w_proj_grad, w_fc1_grad, b_fc1_grad, w_fc2_grad, b_out_grad,
    )


def solution(mesh):
    dp, tensor = mesh.shape["dp"], mesh.shape["tensor"]
    return jax.shard_map(
        functools.partial(local, dp, tensor),
        mesh=mesh,
        in_specs=(
            P("dp", "tensor", None),
            P("dp", "tensor", None),
            P(),
            P("dp", None),
            P("dp", "tensor"),
            P("tensor", None, "dp"),
            P(None, "dp"),
            P(None, "dp", "tensor"),
            P(None, "tensor", "dp"),
            P("tensor", "dp"),
            P("tensor", "dp"),
            P("dp", "tensor"),
            P("tensor", "dp"),
            P("tensor", "dp"),
            P(None, "dp"),
        ),
        out_specs=(
            P("dp", "tensor", None),
            P("dp", "tensor", None),
            P("dp", "tensor"),
            P("tensor", None, "dp"),
            P(None, "dp"),
            P(None, "dp", "tensor"),
            P(None, "tensor", "dp"),
            P("tensor", "dp"),
            P("tensor", "dp"),
            P("dp", "tensor"),
            P("tensor", "dp"),
            P("tensor", "dp"),
            P(None, "dp"),
        ),
        check_vma=False,
    )
```

```python
import functools

import jax
import jax.numpy as jnp
from jax import lax
from jax.experimental import pallas as pl
from jax.experimental.pallas import tpu as pltpu
from jax.sharding import PartitionSpec as P

MESH = pl.DeviceIdType.MESH
F32, B16 = jnp.float32, jnp.bfloat16
SLOTS = 3
CHUNK = 256
EPS = 1e-06
FAR = 256.0


def dot(a, b):
    return lax.dot_general(a, b, (((1,), (0,)), ((), ())), preferred_element_type=F32)


def dot_nt(a, b):
    return lax.dot_general(a, b, (((1,), (1,)), ((), ())), preferred_element_type=F32)


def dot_tn(a, b):
    return lax.dot_general(a, b, (((0,), (0,)), ((), ())), preferred_element_type=F32)


def split_dot(a, b):
    high = a.astype(B16)
    low = (a - high.astype(F32)).astype(B16)
    return dot(high, b) + dot(low, b)


def row_sum(a):
    return jnp.sum(a, axis=0, keepdims=True)


class Dims:
    def __init__(self, dp, tensor, rows, width, head, hidden):
        self.T = tensor
        self.NC = dp // 2
        self.bits = self.NC.bit_length() - 1
        self.Q = rows
        self.M = rows * tensor
        self.D = width
        self.hd = head
        self.hq = width // tensor // 2
        self.fu = hidden // tensor // 2
        self.R = width // dp
        self.C = 4 * self.hq + 2 * self.fu
        self.NCH = width // CHUNK
        self.inside = self.R % 128 == 0 and self.NC <= 8 and hidden // tensor <= width
        self.W = self.hq + self.fu + width
        hq, fu, half = self.hq, self.fu, self.fu // 2
        up, down = 4 * hq, 4 * hq + fu
        self.up, self.down, self.half = up, down, half
        self.pieces = ((0, hq), (hq, hq), (2 * hq, hq), (3 * hq, hq), (up, half), (down, half), (up + half, half), (down + half, half))
        self.sums_order = (5, 4, 7, 6, 3, 2, 1, 0)
        assert 1 << self.bits == self.NC


class Refs:
    pass


def block_kernel(dm, names, *refs):
    m = Refs()
    for name, ref in zip(names, refs):
        if name.startswith("rb"):
            m.rb = getattr(m, "rb", []) + [ref]
        else:
            setattr(m, name, ref)
    T, NC, NB, Q, M, D, R, C = dm.T, dm.NC, dm.bits, dm.Q, dm.M, dm.D, dm.R, dm.C
    hq, fu, NCH, half = dm.hq, dm.fu, dm.NCH, dm.half
    TH = T // 2
    NP = len(dm.pieces)
    wall, xs, dys, h1, h2 = m.wall, m.xs, m.dys, m.h1, m.h2
    mods, hp, hb, sums, hsum, fsum = m.mods, m.hp, m.hb, m.sums, m.hsum, m.fsum
    dpi = lax.axis_index("dp")
    me_z = lax.axis_index("tensor")
    core = lax.rem(dpi, 2)
    chip = dpi // 2
    mybit = [lax.rem(chip // (1 << b), 2) for b in range(NB)]
    partner = (dpi + 1 - 2 * core, me_z)

    def z_dev(off):
        return (dpi, lax.rem(me_z + off, T))

    def bit_dev(b):
        return (dpi + (1 - 2 * mybit[b]) * (2 << b), me_z)

    def chip_dev(k):
        return (lax.rem(chip + k, NC) * 2 + core, me_z)

    bar = pltpu.get_barrier_semaphore()
    friends = [partner] + [z_dev(k) for k in range(1, T)]
    friends += [chip_dev(k) for k in range(1, NC)] if dm.inside else [bit_dev(b) for b in range(NB)]
    for dev in friends:
        pl.semaphore_signal(bar, inc=1, device_id=dev, device_id_type=MESH)
    pl.semaphore_wait(bar, len(friends))

    def rdma(src, dst, ss, rs, dev):
        return pltpu.make_async_remote_copy(
            src_ref=src, dst_ref=dst, send_sem=ss, recv_sem=rs, device_id=dev, device_id_type=MESH
        )

    every = slice(None)

    def place(fixed):
        return tuple(fixed.get(b, every) for b in reversed(range(NB)))

    mine = place({b: mybit[b] for b in range(NB)})

    def cols(pc):
        return pl.ds(*dm.pieces[pc])

    def core_rows(c):
        return pl.ds(pl.multiple_of(c * R, R), R)

    def core_copy(pc):
        dst = wall.at[(me_z,) + mine + (core_rows(core), cols(pc))]
        return rdma(m.ws.at[1 - core, :, cols(pc)], dst, m.c_s.at[pc], m.c_r.at[pc], partner)

    def core_local(pc):
        dst = wall.at[(me_z,) + mine + (core_rows(core), cols(pc))]
        return pltpu.make_async_copy(m.ws.at[core, :, cols(pc)], dst, m.c_l.at[pc])

    def z_copy(pc, off):
        part = wall.at[(me_z,) + mine + (every, cols(pc))]
        return rdma(part, part, m.z_s.at[pc, off - 1], m.z_r.at[pc, off - 1], z_dev(off))

    order = [list(range(NB)), list(reversed(range(NB)))]

    def half_z(h):
        return pl.ds(h * TH, TH)

    def p_copy(pc, step, h, landing):
        b = order[h][step]
        fixed = {k: mybit[k] for k in order[h][step:]}
        if landing:
            fixed[b] = 1 - mybit[b]
        part = wall.at[(half_z(h),) + place(fixed) + (every, cols(pc))]
        return rdma(part, part, m.p_s.at[pc, step, h], m.p_r.at[pc, step, h], bit_dev(b))

    def gather_stage(pc, s):
        if not 0 <= pc < NP:
            return
        if s == 0:
            core_local(pc).wait()
            other = wall.at[(me_z,) + mine + (core_rows(1 - core), cols(pc))]
            rdma(other, other, m.c_s.at[pc], m.c_r.at[pc], partner).wait_recv()
            for off in range(1, T):
                z_copy(pc, off).start()
            return
        if s == 1:
            for off in range(1, T):
                part = wall.at[(lax.rem(me_z - off + T, T),) + mine + (every, cols(pc))]
                rdma(part, part, m.z_s.at[pc, off - 1], m.z_r.at[pc, off - 1], z_dev(off)).wait_recv()
        for h in range(2):
            if s > 1:
                p_copy(pc, s - 2, h, True).wait_recv()
            if s <= NB:
                p_copy(pc, s - 1, h, False).start()

    ticks = [0]

    def gather_tick():
        t = ticks[0]
        ticks[0] += 1
        for s in range(NB, -1, -1):
            gather_stage(t - s, s)
        gather_stage(t - NB - 1, NB + 1)

    def gather_until(pc):
        while ticks[0] <= pc + NB + 1:
            gather_tick()

    def gather_sent(which):
        for pc in which:
            core_copy(pc).wait_send()
            for off in range(1, T):
                z_copy(pc, off).wait_send()
            for step in range(NB):
                for h in range(2):
                    p_copy(pc, step, h, False).wait_send()

    owner = me_z // 2 == core

    def tok_copy(which, src, dst, i):
        zt = 2 * core + i
        return rdma(src.at[i], dst.at[me_z], m.x_s.at[which, i], m.x_r.at[which, me_z], (dpi, zt))

    def tok_start(which, src, dst):
        for i in range(2):
            @pl.when(2 * core + i != me_z)
            def _():
                tok_copy(which, src, dst, i).start()

            @pl.when(2 * core + i == me_z)
            def _():
                pltpu.make_async_copy(src.at[i], dst.at[me_z], m.x_l.at[which]).start()

    def tok_forward(which, dst):
        return rdma(dst, dst, m.x_f.at[which, 0], m.x_f.at[which, 1], partner)

    def tok_wait(which, src, dst):
        @pl.when(owner)
        def _():
            for off in range(1, T):
                zq = lax.rem(me_z + off, T)
                rdma(dst.at[zq], dst.at[zq], m.x_s.at[which, 0], m.x_r.at[which, zq], (dpi, zq)).wait_recv()
            pltpu.make_async_copy(src.at[0], dst.at[me_z], m.x_l.at[which]).wait()
            tok_forward(which, dst).start()

        @pl.when(jnp.logical_not(owner))
        def _():
            tok_forward(which, dst).wait_recv()

    def tok_sent(which, src, dst):
        for i in range(2):
            @pl.when(2 * core + i != me_z)
            def _():
                tok_copy(which, src, dst, i).wait_send()

        @pl.when(owner)
        def _():
            tok_forward(which, dst).wait_send()

    back_from = (m.n2, m.ab)

    def back_copy(which, dst, zq):
        i = lax.rem(me_z, 2)
        return rdma(back_from[which].at[zq], dst.at[i], m.o_s.at[which, zq], m.o_r.at[which, i], (dpi, zq))

    def back_start(which, dst):
        @pl.when(owner)
        def _():
            for off in range(1, T):
                back_copy(which, dst, lax.rem(me_z + off, T)).start()
            pltpu.make_async_copy(back_from[which].at[me_z], dst.at[lax.rem(me_z, 2)], m.o_l.at[which]).start()

    def back_wait(which, dst):
        @pl.when(owner)
        def _():
            for off in range(1, T):
                back_copy(which, dst, lax.rem(me_z + off, T)).wait_send()
            pltpu.make_async_copy(back_from[which].at[me_z], dst.at[lax.rem(me_z, 2)], m.o_l.at[which]).wait()

        for i in range(2):
            @pl.when(2 * core + i != me_z)
            def _():
                rdma(dst.at[i], dst.at[i], m.o_s.at[which, 0], m.o_r.at[which, i], (dpi, 2 * core + i)).wait_recv()

    def x_copy(k, n):
        return rdma(m.send.at[n], m.recv.at[k % 2, n], m.e_s.at[k, n], m.e_r.at[k, n], partner)

    def exchange(k, n, value):
        m.send[n] = value.astype(B16).reshape(T, Q, CHUNK)
        x_copy(k, n).start()

    def exchange_wait(k):
        for n in range(NCH):
            x_copy(k, n).wait_recv()

    def exchange_sent(k):
        for n in range(NCH):
            x_copy(k, n).wait_send()

    def both(k, t):
        parts = [m.send[n, t].astype(F32) + m.recv[k % 2, n, t].astype(F32) for n in range(NCH)]
        return jnp.concatenate(parts, axis=-1)

    def wz(z, lo, n):
        return wall[(z,) + (every,) * NB + (every, pl.ds(lo, n))].reshape(D, n)

    def wrows(z, n, lo, width):
        per = CHUNK // (2 * R)
        low = per.bit_length() - 1
        top = n * per
        fixed = {b: (top >> b) & 1 for b in range(low, NB)}
        return wall[(z,) + place(fixed) + (every, pl.ds(lo, width))].reshape(CHUNK, width)

    def wrows_all(n, lo, width):
        return jnp.concatenate([wrows(z, n, lo, width) for z in range(T)], axis=-1)

    def wstore(z, lo, n, value):
        wall[(z,) + (every,) * NB + (every, pl.ds(lo, n))] = value.astype(B16).reshape(
            (2,) * NB + (2 * R, n)
        )

    def all_z(ref):
        return jnp.concatenate([ref[z] for z in range(T)], axis=-1)

    def whole(ref):
        return ref[...].reshape(M, D)

    def mod(r):
        return mods[r : r + 1, :]

    def transpose_into(dst, ref):
        for n in range(D // 128):
            block = ref[:, :, n * 128 : (n + 1) * 128].reshape(M, 128)
            dst[n * 128 : (n + 1) * 128, :] = block.T

    place_of = {pc: j for j, pc in enumerate(dm.sums_order)}

    def rs_fixed(step, h, away):
        order_r = order[h][::-1]
        fixed = {k: mybit[k] for k in order_r[: step + 1]}
        b = order_r[step]
        if away:
            fixed[b] = 1 - mybit[b]
        return b, fixed

    def rs_copy(j, step, h):
        pc = dm.sums_order[j]
        b, fixed = rs_fixed(step, h, True)
        part = wall.at[(half_z(h),) + place(fixed) + (every, cols(pc))]
        buf = m.rb[step].at[(j % SLOTS, h) + (every,) * (NB - step) + (every, pl.ds(0, dm.pieces[pc][1]))]
        return rdma(part, buf, m.rs_s.at[j, step, h], m.rs_r.at[j, step, h], bit_dev(b))

    def rs_start(j, step, h):
        if j >= SLOTS:
            pl.semaphore_wait(m.free.at[step, h], 1)
        rs_copy(j, step, h).start()

    def rs_add(j, step, h):
        pc = dm.sums_order[j]
        rs_copy(j, step, h).wait_recv()
        b, fixed = rs_fixed(step, h, False)
        rest = [k for k in reversed(range(NB)) if k not in fixed]
        slot, width = j % SLOTS, dm.pieces[pc][1]

        def one(i, carry):
            zz, r = i // (1 << len(rest)), lax.rem(i, 1 << len(rest))
            at = dict(fixed)
            inner = ()
            for pos, k in enumerate(rest):
                v = lax.rem(r // (1 << (len(rest) - 1 - pos)), 2)
                at[k] = v
                inner += (v,)
            where = (h * TH + zz,) + place(at) + (every, cols(pc))
            got = m.rb[step][(slot, h, zz) + inner + (every, pl.ds(0, width))]
            wall[where] = (wall[where].astype(F32) + got.astype(F32)).astype(B16)
            return carry

        lax.fori_loop(0, TH << len(rest), one, 0)
        if j + SLOTS < NP:
            pl.semaphore_signal(m.free.at[step, h], inc=1, device_id=bit_dev(b), device_id_type=MESH)

    def rz_copy(j, off):
        pc = dm.sums_order[j]
        part = wall.at[(lax.rem(me_z + off, T),) + mine + (every, cols(pc))]
        return rdma(part, m.zb.at[off - 1, :, cols(pc)], m.rz_s.at[j, off - 1], m.rz_r.at[j, off - 1], z_dev(off))

    def fin_copy(j):
        pc = dm.sums_order[j]
        return rdma(m.fbuf.at[:, cols(pc)], m.fin.at[core, :, cols(pc)], m.f_s.at[j], m.f_r.at[j], partner)

    def rs_event(j, s):
        pc = dm.sums_order[j]
        if s <= NB:
            for h in range(2):
                rs_add(j, s - 1, h)
                if s < NB:
                    rs_start(j, s, h)
            if s == NB:
                for off in range(1, T):
                    rz_copy(j, off).start()
            return
        for off in range(1, T):
            rz_copy(j, off).wait_recv()

        def total(rows):
            acc = wall[(me_z,) + mine + (rows, cols(pc))].astype(F32)
            for off in range(1, T):
                acc = acc + m.zb[off - 1, rows, cols(pc)].astype(F32)
            return acc

        m.fbuf[:, cols(pc)] = total(core_rows(1 - core))
        fin_copy(j).start()
        m.fin[core, :, cols(pc)] = total(core_rows(core))

    events = sorted(((j, s) for j in range(NP) for s in range(1, NB + 2)), key=lambda e: (e[0] + 1.5 * e[1], e[0]))
    begun = set()

    def pump(count):
        while count and events and (events[0][0], 1) in begun:
            rs_event(*events.pop(0))
            count -= 1

    def rs_begin(pc, h):
        j = place_of[pc]
        while (j - SLOTS, 1) in events:
            pump(1)
        rs_start(j, 0, h)
        begun.add((j, h))

    def rs_end():
        for j in range(NP):
            for step in range(NB):
                for h in range(2):
                    rs_copy(j, step, h).wait_send()
            for off in range(1, T):
                rz_copy(j, off).wait_send()
            fin_copy(j).wait()

    def small(src, dst, k, dev):
        return rdma(src, dst, m.s_s.at[k], m.s_r.at[k], dev)

    def sum_step(acc, got, i, base, sign):
        dev = partner if i < sign else bit_dev(i - sign)
        return small(acc.at[i], got.at[i], base + i, dev)

    def sum_finish(acc, got, i, base, sign):
        sum_step(acc, got, i, base, sign).wait_recv()
        acc[i + 1] = acc[i] + got[i]

    S_SID = 0
    S_M1 = 1
    S_M2 = S_M1 + NB + 1
    S_SM = S_M2 + T - 1
    S_M3 = S_SM + T - 1
    S_M4 = S_M3 + NC - 1
    S_B1 = S_M4 + 1
    S_B2 = S_B1 + NC - 1
    S_B3 = S_B2 + T - 1
    S_PZ = S_B3 + NB + 1
    S_PB = S_PZ + T - 1
    S_PC = S_PB + NB

    sid_copy = small(m.sid, m.sidr, S_SID, partner)
    sid_copy.start()
    if dm.inside:
        m.macc[0] = m.m1[...]
        sum_step(m.macc, m.mrec, 0, S_M1, 1).start()
    core_copy(0).start()
    core_local(0).start()
    tok_start(0, m.xb, xs)
    for pc in range(1, NP):
        core_copy(pc).start()
        core_local(pc).start()
    gather_tick()
    sums[...] = jnp.zeros_like(sums)
    hsum[...] = jnp.zeros_like(hsum)
    fsum[...] = jnp.zeros_like(fsum)

    if dm.inside:
        for i in range(NB + 1):
            sum_finish(m.macc, m.mrec, i, S_M1, 1)
            if i < NB:
                sum_step(m.macc, m.mrec, i + 1, S_M1, 1).start()
        m.sm[me_z] = m.macc[NB + 1, 8:16, :]
        for off in range(1, T):
            small(m.sm.at[me_z], m.sm.at[me_z], S_SM + off - 1, z_dev(off)).start()
        m.cond[...] = m.macc[NB + 1, 0:8, :]
        width = D // T
        for zz in range(T):
            c = m.cond[:, zz * width : (zz + 1) * width]
            low = (c / (1.0 + jnp.exp(-c))).astype(B16)
            rows = [dot(low, m.wada[j]) for j in range(6)] + [jnp.zeros((8, 2 * R), F32)]
            m.m2s[zz] = jnp.concatenate(rows, axis=-1)
        for off in range(1, T):
            small(m.m2s.at[lax.rem(me_z + off, T)], m.m2r.at[off - 1], S_M2 + off - 1, z_dev(off)).start()

    gather_tick()

    if dm.inside:
        for off in range(1, T):
            small(m.m2s.at[0], m.m2r.at[off - 1], S_M2 + off - 1, z_dev(off)).wait_recv()
        m.m3c[core, chip] = m.m2s[me_z] + sum(m.m2r[k] for k in range(T - 1)) + m.badd[...]
        own = m.m3c.at[core, chip]
        for k in range(1, NC):
            small(own, own, S_M3 + k - 1, chip_dev(k)).start()
        for k in range(1, NC):
            got = m.m3c.at[core, lax.rem(chip - k + NC, NC)]
            small(got, got, S_M3 + k - 1, chip_dev(k)).wait_recv()
        small(m.m3c.at[core], m.m3c.at[core], S_M4, partner).start()
        for off in range(1, T):
            got = m.sm.at[lax.rem(me_z - off + T, T)]
            small(got, got, S_SM + off - 1, z_dev(off)).wait_recv()
        head_cols = pl.ds(pl.multiple_of(core * hq, hq), hq)
        for z in range(T):
            for r in range(3):
                hp[z, r : r + 1, :] = m.sm[z, r + 1 : r + 2, head_cols]
            hp[z, 3:4, :] = 1.0 / hp[z, 2:3, :]
            hb[z, 0:1, :] = m.sm[z, 0:1, pl.ds(pl.multiple_of(core * fu, fu), fu)]
        got = m.m3c.at[1 - core]
        small(got, got, S_M4, partner).wait_recv()
        for c in range(2):
            for p in range(NC):
                row = m.m3c[c, p, pl.ds(chip, 1), :]
                d = 2 * p + c
                for j in range(8):
                    mods[j : j + 1, d * R : (d + 1) * R] = row[:, j * R : (j + 1) * R]

    got = small(m.sidr, m.sidr, S_SID, partner)
    got.wait_recv()
    pick = lax.rem(me_z, 2)
    ids = jnp.where(owner, m.sid[pl.ds(pick, 1), :], m.sidr[pl.ds(pick, 1), :])
    lanes = lax.broadcasted_iota(jnp.int32, (128, 1), 0).astype(F32)
    m.psi[...] = jnp.where(lanes > ids, FAR, 0.0).astype(B16).T
    m.phi[...] = jnp.where(lanes == ids, -1.0, 0.0).astype(B16).T
    tok_wait(0, m.xb, xs)

    def ln(rows):
        centred = rows - jnp.mean(rows, axis=-1, keepdims=True)
        inv = lax.rsqrt(jnp.mean(centred * centred, axis=-1, keepdims=True) + EPS)
        return centred * inv, inv

    def first_norm(t, carry):
        normed, _ = ln(xs[t].astype(F32))
        h1[t] = (normed * (1.0 + mod(2)) + mod(4)).astype(B16)
        return carry

    lax.fori_loop(0, T, first_norm, 0)
    tok_start(1, m.dyb, dys)
    gather_until(2)

    lane = lax.broadcasted_iota(jnp.int32, (1, hq), 1)
    halves = [(lane // dm.hd) == k for k in range(hq // dm.hd)]
    bi = lax.broadcasted_iota(jnp.int32, (hq, hq), 0) // dm.hd
    bj = lax.broadcasted_iota(jnp.int32, (hq, hq), 1) // dm.hd
    same_head = (bi == bj).astype(B16)

    def qkv(z, carry):
        t = dot(whole(h1), wz(z, 0, 3 * hq))
        q = t[:, :hq] + hp[z, 0:1, :]
        k = t[:, hq : 2 * hq]
        v = t[:, 2 * hq :] + hp[z, 1:2, :]
        qi = lax.rsqrt(split_dot(q * q, same_head) + EPS)
        ki = lax.rsqrt(split_dot(k * k, same_head) + EPS)
        m.qs[z] = (q * qi * hp[z, 2:3, :]).astype(B16)
        m.ks[z] = (k * ki).astype(B16)
        m.vs[z] = v.astype(B16)
        m.rq[z] = qi.astype(B16)
        m.rk[z] = ki.astype(B16)
        return carry

    lax.fori_loop(0, T, qkv, 0)
    zero16 = jnp.zeros((), B16)

    def expo(z, k, q_all, k_all):
        q_one = jnp.where(halves[k], q_all, zero16)
        left = jnp.concatenate([q_one, m.psi[...]], axis=1)
        right = jnp.concatenate([k_all, m.phi[...]], axis=1)
        return q_one, jnp.exp(dot_nt(left, right)).astype(B16)

    def attend(z, carry):
        q_all, k_all, v_all = m.qs[z], m.ks[z], m.vs[z]
        v_ones = jnp.concatenate([v_all, jnp.ones((M, hq), B16)], axis=1)
        mixed = inverse = None
        for k in range(hq // dm.hd):
            _, e = expo(z, k, q_all, k_all)
            both_ = dot(e, v_ones)
            inv = 1.0 / both_[:, hq:]
            one = both_[:, :hq] * inv
            mixed = one if mixed is None else jnp.where(halves[k], one, mixed)
            inverse = inv if inverse is None else jnp.where(halves[k], inv, inverse)
        m.o[z] = mixed.astype(B16)
        m.ol[z] = (mixed - mixed.astype(B16).astype(F32)).astype(B16)
        m.linv[z] = inverse
        return carry

    lax.fori_loop(0, TH, attend, 0)
    gather_until(3)
    lax.fori_loop(TH, T, attend, 0)

    o_all = all_z(m.o)
    for n in range(NCH):
        exchange(0, n, dot_nt(o_all, wrows_all(n, 3 * hq, hq)))
    tok_wait(1, m.dyb, dys)

    def out_grad(t, carry):
        d = (mod(1) * dys[t].astype(F32)).astype(B16)
        m.df[t] = d
        sums[7:8, :] += row_sum(d.astype(F32))
        return carry

    lax.fori_loop(0, T, out_grad, 0)
    exchange_wait(0)

    def second_norm(t, carry):
        a = both(0, t) + mod(6)
        m.ab[t] = a.astype(B16)
        normed, inv = ln(xs[t].astype(F32) + mod(0) * a)
        h2[t] = (normed * (1.0 + mod(3)) + mod(5)).astype(B16)
        m.n2[t] = normed.astype(B16)
        m.r2[t] = jnp.broadcast_to(inv, (Q, 128))
        return carry

    lax.fori_loop(0, T, second_norm, 0)
    exchange_sent(0)
    gather_until(4)
    transpose_into(m.xt, h2)
    transpose_into(m.xt2, m.df)

    root = 0.7978845608028654

    def hidden(k):
        lo_u, lo_d = dm.up + k * half, dm.down + k * half

        def up(z, carry):
            u = dot(whole(h2), wz(z, lo_u, half)) + hb[z, 0:1, k * half : (k + 1) * half]
            uu = u * u
            th = jnp.tanh(root * u * (1.0 + 0.044715 * uu))
            m.gk[z] = (0.5 * u * (1.0 + th)).astype(B16)
            m.duk[z] = (0.5 * (1.0 + th) + (0.5 * root) * u * (1.0 - th * th) * (1.0 + 0.134145 * uu)).astype(B16)
            return carry

        def down(z, carry):
            dg = dot(whole(m.df), wz(z, lo_d, half))
            du = (dg * m.duk[z].astype(F32)).astype(B16)
            m.duk[z] = du
            fsum[z, 0:1, k * half : (k + 1) * half] = row_sum(du.astype(F32))
            return carry

        lax.fori_loop(0, T, up, 0)
        gather_until(5 + 2 * k)
        lax.fori_loop(0, T, down, 0)

    def grads(k, begin):
        lo_u, lo_d = dm.up + k * half, dm.down + k * half

        def down_grad(z, carry):
            wstore(z, lo_d, half, dot(m.xt2[...], m.gk[z]))
            return carry

        def up_grad(z, carry):
            wstore(z, lo_u, half, dot(m.xt[...], m.duk[z]))
            return carry

        for pc, body in ((5 + 2 * k, down_grad), (4 + 2 * k, up_grad)):
            for h in range(2):
                lax.fori_loop(h * TH, (h + 1) * TH, body, 0)
                if begin:
                    rs_begin(pc, h)

    hidden(0)
    du_all, g_all = all_z(m.duk), all_z(m.gk)
    for n in range(NCH):
        m.dacc[n] = dot_nt(du_all, wrows_all(n, dm.up, half))
        m.facc[n] = dot_nt(g_all, wrows_all(n, dm.down, half))
    gather_sent((4, 5))
    grads(0, False)
    gather_until(6)
    for pc in (5, 4):
        for h in range(2):
            rs_begin(pc, h)
    hidden(1)
    du_all, g_all = all_z(m.duk), all_z(m.gk)
    for n in range(NCH):
        exchange(1, n, m.dacc[n] + dot_nt(du_all, wrows_all(n, dm.up + half, half)))
    for n in range(NCH):
        m.facc[n] = m.facc[n] + dot_nt(g_all, wrows_all(n, dm.down + half, half))
    gather_sent((0, 1, 2, 3, 6, 7))
    grads(1, True)
    transpose_into(m.xt, h1)
    tok_sent(1, m.dyb, dys)
    exchange_wait(1)

    def ln_back(e, normed, inv):
        return (e - jnp.mean(e, axis=-1, keepdims=True) - normed * jnp.mean(e * normed, axis=-1, keepdims=True)) * inv

    def mid_back(t, carry):
        dh = both(1, t)
        normed = m.n2[t].astype(F32)
        sums[3:4, :] += row_sum(dh * normed)
        sums[5:6, :] += row_sum(dh)
        step_back = ln_back(dh * (1.0 + mod(3)), normed, m.r2[t, :, 0:1])
        h2[t] = step_back.astype(B16)
        dx1 = dys[t].astype(F32) + step_back
        sums[0:1, :] += row_sum(dx1 * m.ab[t].astype(F32))
        da = (mod(0) * dx1).astype(B16)
        m.df[t] = da
        sums[6:7, :] += row_sum(da.astype(F32))
        return carry

    lax.fori_loop(0, T, mid_back, 0)
    exchange_sent(1)
    for n in range(NCH):
        exchange(2, n, m.facc[n])

    w_proj = jnp.concatenate([wz(z, 3 * hq, hq) for z in range(T)], axis=-1)
    do_all = dot(whole(m.df), w_proj).astype(B16)
    for z in range(T):
        m.do[z] = do_all[:, z * hq : (z + 1) * hq]
    transpose_into(m.xt2, m.df)
    dw = dot(m.xt2[...], all_z(m.o))
    for z in range(T):
        wstore(z, 3 * hq, hq, dw[:, z * hq : (z + 1) * hq])
    for h in range(2):
        rs_begin(3, h)
    pump(1)
    exchange_wait(2)

    def last(t, carry):
        f = both(2, t) + mod(7)
        m.n2[t] = (mod(0) * m.ab[t].astype(F32) + mod(1) * f).astype(B16)
        sums[1:2, :] += row_sum(dys[t].astype(F32) * f)
        return carry

    lax.fori_loop(0, T, last, 0)
    exchange_sent(2)
    back_start(0, m.outd)

    ends = jnp.where(lane < 2, -1.0, 0.0).astype(B16)

    def attend_back(z, carry):
        q_all, k_all, v_all = m.qs[z], m.ks[z], m.vs[z]
        dob = (m.do[z].astype(F32) * m.linv[z]).astype(B16)
        prod = dob.astype(F32) * (m.o[z].astype(F32) + m.ol[z].astype(F32))
        v_ends = jnp.concatenate([v_all, jnp.broadcast_to(ends, (M, hq))], axis=1)
        dq = dk = dv = 0.0
        for k in range(hq // dm.hd):
            q_one, e = expo(z, k, q_all, k_all)
            to_all = (bi == k).astype(B16)
            total = split_dot(prod, to_all)
            high = total.astype(B16)
            low = (total - high.astype(F32)).astype(B16)
            extra = jnp.where(lane == 0, high, jnp.where(lane == 1, low, zero16))
            d_one = jnp.where(halves[k], dob, zero16)
            dp = dot_nt(jnp.concatenate([d_one, extra], axis=1), v_ends)
            ds = (e.astype(F32) * dp).astype(B16)
            dq = dq + dot(ds, jnp.where(halves[k], k_all, zero16))
            dk = dk + dot_tn(ds, q_one)
            dv = dv + dot_tn(e, d_one)
        gain = hp[z, 2:3, :]
        q_hat = q_all.astype(F32) * hp[z, 3:4, :]
        k_hat = k_all.astype(F32)
        hsum[z, 2:3, :] = row_sum(dq * q_hat)
        eq = dq * gain
        dq = ((eq - q_hat * split_dot(eq * q_hat, same_head)) * m.rq[z].astype(F32)).astype(B16)
        dk = ((dk - k_hat * split_dot(dk * k_hat, same_head)) * m.rk[z].astype(F32)).astype(B16)
        dv = dv.astype(B16)
        hsum[z, 0:1, :] = row_sum(dq.astype(F32))
        hsum[z, 1:2, :] = row_sum(dv.astype(F32))
        m.dqkv[...] = jnp.concatenate([dq, dk, dv], axis=1)
        return carry

    for z in range(T):
        lax.fori_loop(z, z + 1, attend_back, 0)
        d_one_z = m.dqkv[...]
        for n in range(NCH):
            part = dot_nt(d_one_z, wrows(z, n, 0, 3 * hq))
            if z == T - 1:
                exchange(3, n, m.facc[n] + part)
            else:
                m.facc[n] = part if z == 0 else m.facc[n] + part
        wstore(z, 0, 3 * hq, dot(m.xt[...], d_one_z))
        if z % TH == TH - 1:
            for pc in (2, 1, 0):
                rs_begin(pc, z // TH)
        else:
            pump(2)

    if dm.inside:
        for z in range(T):
            m.pks[z] = jnp.concatenate([hsum[z], fsum[z], sums[...]], axis=-1)
        for off in range(1, T):
            small(m.pks.at[lax.rem(me_z + off, T)], m.pkr.at[off - 1], S_PZ + off - 1, z_dev(off)).start()
    pump(2)
    exchange_wait(3)

    def first_back(t, carry):
        dh = both(3, t)
        normed, inv = ln(xs[t].astype(F32))
        sums[2:3, :] += row_sum(dh * normed)
        sums[4:5, :] += row_sum(dh)
        m.ab[t] = (h2[t].astype(F32) + ln_back(dh * (1.0 + mod(2)), normed, inv)).astype(B16)
        return carry

    lax.fori_loop(0, T, first_back, 0)
    exchange_sent(3)
    back_start(1, m.gind)

    if dm.inside:
        for p in range(NC):
            d = pl.multiple_of((2 * p + core) * R, R)
            rows = [sums[j : j + 1, pl.ds(d, R)] for j in range(8)]
            m.b1s[p] = jnp.broadcast_to(jnp.concatenate(rows, axis=-1), (8, 8 * R))
        for k in range(1, NC):
            small(m.b1s.at[lax.rem(chip + k, NC)], m.b1r.at[k - 1], S_B1 + k - 1, chip_dev(k)).start()
        for off in range(1, T):
            small(m.pks.at[0], m.pkr.at[off - 1], S_PZ + off - 1, z_dev(off)).wait_recv()
        m.pka[0] = m.pks[me_z] + sum(m.pkr[k] for k in range(T - 1))
        if NB:
            sum_step(m.pka, m.pkb, 0, S_PB, 0).start()
        for k in range(1, NC):
            small(m.b1s.at[0], m.b1r.at[k - 1], S_B1 + k - 1, chip_dev(k)).wait_recv()
        row8 = lax.broadcasted_iota(jnp.int32, (8, 1), 0)
        packed = jnp.where(row8 == chip, m.b1s[chip], 0.0)
        for k in range(1, NC):
            packed = jnp.where(row8 == lax.rem(chip - k + NC, NC), m.b1r[k - 1], packed)
        m.dmodf[me_z] = packed
        for off in range(1, T):
            small(m.dmodf.at[me_z], m.dmodf.at[me_z], S_B2 + off - 1, z_dev(off)).start()
        pump(1)
        for off in range(1, T):
            got = m.dmodf.at[lax.rem(me_z - off + T, T)]
            small(got, got, S_B2 + off - 1, z_dev(off)).wait_recv()
        width = D // T
        for zz in range(T):
            acc = 0.0
            for j in range(6):
                acc = acc + dot_nt(m.dmodf[zz, :, j * R : (j + 1) * R].astype(B16), m.wada[j])
            m.bacc[0, :, zz * width : (zz + 1) * width] = acc
        sum_step(m.bacc, m.brec, 0, S_B3, 1).start()
        for i in range(NB + 1):
            if i < NB:
                sum_finish(m.pka, m.pkb, i, S_PB, 0)
                if i + 1 < NB:
                    sum_step(m.pka, m.pkb, i + 1, S_PB, 0).start()
            if i == NB:
                m.pk[core] = m.pka[NB]
                small(m.pka.at[NB], m.pk.at[core], S_PC, partner).start()
            sum_finish(m.bacc, m.brec, i, S_B3, 1)
            if i < NB:
                sum_step(m.bacc, m.brec, i + 1, S_B3, 1).start()
            pump(1)
        m.dsil[...] = m.bacc[NB + 1]
    pump(len(events))
    assert not events
    rs_end()
    tok_sent(0, m.xb, xs)
    back_wait(0, m.outd)
    back_wait(1, m.gind)
    sid_copy.wait_send()
    if dm.inside:
        for i in range(NB + 1):
            sum_step(m.macc, m.mrec, i, S_M1, 1).wait_send()
            sum_step(m.bacc, m.brec, i, S_B3, 1).wait_send()
        for i in range(NB):
            sum_step(m.pka, m.pkb, i, S_PB, 0).wait_send()
        for off in range(1, T):
            zt = lax.rem(me_z + off, T)
            small(m.sm.at[me_z], m.sm.at[me_z], S_SM + off - 1, z_dev(off)).wait_send()
            small(m.m2s.at[zt], m.m2r.at[off - 1], S_M2 + off - 1, z_dev(off)).wait_send()
            small(m.pks.at[zt], m.pkr.at[off - 1], S_PZ + off - 1, z_dev(off)).wait_send()
            small(m.dmodf.at[me_z], m.dmodf.at[me_z], S_B2 + off - 1, z_dev(off)).wait_send()
        for k in range(1, NC):
            small(m.m3c.at[core, chip], m.m3c.at[core, chip], S_M3 + k - 1, chip_dev(k)).wait_send()
            small(m.b1s.at[lax.rem(chip + k, NC)], m.b1r.at[k - 1], S_B1 + k - 1, chip_dev(k)).wait_send()
        small(m.m3c.at[core], m.m3c.at[core], S_M4, partner).wait_send()
        small(m.pka.at[NB], m.pk.at[core], S_PC, partner).wait_send()
        got = m.pk.at[1 - core]
        small(got, got, S_PC, partner).wait_recv()


def block_call(dm, ws, xb, dyb, sid, extra):
    T, NC, NB, Q, M, D, R, C, W = dm.T, dm.NC, dm.bits, dm.Q, dm.M, dm.D, dm.R, dm.C, dm.W
    hq, fu, NCH, half = dm.hq, dm.fu, dm.NCH, dm.half
    TH, NP = T // 2, len(dm.pieces)
    two = (2,) * NB
    v = pltpu.VMEM
    dma = pltpu.SemaphoreType.DMA
    any_, vm = pl.BlockSpec(memory_space=pl.ANY), pl.BlockSpec(memory_space=pltpu.VMEM)
    s = jax.ShapeDtypeStruct
    tok, heads, acc = (T, Q, D), (T, M, hq), (NCH, M, CHUNK)
    ins = {"ws": ws, "xb": xb, "dyb": dyb, "sid": sid, **extra}
    outs = {"fin": s((2, R, C), F32), "outd": s((2, Q, D), B16), "gind": s((2, Q, D), B16)}
    totals = {"sums": (8, D), "hsum": (T, 8, hq), "fsum": (T, 8, fu)}
    scratch = {"wall": v((T,) + two + (2 * R, C), B16)}
    for name in "xs dys h1 h2 ab n2 df".split():
        scratch[name] = v(tok, B16)
    for name in "qs ks vs rq rk o ol do".split():
        scratch[name] = v(heads, B16)
    scratch.update(
        linv=v(heads, F32), r2=v((T, Q, 128), F32), psi=v((M, 128), B16), phi=v((M, 128), B16), sidr=v((8, M), F32),
        gk=v((T, M, half), B16), duk=v((T, M, half), B16), facc=v(acc, F32), dacc=v(acc, F32),
        send=v((NCH, T, Q, CHUNK), B16), recv=v((2, NCH, T, Q, CHUNK), B16),
        xt=v((D, M), B16), xt2=v((D, M), B16), dqkv=v((M, 3 * hq), B16),
        zb=v((T - 1, 2 * R, C), B16), fbuf=v((R, C), F32),
    )
    for k in range(NB):
        scratch[f"rb{k}"] = v((SLOTS, 2, TH) + (2,) * (NB - 1 - k) + (2 * R, half), B16)
    if dm.inside:
        outs.update(dmodf=s((T, 8, 8 * R), F32), cond=s((8, D), F32), dsil=s((8, D), F32), pk=s((2, 8, W), F32))
        scratch.update({name: v(shape, F32) for name, shape in totals.items()})
        scratch.update(
            mods=v((8, D), F32), hp=v((T, 8, hq), F32), hb=v((T, 8, fu), F32),
            macc=v((NB + 2, 16, D), F32), mrec=v((NB + 1, 16, D), F32), sm=v((T, 8, D), F32),
            m2s=v((T, 8, 8 * R), F32), m2r=v((T - 1, 8, 8 * R), F32), m3c=v((2, NC, 8, 8 * R), F32),
            b1s=v((NC, 8, 8 * R), F32), b1r=v((NC, 8, 8 * R), F32),
            bacc=v((NB + 2, 8, D), F32), brec=v((NB + 1, 8, D), F32),
            pks=v((T, 8, W), F32), pkr=v((T - 1, 8, W), F32), pka=v((NB + 1, 8, W), F32), pkb=v((max(NB, 1), 8, W), F32),
        )
    else:
        outs.update({name: s(shape, F32) for name, shape in totals.items()})
    small = 4 * NB + 6 * T + 2 * NC + 8
    reg = pltpu.SemaphoreType.REGULAR
    scratch.update(
        c_s=dma((NP,)), c_r=dma((NP,)), c_l=dma((NP,)), z_s=dma((NP, T - 1)), z_r=dma((NP, T - 1)),
        p_s=dma((NP, NB, 2)), p_r=dma((NP, NB, 2)), x_s=dma((2, 2)), x_r=dma((2, T)), x_l=dma((2,)), x_f=dma((2, 2)),
        e_s=dma((4, NCH)), e_r=dma((4, NCH)), rs_s=dma((NP, NB, 2)), rs_r=dma((NP, NB, 2)), free=reg((NB, 2)),
        rz_s=dma((NP, T - 1)), rz_r=dma((NP, T - 1)), f_s=dma((NP,)), f_r=dma((NP,)),
        o_s=dma((2, T)), o_r=dma((2, 2)), o_l=dma((2,)), s_s=dma((small,)), s_r=dma((small,)),
    )
    names = tuple(ins) + tuple(outs) + tuple(scratch)
    got = pl.pallas_call(
        functools.partial(block_kernel, dm, names),
        out_shape=tuple(outs.values()),
        in_specs=[any_ if name in ("ws", "xb", "dyb") else vm for name in ins],
        out_specs=tuple(any_ if name in ("outd", "gind") else vm for name in outs),
        scratch_shapes=list(scratch.values()),
        compiler_params=pltpu.CompilerParams(
            collective_id=0, has_side_effects=True, vmem_limit_bytes=66 * 1024 * 1024
        ),
        cost_estimate=pl.CostEstimate(flops=30 * 10**9, bytes_accessed=10**7, transcendentals=10**7),
    )(*ins.values())
    return dict(zip(outs, got))


def local(
    dp, tensor,
    block_input, cotangent, class_ids, scale_ids, class_table, w_ada, b_ada, query_key_value_weight,
    qv_bias, q_gain, output_projection, up_weight, hidden_bias, down_weight, projection_bias,
):
    seqs, quarter, width = block_input.shape
    length = scale_ids.shape[1]
    assert seqs == 2 and tensor == 4
    rows = -(-quarter // 16) * 16
    head = q_gain.shape[1] * dp
    hidden = up_weight.shape[1] * tensor
    dm = Dims(dp, tensor, rows, width, head, hidden)
    T, R, hq, fu, NC, M = dm.T, dm.R, dm.hq, dm.fu, dm.NC, dm.M
    total = class_ids.shape[0]
    di, zi = lax.axis_index("dp"), lax.axis_index("tensor")
    core = di % 2

    pad_rows = ((0, 0), (0, 0), (0, rows - quarter))
    sid = jnp.pad(scale_ids.astype(F32).reshape(2, T, quarter), pad_rows, constant_values=127.0).reshape(2, M)
    sid = jnp.pad(sid, ((0, 6), (0, 0)))
    my_rows = class_table.shape[0]
    my_ids = di * my_rows + jnp.arange(my_rows, dtype=jnp.int32)

    if dm.inside:
        place = jnp.arange(dp, dtype=jnp.int32) == di

        def spread(w):
            return jnp.where(place[:, None], w[..., None, :], 0).reshape(w.shape[:-2] + (-1,)).astype(F32)

        def pad_lanes(w):
            return jnp.pad(w, ((0, 0), (0, width - w.shape[1])))

        hot = (class_ids[:, None] == my_ids[None, :]).astype(B16)
        cond = jnp.dot(hot, class_table, preferred_element_type=F32).reshape(NC, -1)
        tiny = [spread(hidden_bias)[None], spread(qv_bias), spread(q_gain)[None]]
        tiny = jnp.concatenate([pad_lanes(w) for w in tiny], axis=0)
        m1 = jnp.concatenate([jnp.pad(cond, ((0, 8 - NC), (0, 0))), jnp.pad(tiny, ((0, 4), (0, 0)))], axis=0)
        badd = jnp.concatenate([b_ada, projection_bias], axis=0).astype(F32).reshape(1, -1)
        extra = {"m1": m1, "wada": jnp.moveaxis(w_ada, 1, 0), "badd": badd}
    else:
        hot = (class_ids[:, None] == my_ids[None, :]).astype(B16)
        cond = lax.psum(jnp.dot(hot, class_table, preferred_element_type=F32), "dp")
        silu, silu_back = jax.vjp(jax.nn.silu, cond)
        silu_low = silu.astype(B16)
        parts = jnp.einsum("sc,cjd->sjd", silu_low, w_ada, preferred_element_type=F32)
        parts = parts.reshape((NC, T) + parts.shape[1:])
        mine = lax.psum_scatter(parts, "tensor", scatter_dimension=1, tiled=True)[:, 0] + b_ada.astype(F32)
        spread = lax.all_to_all(jnp.repeat(mine, 2, axis=0), "dp", 0, 0, tiled=True)
        modulation = jnp.moveaxis(spread, 0, 1).reshape(6, width)

        pieces = [qv_bias, q_gain, hidden_bias, projection_bias]
        flat = jnp.concatenate([p.reshape(-1) for p in pieces])
        everyone = lax.all_gather(lax.all_gather(flat, "tensor"), "dp")
        cut, at = [], 0
        for p in pieces:
            cut.append(everyone[:, :, at : at + p.size].reshape((dp, T) + p.shape).astype(F32))
            at += p.size
        qv_all = cut[0].transpose(2, 1, 3, 0, 4).reshape(2, T, 2, hq)[:, :, core]
        gain_all = cut[1].transpose(1, 2, 0, 3).reshape(T, 2, hq)[:, core]
        hidden_all = cut[2].transpose(1, 2, 0, 3).reshape(T, 2, fu)[:, core]
        out_bias = cut[3][:, 0].transpose(1, 0, 2).reshape(2, width)
        mods = jnp.concatenate([modulation, out_bias], axis=0)
        hp = jnp.stack([qv_all[0], qv_all[1], gain_all, 1.0 / gain_all], axis=1)
        hp = jnp.concatenate([hp, jnp.zeros_like(hp)], axis=1)
        hb = jnp.broadcast_to(hidden_all[:, None], (T, 8, fu))

        extra = {"mods": mods, "hp": hp, "hb": hb}

    def halves(w):
        return jnp.moveaxis(w.reshape(w.shape[:-1] + (2, w.shape[-1] // 2)), -2, 0)

    qkv_half = halves(query_key_value_weight)
    ws = jnp.concatenate(
        [qkv_half[:, 0], qkv_half[:, 1], qkv_half[:, 2], halves(output_projection.T), halves(up_weight), halves(down_weight.T)],
        axis=-1,
    )
    pad = ((0, 0), (0, rows - quarter), (0, 0))
    xb = jnp.pad(block_input.astype(B16), pad)
    dyb = jnp.pad(cotangent.astype(B16), pad)

    got = block_call(dm, ws, xb, dyb, sid, extra)
    fin, outd, gind = got["fin"], got["outd"], got["gind"]

    block_output = block_input + outd[:, :quarter].astype(F32)
    input_grad = cotangent + gind[:, :quarter].astype(F32)

    def joined(lo, n):
        return jnp.moveaxis(fin[:, :, lo : lo + n], 0, 1).reshape(R, 2 * n)

    w_qkv_grad = jnp.stack([joined(k * hq, hq) for k in range(3)])
    w_proj_grad = joined(3 * hq, hq).T
    w_fc1_grad = joined(dm.up, fu)
    w_fc2_grad = joined(dm.down, fu).T

    if dm.inside:
        cond = got["cond"][:NC].reshape(total, -1)
        silu, silu_back = jax.vjp(jax.nn.silu, cond)
        dmod = jnp.swapaxes(got["dmodf"][:, :NC], 0, 1).reshape(total, 8, R)[:, :6].astype(B16)
        b_ada_grad = jnp.sum(dmod.astype(F32), axis=0)
        w_ada_grad = jnp.einsum("sc,sjd->cjd", silu.astype(B16), dmod, preferred_element_type=F32)
        (d_cond,) = silu_back(got["dsil"][:NC].reshape(total, -1))
        pk = got["pk"]

        def own(w, n):
            return lax.dynamic_slice_in_dim(w, di * n, n, w.ndim - 1)

        heads = own(jnp.swapaxes(pk[:, :3, :hq], 0, 1).reshape(3, -1, head), head // dp)
        qv_bias_grad, q_gain_grad = heads[:2], heads[2]
        b_fc1_grad = own(pk[:, 0, hq : hq + fu].reshape(hidden_bias.shape[0], -1), hidden_bias.shape[1])
        b_out_grad = own(pk[0, 6:8, hq + fu :], R)
    else:
        sums, hsum, fsum = got["sums"], got["hsum"], got["fsum"]
        dmod = sums[:6].reshape(6, dp, R).astype(B16)
        dmod = lax.all_to_all(jnp.moveaxis(dmod, 1, 0), "dp", 0, 0, tiled=True)
        dmod = lax.all_gather(dmod[::2], "tensor", axis=1)
        dmod = dmod.reshape((total, 6, R))
        b_ada_grad = jnp.sum(dmod.astype(F32), axis=0)
        w_ada_grad = jnp.einsum("sc,sjd->cjd", silu_low, dmod, preferred_element_type=F32)
        d_silu = lax.psum(jnp.einsum("sjd,cjd->sc", dmod, w_ada, preferred_element_type=F32), "dp")
        (d_cond,) = silu_back(d_silu)

        vec = jnp.concatenate([hsum[:, :3].reshape(-1), fsum[:, 0].reshape(-1), sums[6:].reshape(-1) * 0.5])
        nh, nf = T * 3 * hq, T * fu
        place_ = jnp.arange(2, dtype=jnp.int32) == core
        by_core = jnp.where(place_[:, None], vec[None, : nh + nf], 0.0).reshape(-1)
        vec = lax.psum(jnp.concatenate([by_core, vec[nh + nf :]]), ("dp", "tensor"))
        by_core = vec[: 2 * (nh + nf)].reshape(2, nh + nf)
        heads = by_core[:, :nh].reshape(2, T, 3, hq)
        heads = lax.dynamic_index_in_dim(heads, zi, 1, keepdims=False)
        heads = jnp.moveaxis(heads, 0, 1).reshape(3, -1, head)
        step = head // dp
        heads = lax.dynamic_slice_in_dim(heads, di * step, step, 2)
        qv_bias_grad, q_gain_grad = heads[:2], heads[2]
        fc1 = lax.dynamic_index_in_dim(by_core[:, nh:].reshape(2, T, fu), zi, 1, keepdims=False)
        fc1 = fc1.reshape(-1, hidden_bias.shape[1] * dp)
        step = hidden_bias.shape[1]
        b_fc1_grad = lax.dynamic_slice_in_dim(fc1, di * step, step, 1)
        b_out_grad = lax.dynamic_slice_in_dim(vec[2 * (nh + nf) :].reshape(2, width), di * R, R, 1)

    table_grad = jnp.dot(hot.astype(F32).T, d_cond, precision=lax.Precision.HIGHEST, preferred_element_type=F32)

    return (
        block_output, input_grad, table_grad, w_ada_grad, b_ada_grad, w_qkv_grad, qv_bias_grad, q_gain_grad,
        w_proj_grad, w_fc1_grad, b_fc1_grad, w_fc2_grad, b_out_grad,
    )


def solution(mesh):
    dp, tensor = mesh.shape["dp"], mesh.shape["tensor"]
    return jax.shard_map(
        functools.partial(local, dp, tensor),
        mesh=mesh,
        in_specs=(
            P("dp", "tensor", None),
            P("dp", "tensor", None),
            P(),
            P("dp", None),
            P("dp", "tensor"),
            P("tensor", None, "dp"),
            P(None, "dp"),
            P(None, "dp", "tensor"),
            P(None, "tensor", "dp"),
            P("tensor", "dp"),
            P("tensor", "dp"),
            P("dp", "tensor"),
            P("tensor", "dp"),
            P("tensor", "dp"),
            P(None, "dp"),
        ),
        out_specs=(
            P("dp", "tensor", None),
            P("dp", "tensor", None),
            P("dp", "tensor"),
            P("tensor", None, "dp"),
            P(None, "dp"),
            P(None, "dp", "tensor"),
            P(None, "tensor", "dp"),
            P("tensor", "dp"),
            P("tensor", "dp"),
            P("dp", "tensor"),
            P("tensor", "dp"),
            P("tensor", "dp"),
            P(None, "dp"),
        ),
        check_vma=False,
    )
```

```python
import functools

import jax
import jax.numpy as jnp
from jax import lax
from jax.experimental import pallas as pl
from jax.experimental.pallas import tpu as pltpu
from jax.sharding import PartitionSpec as P

MESH = pl.DeviceIdType.MESH
F32, B16 = jnp.float32, jnp.bfloat16
FINS = 3
SLOTS = 3
PUMPS = (0, 0, 0, 1, 2, 3, 3, 2, 2, 2, 2, 2, 2, 2)
BEGIN = ((), ((2, 0),), ((1, 0),), ((2, 1), (1, 1), (0, 0), (0, 1)))
LEAN = 1.5
CHUNK = 256
EPS = 1e-06
FAR = 256.0


def dot(a, b):
    return lax.dot_general(a, b, (((1,), (0,)), ((), ())), preferred_element_type=F32)


def dot_nt(a, b):
    return lax.dot_general(a, b, (((1,), (1,)), ((), ())), preferred_element_type=F32)


def dot_tn(a, b):
    return lax.dot_general(a, b, (((0,), (0,)), ((), ())), preferred_element_type=F32)


def split_dot(a, b):
    high = a.astype(B16)
    low = (a - high.astype(F32)).astype(B16)
    return dot(high, b) + dot(low, b)


def row_sum(a):
    return jnp.sum(a, axis=0, keepdims=True)


class Dims:
    def __init__(self, dp, tensor, rows, width, head, hidden):
        self.T = tensor
        self.NC = dp // 2
        self.bits = self.NC.bit_length() - 1
        self.Q = rows
        self.M = rows * tensor
        self.D = width
        self.hd = head
        self.hq = width // tensor // 2
        self.fu = hidden // tensor // 2
        self.R = width // dp
        self.C = 4 * self.hq + 2 * self.fu
        self.NCH = width // CHUNK
        self.inside = self.R % 128 == 0 and self.NC <= 8 and hidden // tensor <= width
        self.W = self.hq + self.fu + width
        hq, fu, half = self.hq, self.fu, self.fu // 2
        up, down = 4 * hq, 4 * hq + fu
        self.up, self.down, self.half = up, down, half
        self.pieces = ((0, hq), (hq, hq), (2 * hq, hq), (3 * hq, hq), (up, half), (down, half), (up + half, half), (down + half, half))
        self.sums_order = (5, 4, 7, 6, 3, 2, 1, 0)
        assert 1 << self.bits == self.NC


class Refs:
    pass


def block_kernel(dm, names, *refs):
    m = Refs()
    for name, ref in zip(names, refs):
        if name.startswith("rb"):
            m.rb = getattr(m, "rb", []) + [ref]
        else:
            setattr(m, name, ref)
    T, NC, NB, Q, M, D, R, C = dm.T, dm.NC, dm.bits, dm.Q, dm.M, dm.D, dm.R, dm.C
    hq, fu, NCH, half = dm.hq, dm.fu, dm.NCH, dm.half
    TH = T // 2
    NP = len(dm.pieces)
    wall, xs, dys, h1, h2 = m.wall, m.xs, m.dys, m.h1, m.h2
    mods, hp, hb, sums, hsum, fsum = m.mods, m.hp, m.hb, m.sums, m.hsum, m.fsum
    dpi = lax.axis_index("dp")
    me_z = lax.axis_index("tensor")
    core = lax.rem(dpi, 2)
    chip = dpi // 2
    mybit = [lax.rem(chip // (1 << b), 2) for b in range(NB)]
    partner = (dpi + 1 - 2 * core, me_z)

    def tag_z(dev):
        return dev

    def z_dev(off):
        return (dpi, lax.rem(me_z + off, T))

    def bit_dev(b):
        return (dpi + (1 - 2 * mybit[b]) * (2 << b), me_z)

    def chip_dev(k):
        return (lax.rem(chip + k, NC) * 2 + core, me_z)

    bar = pltpu.get_barrier_semaphore()
    friends = [partner] + [z_dev(k) for k in range(1, T)]
    friends += [chip_dev(k) for k in range(1, NC)] if dm.inside else [bit_dev(b) for b in range(NB)]
    for dev in friends:
        pl.semaphore_signal(bar, inc=1, device_id=dev, device_id_type=MESH)
    pl.semaphore_wait(bar, len(friends))

    def rdma(src, dst, ss, rs, dev):
        return pltpu.make_async_remote_copy(
            src_ref=src, dst_ref=dst, send_sem=ss, recv_sem=rs, device_id=dev, device_id_type=MESH
        )

    every = slice(None)

    def place(fixed):
        return tuple(fixed.get(b, every) for b in reversed(range(NB)))

    mine = place({b: mybit[b] for b in range(NB)})

    def cols(pc):
        return pl.ds(*dm.pieces[pc])

    def core_rows(c):
        return pl.ds(pl.multiple_of(c * R, R), R)

    def lanes_of(start, n):
        return pl.ds(pl.multiple_of(start, 128), n)

    def own_weight(pc, c):
        if pc < 3:
            return m.wqkv.at[pc, :, lanes_of(c * hq, hq)]
        if pc == 3:
            return m.gk.at[0, 128 : 128 + R, lanes_of(c * hq, hq)]
        k = (pc - 4) // 2
        if pc % 2 == 0:
            return m.wup.at[:, lanes_of(c * fu + k * half, half)]
        return m.gk.at[2 * c + k, 0:R, :]

    def transpose_own():
        m.gk[0, 128 : 128 + R, :] = m.wproj[...].T
        for i in range(4):
            m.gk[i, 0:R, :] = m.wdown[i * half : (i + 1) * half, :].T

    def core_copy(pc):
        dst = wall.at[(me_z,) + mine + (core_rows(core), cols(pc))]
        return rdma(own_weight(pc, 1 - core), dst, m.c_s.at[pc], m.c_r.at[pc], partner)

    def core_local(pc):
        dst = wall.at[(me_z,) + mine + (core_rows(core), cols(pc))]
        return pltpu.make_async_copy(own_weight(pc, core), dst, m.c_l.at[pc])

    def z_copy(pc, off):
        part = wall.at[(me_z,) + mine + (every, cols(pc))]
        return rdma(part, part, m.z_s.at[pc, off - 1], m.z_r.at[pc, off - 1], z_dev(off))

    inner = jnp.logical_and(me_z > 0, me_z < T - 1)
    line_sends = ((2, me_z >= 0), (1, me_z < T - 1), (3, me_z > 0))

    def z_landed(pc, off):
        part = wall.at[(lax.rem(me_z - off + T, T),) + mine + (every, cols(pc))]
        rdma(part, part, m.z_s.at[pc, off - 1], m.z_r.at[pc, off - 1], z_dev(off)).wait_recv()

    def z_forward(pc):
        part = wall.at[(lax.rem(me_z + 2, T),) + mine + (every, cols(pc))]
        up = lax.rem(me_z + 1, 2)
        return rdma(part, part, m.z_f.at[pc], m.z_r.at[pc, 2 * up], tag_z((dpi, me_z + 2 * up - 1)))

    order = [list(range(NB)), list(reversed(range(NB)))]

    def half_z(h):
        return pl.ds(h * TH, TH)

    def p_copy(pc, step, h, landing):
        b = order[h][step]
        fixed = {k: mybit[k] for k in order[h][step:]}
        if landing:
            fixed[b] = 1 - mybit[b]
        part = wall.at[(half_z(h),) + place(fixed) + (every, cols(pc))]
        return rdma(part, part, m.p_s.at[pc, step, h], m.p_r.at[pc, step, h], bit_dev(b))

    def gather_stage(pc, s):
        if not 0 <= pc < NP:
            return
        if s == 0:
            core_local(pc).wait()
            other = wall.at[(me_z,) + mine + (core_rows(1 - core), cols(pc))]
            rdma(other, other, m.c_s.at[pc], m.c_r.at[pc], partner).wait_recv()
            for off, allowed in line_sends:
                @pl.when(allowed)
                def _():
                    z_copy(pc, off).start()
            return
        if s == -1:
            @pl.when(inner)
            def _():
                z_landed(pc, 2)
                z_forward(pc).start()
            return
        if s == 1:
            z_landed(pc, 1)
            z_landed(pc, 3)

            @pl.when(jnp.logical_not(inner))
            def _():
                z_landed(pc, 2)
        for h in range(2):
            if s > 1:
                p_copy(pc, s - 2, h, True).wait_recv()
            if s <= NB:
                p_copy(pc, s - 1, h, False).start()

    starts = [(pc - 2.2, pc, 0) for pc in range(NP)] + [(pc - 1.1, pc, -1) for pc in range(NP)]
    starts += [(pc + 1.1 * (s - 1), pc, s) for pc in range(NP) for s in range(1, NB + 1)]
    if NB == 2:
        starts[starts.index((4 + 1.1, 4, 2))] = (4.95, 4, 2)
    starts.sort()

    here = [0]

    def gather_to(key):
        while starts and starts[0][0] <= key:
            gather_stage(*starts.pop(0)[1:])

    def gather_until(pc):
        gather_to(pc + 1.1 * NB)
        while here[0] <= pc:
            gather_stage(here[0], NB + 1)
            here[0] += 1

    def gather_sent(which):
        for pc in which:
            for off, allowed in line_sends:
                @pl.when(allowed)
                def _():
                    z_copy(pc, off).wait_send()

            @pl.when(inner)
            def _():
                z_forward(pc).wait_send()

            for step in range(NB):
                for h in range(2):
                    p_copy(pc, step, h, False).wait_send()

    owner = me_z // 2 == core

    def tok_copy(which, src, dst, i):
        zt = 2 * core + i
        return rdma(src.at[i], dst.at[me_z], m.x_s.at[which, i], m.x_r.at[which, me_z], (dpi, zt))

    def tok_start(which, src, dst):
        for i in range(2):
            @pl.when(2 * core + i != me_z)
            def _():
                tok_copy(which, src, dst, i).start()

            @pl.when(2 * core + i == me_z)
            def _():
                pltpu.make_async_copy(src.at[i], dst.at[me_z], m.x_l.at[which]).start()

    def tok_forward(which, dst):
        return rdma(dst, dst, m.x_f.at[which, 0], m.x_f.at[which, 1], partner)

    def tok_wait(which, src, dst):
        @pl.when(owner)
        def _():
            for off in range(1, T):
                zq = lax.rem(me_z + off, T)
                rdma(dst.at[zq], dst.at[zq], m.x_s.at[which, 0], m.x_r.at[which, zq], (dpi, zq)).wait_recv()
            pltpu.make_async_copy(src.at[0], dst.at[me_z], m.x_l.at[which]).wait()
            tok_forward(which, dst).start()

        @pl.when(jnp.logical_not(owner))
        def _():
            tok_forward(which, dst).wait_recv()

    def tok_sent(which, src, dst):
        for i in range(2):
            @pl.when(2 * core + i != me_z)
            def _():
                tok_copy(which, src, dst, i).wait_send()

        @pl.when(owner)
        def _():
            tok_forward(which, dst).wait_send()

    back_from = (m.n2, m.ab)

    def back_copy(which, dst, zq):
        i = lax.rem(me_z, 2)
        return rdma(back_from[which].at[zq], dst.at[i], m.o_s.at[which, zq], m.o_r.at[which, i], (dpi, zq))

    def back_start(which, dst):
        @pl.when(owner)
        def _():
            for off in range(1, T):
                back_copy(which, dst, lax.rem(me_z + off, T)).start()
            pltpu.make_async_copy(back_from[which].at[me_z], dst.at[lax.rem(me_z, 2)], m.o_l.at[which]).start()

    def back_wait(which, dst):
        @pl.when(owner)
        def _():
            for off in range(1, T):
                back_copy(which, dst, lax.rem(me_z + off, T)).wait_send()
            pltpu.make_async_copy(back_from[which].at[me_z], dst.at[lax.rem(me_z, 2)], m.o_l.at[which]).wait()

        for i in range(2):
            @pl.when(2 * core + i != me_z)
            def _():
                rdma(dst.at[i], dst.at[i], m.o_s.at[which, 0], m.o_r.at[which, i], (dpi, 2 * core + i)).wait_recv()

    def sender(k):
        return m.duk if k == 2 and m.duk.shape == m.send.shape else m.send

    def x_copy(k, n):
        return rdma(sender(k).at[n], m.recv.at[k % 2, n], m.e_s.at[k, n], m.e_r.at[k, n], partner)

    def exchange(k, n, value):
        sender(k)[n] = value.astype(B16)
        x_copy(k, n).start()

    def exchange_wait(k):
        for n in range(NCH):
            x_copy(k, n).wait_recv()

    def exchange_sent(k):
        for n in range(NCH):
            x_copy(k, n).wait_send()

    def both(k, t):
        rows = pl.ds(pl.multiple_of(t * Q, 16), Q)
        parts = [sender(k)[n, rows, :].astype(F32) + m.recv[k % 2, n, rows, :].astype(F32) for n in range(NCH)]
        return jnp.concatenate(parts, axis=-1)

    def wz(z, lo, n):
        return wall[(z,) + (every,) * NB + (every, pl.ds(lo, n))].reshape(D, n)

    def wrows(z, n, lo, width):
        per = CHUNK // (2 * R)
        low = per.bit_length() - 1
        top = n * per
        fixed = {b: (top >> b) & 1 for b in range(low, NB)}
        return wall[(z,) + place(fixed) + (every, pl.ds(lo, width))].reshape(CHUNK, width)

    def wrows_all(n, lo, width):
        return jnp.concatenate([wrows(z, n, lo, width) for z in range(T)], axis=-1)

    def wstore(z, lo, n, value):
        wall[(z,) + (every,) * NB + (every, pl.ds(lo, n))] = value.astype(B16).reshape(
            (2,) * NB + (2 * R, n)
        )

    def all_z(ref):
        return jnp.concatenate([ref[z] for z in range(T)], axis=-1)

    def whole(ref):
        return ref[...].reshape(M, D)

    def mod(r):
        return mods[r : r + 1, :]

    def transpose_into(dst, ref):
        for n in range(D // 128):
            block = ref[:, :, n * 128 : (n + 1) * 128].reshape(M, 128)
            dst[n * 128 : (n + 1) * 128, :] = block.T

    place_of = {pc: j for j, pc in enumerate(dm.sums_order)}

    def rs_fixed(step, h, away):
        order_r = order[h][::-1]
        fixed = {k: mybit[k] for k in order_r[: step + 1]}
        b = order_r[step]
        if away:
            fixed[b] = 1 - mybit[b]
        return b, fixed

    def rs_copy(j, step, h):
        pc = dm.sums_order[j]
        b, fixed = rs_fixed(step, h, True)
        part = wall.at[(half_z(h),) + place(fixed) + (every, cols(pc))]
        buf = m.rb[step].at[(j % SLOTS, h) + (every,) * (NB - step) + (every, pl.ds(0, dm.pieces[pc][1]))]
        return rdma(part, buf, m.rs_s.at[j, step, h], m.rs_r.at[j, step, h], bit_dev(b))

    def rs_start(j, step, h):
        if j >= SLOTS:
            pl.semaphore_wait(m.free.at[step, h], 1)
        rs_copy(j, step, h).start()

    def rs_add(j, step, h):
        pc = dm.sums_order[j]
        rs_copy(j, step, h).wait_recv()
        b, fixed = rs_fixed(step, h, False)
        rest = [k for k in reversed(range(NB)) if k not in fixed]
        slot, width = j % SLOTS, dm.pieces[pc][1]

        def one(i, carry):
            zz, r = i // (1 << len(rest)), lax.rem(i, 1 << len(rest))
            at = dict(fixed)
            inner = ()
            for pos, k in enumerate(rest):
                v = lax.rem(r // (1 << (len(rest) - 1 - pos)), 2)
                at[k] = v
                inner += (v,)
            where = (h * TH + zz,) + place(at) + (every, cols(pc))
            got = m.rb[step][(slot, h, zz) + inner + (every, pl.ds(0, width))]
            wall[where] = (wall[where].astype(F32) + got.astype(F32)).astype(B16)
            return carry

        lax.fori_loop(0, TH << len(rest), one, 0)
        if j + SLOTS < NP:
            pl.semaphore_signal(m.free.at[step, h], inc=1, device_id=bit_dev(b), device_id_type=MESH)

    def rz_copy(j, off):
        pc = dm.sums_order[j]
        part = wall.at[(lax.rem(me_z + off, T),) + mine + (every, cols(pc))]
        return rdma(part, m.zb.at[off - 1, :, cols(pc)], m.rz_s.at[j, off - 1], m.rz_r.at[j, off - 1], z_dev(off))

    def rz_special(j):
        pc = dm.sums_order[j]
        far = T - 1 - me_z
        part = wall.at[(far,) + mine + (every, cols(pc))]
        return rdma(part, m.zx.at[:, cols(pc)], m.rx.at[j, 0], m.rx.at[j, 1], tag_z((dpi, jnp.where(me_z == 0, 1, T - 2))))

    ends_here = jnp.logical_not(inner)

    def rz_begin(j):
        @pl.when(ends_here)
        def _():
            rz_special(j).start()
            rz_copy(j, 2).start()

        for off, allowed in line_sends[1:]:
            @pl.when(allowed)
            def _():
                rz_copy(j, off).start()

    def rz_middle(j):
        pc = dm.sums_order[j]

        @pl.when(inner)
        def _():
            got = m.zx.at[:, cols(pc)]
            rdma(got, got, m.rx.at[j, 0], m.rx.at[j, 1], tag_z((dpi, me_z))).wait_recv()
            where = (lax.rem(me_z + 2, T),) + mine + (every, cols(pc))
            wall[where] = (wall[where].astype(F32) + m.zx[:, cols(pc)].astype(F32)).astype(B16)
            rz_copy(j, 2).start()

    def rz_wait(j):
        rz_copy(j, 2).wait_recv()
        for off, came in ((1, me_z > 0), (3, me_z < T - 1)):
            @pl.when(came)
            def _():
                rz_copy(j, off).wait_recv()

    def rz_sent(j):
        rz_copy(j, 2).wait_send()
        for off, allowed in line_sends[1:]:
            @pl.when(allowed)
            def _():
                rz_copy(j, off).wait_send()

        @pl.when(ends_here)
        def _():
            rz_special(j).wait_send()

    def final(pc, c):
        if pc < 3:
            return m.g_qkv, (pc, every, lanes_of(c * hq, hq))
        if pc == 3:
            return m.g_proj, (pl.ds(pl.multiple_of(c * hq, hq), hq), every)
        at = c * fu + (pc - 4) // 2 * half
        if pc % 2 == 0:
            return m.g_up, (every, lanes_of(at, half))
        return m.g_down, (pl.ds(pl.multiple_of(at, half), half), every)

    def turned(pc):
        return pc in (3, 5, 7)

    def fin_from(j):
        pc = dm.sums_order[j]
        width = dm.pieces[pc][1]
        if turned(pc):
            return m.fturn, (j // 2 % 2, pl.ds(0, width))
        return m.fbuf, (j % FINS, every, pl.ds(0, width))

    def fin_copy(j):
        pc = dm.sums_order[j]
        ref, at = fin_from(j)
        out, place_ = final(pc, core)
        return rdma(ref.at[at], out.at[place_], m.f_s.at[j], m.f_r.at[j], partner)

    def rs_event(j, s):
        pc = dm.sums_order[j]
        if s <= NB:
            for h in range(2):
                rs_add(j, s - 1, h)
                if s < NB:
                    rs_start(j, s, h)
            if s == NB:
                rz_begin(j)
            return
        if s == NB + 1:
            rz_middle(j)
            return
        rz_wait(j)

        def total(rows):
            acc = wall[(me_z,) + mine + (rows, cols(pc))].astype(F32)
            for off in range(1, T):
                acc = acc + m.zb[off - 1, rows, cols(pc)].astype(F32)
            return acc

        if j >= FINS:
            fin_copy(j - FINS).wait_send()
        ref, at = fin_from(j)
        out, place_ = final(pc, core)
        away, kept = total(core_rows(1 - core)), total(core_rows(core))
        ref[at] = away.T if turned(pc) else away
        fin_copy(j).start()
        out[place_] = kept.T if turned(pc) else kept

    events = sorted(((j, s) for j in range(NP) for s in range(1, NB + 3)), key=lambda e: (e[0] + LEAN * e[1], e[0]))
    begun = set()

    def pump(count):
        while count and events and (events[0][0], 1) in begun:
            rs_event(*events.pop(0))
            count -= 1

    stops = list(PUMPS)

    def stop():
        pump(stops.pop(0) if stops else 0)

    def rs_begin(pc, h):
        j = place_of[pc]
        while (j - SLOTS, 1) in events:
            pump(1)
        rs_start(j, 0, h)
        begun.add((j, h))

    def rs_end():
        for j in range(NP):
            for step in range(NB):
                for h in range(2):
                    rs_copy(j, step, h).wait_send()
            rz_sent(j)
            fin_copy(j).wait_recv()
            if j + FINS >= NP:
                fin_copy(j).wait_send()

    def small(src, dst, k, dev):
        return rdma(src, dst, m.s_s.at[k], m.s_r.at[k], dev)

    def sum_step(acc, got, i, base, sign, rows=None):
        dev = partner if i < sign else bit_dev(i - sign)
        n = acc.shape[1] if rows is None else rows
        return small(acc.at[i, pl.ds(0, n)], got.at[i, pl.ds(0, n)], base + i, dev)

    def sum_finish(acc, got, i, base, sign, rows=None):
        sum_step(acc, got, i, base, sign, rows).wait_recv()
        n = acc.shape[1] if rows is None else rows
        acc[i + 1, 0:n] = acc[i, 0:n] + got[i, 0:n]

    S_SID = 0
    S_M1 = 1
    S_M2 = S_M1 + NB + 1
    S_SM = S_M2 + T - 1
    S_M3 = S_SM + T - 1
    S_M4 = S_M3 + NC - 1
    S_B1 = S_M4 + 1
    S_B2 = S_B1 + NC - 1
    S_B3 = S_B2 + T - 1
    S_PZ = S_B3 + NB + 1
    S_PB = S_PZ + T - 1
    S_PC = S_PB + NB

    sid_copy = small(m.sid, m.sidr, S_SID, partner)
    sid_copy.start()
    if dm.inside:
        m.macc[0] = m.m1[...]
        sum_step(m.macc, m.mrec, 0, S_M1, 1).start()
    for pc in (0, 1, 2, 4, 6):
        core_copy(pc).start()
        core_local(pc).start()
    gather_to(-1.0)
    transpose_own()
    for pc in (3, 5, 7):
        core_copy(pc).start()
        core_local(pc).start()
    for z, slot in ((0, 0), (T - 1, T - 2)):
        @pl.when(me_z == z)
        def _():
            m.zb[slot] = jnp.zeros(m.zb.shape[1:], B16)

    sums[...] = jnp.zeros_like(sums)
    hsum[...] = jnp.zeros_like(hsum)
    fsum[...] = jnp.zeros_like(fsum)

    if dm.inside:
        for i in range(NB + 1):
            sum_finish(m.macc, m.mrec, i, S_M1, 1)
            if i < NB:
                sum_step(m.macc, m.mrec, i + 1, S_M1, 1).start()
        m.sm[me_z] = m.macc[NB + 1, 8:16, :]
        for off in range(1, T):
            small(m.sm.at[me_z], m.sm.at[me_z], S_SM + off - 1, z_dev(off)).start()
        m.cond[...] = m.macc[NB + 1, 0:8, :]
        width = D // T
        for zz in range(T):
            c = m.cond[:, zz * width : (zz + 1) * width]
            low = (c / (1.0 + jnp.exp(-c))).astype(B16)
            rows = [dot(low, m.wada[j]) for j in range(6)] + [jnp.zeros((8, 2 * R), F32)]
            m.m2s[zz] = jnp.concatenate(rows, axis=-1)
        for off in range(1, T):
            small(m.m2s.at[lax.rem(me_z + off, T)], m.m2r.at[off - 1], S_M2 + off - 1, z_dev(off)).start()

    gather_to(1.85)
    tok_start(0, m.xb, xs)

    if dm.inside:
        for off in range(1, T):
            small(m.m2s.at[0], m.m2r.at[off - 1], S_M2 + off - 1, z_dev(off)).wait_recv()
        m.m3c[core, chip] = m.m2s[me_z] + sum(m.m2r[k] for k in range(T - 1)) + m.badd[...]
        own = m.m3c.at[core, chip]
        for k in range(1, NC):
            small(own, own, S_M3 + k - 1, chip_dev(k)).start()
        gather_to(2.15)
        for off in range(1, T):
            got = m.sm.at[lax.rem(me_z - off + T, T)]
            small(got, got, S_SM + off - 1, z_dev(off)).wait_recv()
        head_cols = pl.ds(pl.multiple_of(core * hq, hq), hq)
        for z in range(T):
            for r in range(3):
                hp[z, r : r + 1, :] = m.sm[z, r + 1 : r + 2, head_cols]
            hp[z, 3:4, :] = 1.0 / hp[z, 2:3, :]
            hb[z, 0:1, :] = m.sm[z, 0:1, pl.ds(pl.multiple_of(core * fu, fu), fu)]
        for k in range(1, NC):
            got = m.m3c.at[core, lax.rem(chip - k + NC, NC)]
            small(got, got, S_M3 + k - 1, chip_dev(k)).wait_recv()
        small(m.m3c.at[core], m.m3c.at[core], S_M4, partner).start()

    got = small(m.sidr, m.sidr, S_SID, partner)
    got.wait_recv()
    pick = lax.rem(me_z, 2)
    ids = jnp.where(owner, m.sid[pl.ds(pick, 1), :], m.sidr[pl.ds(pick, 1), :])
    lanes = lax.broadcasted_iota(jnp.int32, (128, 1), 0).astype(F32)
    m.psi[...] = jnp.where(lanes > ids, FAR, 0.0).astype(B16).T
    m.phi[...] = jnp.where(lanes == ids, -1.0, 0.0).astype(B16).T

    if dm.inside:
        got = m.m3c.at[1 - core]
        small(got, got, S_M4, partner).wait_recv()
        for c in range(2):
            for p in range(NC):
                row = m.m3c[c, p, pl.ds(chip, 1), :]
                d = 2 * p + c
                for j in range(8):
                    mods[j : j + 1, d * R : (d + 1) * R] = row[:, j * R : (j + 1) * R]

    gather_to(4.1)
    tok_wait(0, m.xb, xs)

    def ln(rows):
        centred = rows - jnp.mean(rows, axis=-1, keepdims=True)
        inv = lax.rsqrt(jnp.mean(centred * centred, axis=-1, keepdims=True) + EPS)
        return centred * inv, inv

    def first_norm(t, carry):
        normed, _ = ln(xs[t].astype(F32))
        h1[t] = (normed * (1.0 + mod(2)) + mod(4)).astype(B16)
        return carry

    lax.fori_loop(0, T, first_norm, 0)
    gather_to(4.96)
    if dm.inside:
        for i in range(NB + 1):
            sum_step(m.macc, m.mrec, i, S_M1, 1).wait_send()
    gather_until(2)

    lane = lax.broadcasted_iota(jnp.int32, (1, hq), 1)
    halves = [(lane // dm.hd) == k for k in range(hq // dm.hd)]
    bi = lax.broadcasted_iota(jnp.int32, (hq, hq), 0) // dm.hd
    bj = lax.broadcasted_iota(jnp.int32, (hq, hq), 1) // dm.hd
    same_head = (bi == bj).astype(B16)

    def qkv(z, carry):
        t = dot(whole(h1), wz(z, 0, 3 * hq))
        q = t[:, :hq] + hp[z, 0:1, :]
        k = t[:, hq : 2 * hq]
        v = t[:, 2 * hq :] + hp[z, 1:2, :]
        qi = lax.rsqrt(split_dot(q * q, same_head) + EPS)
        ki = lax.rsqrt(split_dot(k * k, same_head) + EPS)
        m.qs[z] = (q * qi * hp[z, 2:3, :]).astype(B16)
        m.ks[z] = (k * ki).astype(B16)
        m.vs[z] = v.astype(B16)
        m.rq[z] = qi.astype(B16)
        m.rk[z] = ki.astype(B16)
        return carry

    lax.fori_loop(0, T, qkv, 0)
    zero16 = jnp.zeros((), B16)

    def expo(z, k, q_all, k_all):
        q_one = jnp.where(halves[k], q_all, zero16)
        left = jnp.concatenate([q_one, m.psi[...]], axis=1)
        right = jnp.concatenate([k_all, m.phi[...]], axis=1)
        return q_one, jnp.exp(dot_nt(left, right)).astype(B16)

    def attend(z, carry):
        q_all, k_all, v_all = m.qs[z], m.ks[z], m.vs[z]
        v_ones = jnp.concatenate([v_all, jnp.ones((M, hq), B16)], axis=1)
        mixed = inverse = None
        for k in range(hq // dm.hd):
            _, e = expo(z, k, q_all, k_all)
            both_ = dot(e, v_ones)
            inv = 1.0 / both_[:, hq:]
            one = both_[:, :hq] * inv
            mixed = one if mixed is None else jnp.where(halves[k], one, mixed)
            inverse = inv if inverse is None else jnp.where(halves[k], inv, inverse)
        m.o[z] = mixed.astype(B16)
        m.ol[z] = (mixed - mixed.astype(B16).astype(F32)).astype(B16)
        m.do[z] = inverse.astype(B16)
        return carry

    gather_to(5.0)
    for z in range(T):
        lax.fori_loop(z, z + 1, attend, 0)
        if z == 1:
            gather_to(5.9)
            tok_start(1, m.dyb, dys)

    gather_until(3)
    o_all = all_z(m.o)
    for n in range(NCH):
        exchange(0, n, dot_nt(o_all, wrows_all(n, 3 * hq, hq)))
    exchange_wait(0)

    def second_norm(t, carry):
        a = both(0, t) + mod(6)
        m.ab[t] = a.astype(B16)
        normed, inv = ln(xs[t].astype(F32) + mod(0) * a)
        h2[t] = (normed * (1.0 + mod(3)) + mod(5)).astype(B16)
        m.n2[t] = normed.astype(B16)
        m.r2[t] = jnp.broadcast_to(inv, (Q, 128))
        return carry

    lax.fori_loop(0, T, second_norm, 0)
    gather_to(7.05)
    exchange_sent(0)
    transpose_into(m.xt, h2)

    def out_grad(t, carry):
        d = (mod(1) * dys[t].astype(F32)).astype(B16)
        m.df[t] = d
        sums[7:8, :] += row_sum(d.astype(F32))
        return carry

    root = 0.7978845608028654

    def hidden(k):
        lo_u, lo_d = dm.up + k * half, dm.down + k * half

        def up(z, carry):
            u = dot(whole(h2), wz(z, lo_u, half)) + hb[z, 0:1, k * half : (k + 1) * half]
            uu = u * u
            th = jnp.tanh(root * u * (1.0 + 0.044715 * uu))
            m.gk[z] = (0.5 * u * (1.0 + th)).astype(B16)
            m.duk[z] = (0.5 * (1.0 + th) + (0.5 * root) * u * (1.0 - th * th) * (1.0 + 0.134145 * uu)).astype(B16)
            return carry

        def down(z, carry):
            dg = dot(whole(m.df), wz(z, lo_d, half))
            du = (dg * m.duk[z].astype(F32)).astype(B16)
            m.duk[z] = du
            fsum[z, 0:1, k * half : (k + 1) * half] = row_sum(du.astype(F32))
            return carry

        gather_until(4 + 2 * k)
        lax.fori_loop(0, T, up, 0)
        if k == 0:
            gather_to(7.15)
            tok_wait(1, m.dyb, dys)
            lax.fori_loop(0, T, out_grad, 0)
            transpose_into(m.xt2, m.df)
        gather_until(5 + 2 * k)
        lax.fori_loop(0, T, down, 0)

    def grads(k, begin):
        lo_u, lo_d = dm.up + k * half, dm.down + k * half

        def down_grad(z, carry):
            wstore(z, lo_d, half, dot(m.xt2[...], m.gk[z]))
            return carry

        def up_grad(z, carry):
            wstore(z, lo_u, half, dot(m.xt[...], m.duk[z]))
            return carry

        for pc, body in ((5 + 2 * k, down_grad), (4 + 2 * k, up_grad)):
            for h in range(2):
                lax.fori_loop(h * TH, (h + 1) * TH, body, 0)
                if pc in begin:
                    rs_begin(pc, h)

    for pc in range(NP):
        core_copy(pc).wait_send()
    hidden(0)
    du_all, g_all = all_z(m.duk), all_z(m.gk)
    for n in range(NCH):
        m.dacc[n] = dot_nt(du_all, wrows_all(n, dm.up, half))
        m.facc[n] = dot_nt(g_all, wrows_all(n, dm.down, half))
    gather_sent((4, 5))
    gather_to(99.0)
    grads(0, (5, 4))
    hidden(1)
    du_all, g_all = all_z(m.duk), all_z(m.gk)
    for n in range(NCH):
        exchange(1, n, m.dacc[n] + dot_nt(du_all, wrows_all(n, dm.up + half, half)))
    for n in range(NCH):
        m.facc[n] = m.facc[n] + dot_nt(g_all, wrows_all(n, dm.down + half, half))
    gather_sent((0, 1, 2, 3, 6, 7))
    grads(1, (7,))
    stop()
    transpose_into(m.xt, h1)
    tok_sent(1, m.dyb, dys)
    exchange_wait(1)
    if sender(2) is not m.send:
        for n in range(NCH):
            exchange(2, n, m.facc[n])

    def ln_back(e, normed, inv):
        return (e - jnp.mean(e, axis=-1, keepdims=True) - normed * jnp.mean(e * normed, axis=-1, keepdims=True)) * inv

    def mid_back(t, carry):
        dh = both(1, t)
        normed = m.n2[t].astype(F32)
        sums[3:4, :] += row_sum(dh * normed)
        sums[5:6, :] += row_sum(dh)
        step_back = ln_back(dh * (1.0 + mod(3)), normed, m.r2[t, :, 0:1])
        h2[t] = step_back.astype(B16)
        dx1 = dys[t].astype(F32) + step_back
        sums[0:1, :] += row_sum(dx1 * m.ab[t].astype(F32))
        da = (mod(0) * dx1).astype(B16)
        m.df[t] = da
        sums[6:7, :] += row_sum(da.astype(F32))
        return carry

    lax.fori_loop(0, T, mid_back, 0)
    pl.semaphore_signal(m.took, inc=1, device_id=partner, device_id_type=MESH)
    stop()
    for h in range(2):
        rs_begin(6, h)
    exchange_sent(1)
    if sender(2) is m.send:
        for n in range(NCH):
            exchange(2, n, m.facc[n])

    def last(t, carry):
        f = both(2, t) + mod(7)
        m.n2[t] = (mod(0) * m.ab[t].astype(F32) + mod(1) * f).astype(B16)
        sums[1:2, :] += row_sum(dys[t].astype(F32) * f)
        return carry

    exchange_wait(2)
    lax.fori_loop(0, T, last, 0)
    exchange_sent(2)
    back_start(0, m.outd)

    w_proj = jnp.concatenate([wz(z, 3 * hq, hq) for z in range(T)], axis=-1)
    do_all = dot(whole(m.df), w_proj).astype(B16)
    for z in range(T):
        m.do[z] = (do_all[:, z * hq : (z + 1) * hq].astype(F32) * m.do[z].astype(F32)).astype(B16)
    transpose_into(m.xt2, m.df)
    dw = dot(m.xt2[...], all_z(m.o))
    for z in range(T):
        wstore(z, 3 * hq, hq, dw[:, z * hq : (z + 1) * hq])
    for h in range(2):
        rs_begin(3, h)
    stop()

    ends = jnp.where(lane < 2, -1.0, 0.0).astype(B16)

    def attend_back(z, carry):
        q_all, k_all, v_all = m.qs[z], m.ks[z], m.vs[z]
        dob = m.do[z]
        prod = dob.astype(F32) * (m.o[z].astype(F32) + m.ol[z].astype(F32))
        v_ends = jnp.concatenate([v_all, jnp.broadcast_to(ends, (M, hq))], axis=1)
        dq = dk = dv = 0.0
        for k in range(hq // dm.hd):
            q_one, e = expo(z, k, q_all, k_all)
            to_all = (bi == k).astype(B16)
            total = split_dot(prod, to_all)
            high = total.astype(B16)
            low = (total - high.astype(F32)).astype(B16)
            extra = jnp.where(lane == 0, high, jnp.where(lane == 1, low, zero16))
            d_one = jnp.where(halves[k], dob, zero16)
            dp = dot_nt(jnp.concatenate([d_one, extra], axis=1), v_ends)
            ds = (e.astype(F32) * dp).astype(B16)
            dq = dq + dot(ds, jnp.where(halves[k], k_all, zero16))
            dk = dk + dot_tn(ds, q_one)
            dv = dv + dot_tn(e, d_one)
        gain = hp[z, 2:3, :]
        q_hat = q_all.astype(F32) * hp[z, 3:4, :]
        k_hat = k_all.astype(F32)
        hsum[z, 2:3, :] = row_sum(dq * q_hat)
        eq = dq * gain
        dq = ((eq - q_hat * split_dot(eq * q_hat, same_head)) * m.rq[z].astype(F32)).astype(B16)
        dk = ((dk - k_hat * split_dot(dk * k_hat, same_head)) * m.rk[z].astype(F32)).astype(B16)
        dv = dv.astype(B16)
        hsum[z, 0:1, :] = row_sum(dq.astype(F32))
        hsum[z, 1:2, :] = row_sum(dv.astype(F32))
        m.dqkv[...] = jnp.concatenate([dq, dk, dv], axis=1)
        return carry

    for z in range(T):
        lax.fori_loop(z, z + 1, attend_back, 0)
        if z == T - 1:
            pl.semaphore_wait(m.took, 1)
        d_one_z = m.dqkv[...]
        for n in range(NCH):
            part = dot_nt(d_one_z, wrows(z, n, 0, 3 * hq))
            if z == T - 1:
                exchange(3, n, m.facc[n] + part)
            else:
                m.facc[n] = part if z == 0 else m.facc[n] + part
        wstore(z, 0, 3 * hq, dot(m.xt[...], d_one_z))
        for pc, h in BEGIN[z]:
            rs_begin(pc, h)
        stop()

    if dm.inside:
        for z in range(T):
            m.pks[z] = jnp.concatenate([hsum[z], fsum[z], sums[...]], axis=-1)
        for off in range(1, T):
            small(m.pks.at[lax.rem(me_z + off, T)], m.pkr.at[off - 1], S_PZ + off - 1, z_dev(off)).start()
    exchange_wait(3)

    def first_back(t, carry):
        dh = both(3, t)
        normed, inv = ln(xs[t].astype(F32))
        sums[2:3, :] += row_sum(dh * normed)
        sums[4:5, :] += row_sum(dh)
        m.ab[t] = (h2[t].astype(F32) + ln_back(dh * (1.0 + mod(2)), normed, inv)).astype(B16)
        return carry

    for t in range(T):
        lax.fori_loop(t, t + 1, first_back, 0)
        if t % 2:
            stop()
    exchange_sent(3)
    if not dm.inside:
        back_start(1, m.gind)

    if dm.inside:
        for p in range(NC):
            d = pl.multiple_of((2 * p + core) * R, R)
            rows = [sums[j : j + 1, pl.ds(d, R)] for j in range(8)]
            m.b1s[p] = jnp.broadcast_to(jnp.concatenate(rows, axis=-1), (8, 8 * R))
        for k in range(1, NC):
            small(m.b1s.at[lax.rem(chip + k, NC)], m.b1r.at[k - 1], S_B1 + k - 1, chip_dev(k)).start()
        stop()
        stop()
        for k in range(1, NC):
            small(m.b1s.at[0], m.b1r.at[k - 1], S_B1 + k - 1, chip_dev(k)).wait_recv()
        row8 = lax.broadcasted_iota(jnp.int32, (8, 1), 0)
        packed = jnp.where(row8 == chip, m.b1s[chip], 0.0)
        for k in range(1, NC):
            packed = jnp.where(row8 == lax.rem(chip - k + NC, NC), m.b1r[k - 1], packed)
        m.dmodf[me_z] = packed
        for off in range(1, T):
            small(m.dmodf.at[me_z], m.dmodf.at[me_z], S_B2 + off - 1, z_dev(off)).start()
        back_start(1, m.gind)
        stop()
        for off in range(1, T):
            small(m.pks.at[0], m.pkr.at[off - 1], S_PZ + off - 1, z_dev(off)).wait_recv()
        m.pka[0] = m.pks[me_z] + sum(m.pkr[k] for k in range(T - 1))
        if NB:
            sum_step(m.pka, m.pkb, 0, S_PB, 0).start()
        for off in range(1, T):
            got = m.dmodf.at[lax.rem(me_z - off + T, T)]
            small(got, got, S_B2 + off - 1, z_dev(off)).wait_recv()
        width = D // T
        for zz in range(T):
            acc = 0.0
            for j in range(6):
                acc = acc + dot_nt(m.dmodf[zz, :, j * R : (j + 1) * R].astype(B16), m.wada[j])
            m.macc[0, 0:8, zz * width : (zz + 1) * width] = acc
        sum_step(m.macc, m.mrec, 0, S_B3, 1, 8).start()
        for i in range(NB + 1):
            if i < NB:
                sum_finish(m.pka, m.pkb, i, S_PB, 0)
                if i + 1 < NB:
                    sum_step(m.pka, m.pkb, i + 1, S_PB, 0).start()
            if i == NB:
                m.pk[core] = m.pka[NB]
                small(m.pka.at[NB], m.pk.at[core], S_PC, partner).start()
            sum_finish(m.macc, m.mrec, i, S_B3, 1, 8)
            if i < NB:
                sum_step(m.macc, m.mrec, i + 1, S_B3, 1, 8).start()
            stop()
        m.dsil[...] = m.macc[NB + 1, 0:8]
    pump(len(events))
    assert not events
    rs_end()
    tok_sent(0, m.xb, xs)
    back_wait(0, m.outd)
    back_wait(1, m.gind)
    sid_copy.wait_send()
    if dm.inside:
        for i in range(NB + 1):
            sum_step(m.macc, m.mrec, i, S_B3, 1, 8).wait_send()
        for i in range(NB):
            sum_step(m.pka, m.pkb, i, S_PB, 0).wait_send()
        for off in range(1, T):
            zt = lax.rem(me_z + off, T)
            small(m.sm.at[me_z], m.sm.at[me_z], S_SM + off - 1, z_dev(off)).wait_send()
            small(m.m2s.at[zt], m.m2r.at[off - 1], S_M2 + off - 1, z_dev(off)).wait_send()
            small(m.pks.at[zt], m.pkr.at[off - 1], S_PZ + off - 1, z_dev(off)).wait_send()
            small(m.dmodf.at[me_z], m.dmodf.at[me_z], S_B2 + off - 1, z_dev(off)).wait_send()
        for k in range(1, NC):
            small(m.m3c.at[core, chip], m.m3c.at[core, chip], S_M3 + k - 1, chip_dev(k)).wait_send()
            small(m.b1s.at[lax.rem(chip + k, NC)], m.b1r.at[k - 1], S_B1 + k - 1, chip_dev(k)).wait_send()
        small(m.m3c.at[core], m.m3c.at[core], S_M4, partner).wait_send()
        small(m.pka.at[NB], m.pk.at[core], S_PC, partner).wait_send()
        got = m.pk.at[1 - core]
        small(got, got, S_PC, partner).wait_recv()


def block_call(dm, weights, xb, dyb, sid, extra):
    T, NC, NB, Q, M, D, R, C, W = dm.T, dm.NC, dm.bits, dm.Q, dm.M, dm.D, dm.R, dm.C, dm.W
    hq, fu, NCH, half = dm.hq, dm.fu, dm.NCH, dm.half
    TH, NP = T // 2, len(dm.pieces)
    two = (2,) * NB
    v = pltpu.VMEM
    dma = pltpu.SemaphoreType.DMA
    any_, vm = pl.BlockSpec(memory_space=pl.ANY), pl.BlockSpec(memory_space=pltpu.VMEM)
    s = jax.ShapeDtypeStruct
    tok, heads, acc = (T, Q, D), (T, M, hq), (NCH, M, CHUNK)
    ins = {**weights, "xb": xb, "dyb": dyb, "sid": sid, **extra}
    outs = {"g_qkv": s((3, R, 2 * hq), F32), "g_proj": s((2 * hq, R), F32), "g_up": s((R, 2 * fu), F32), "g_down": s((2 * fu, R), F32), "outd": s((2, Q, D), B16), "gind": s((2, Q, D), B16)}
    totals = {"sums": (8, D), "hsum": (T, 8, hq), "fsum": (T, 8, fu)}
    scratch = {"wall": v((T,) + two + (2 * R, C), B16)}
    for name in "xs dys h1 h2 ab n2 df".split():
        scratch[name] = v(tok, B16)
    for name in "qs ks vs rq rk o ol do".split():
        scratch[name] = v(heads, B16)
    scratch.update(
        r2=v((T, Q, 128), F32), psi=v((M, 128), B16), phi=v((M, 128), B16), sidr=v((8, M), F32),
        gk=v((T, M, half), B16), duk=v((T, M, half), B16), facc=v(acc, F32), dacc=v(acc, F32),
        send=v((NCH, M, CHUNK), B16), recv=v((2, NCH, M, CHUNK), B16),
        xt=v((D, M), B16), xt2=v((D, M), B16), dqkv=v((M, 3 * hq), B16),
        zb=v((T - 1, 2 * R, C), B16), zx=v((2 * R, C), B16), fbuf=v((FINS, R, half), F32), fturn=v((2, half, R), F32),
    )
    for k in range(NB):
        scratch[f"rb{k}"] = v((SLOTS, 2, TH) + (2,) * (NB - 1 - k) + (2 * R, half), B16)
    if dm.inside:
        outs.update(dmodf=s((T, 8, 8 * R), F32), cond=s((8, D), F32), dsil=s((8, D), F32), pk=s((2, 8, W), F32))
        scratch.update({name: v(shape, F32) for name, shape in totals.items()})
        scratch.update(
            mods=v((8, D), F32), hp=v((T, 8, hq), F32), hb=v((T, 8, fu), F32),
            macc=v((NB + 2, 16, D), F32), mrec=v((NB + 1, 16, D), F32), sm=v((T, 8, D), F32),
            m2s=v((T, 8, 8 * R), F32), m2r=v((T - 1, 8, 8 * R), F32), m3c=v((2, NC, 8, 8 * R), F32),
            b1s=v((NC, 8, 8 * R), F32), b1r=v((NC, 8, 8 * R), F32),
            pks=v((T, 8, W), F32), pkr=v((T - 1, 8, W), F32), pka=v((NB + 1, 8, W), F32), pkb=v((max(NB, 1), 8, W), F32),
        )
    else:
        outs.update({name: s(shape, F32) for name, shape in totals.items()})
    small = 4 * NB + 6 * T + 2 * NC + 8
    reg = pltpu.SemaphoreType.REGULAR
    scratch.update(
        c_s=dma((NP,)), c_r=dma((NP,)), c_l=dma((NP,)), z_s=dma((NP, T - 1)), z_r=dma((NP, T - 1)),
        p_s=dma((NP, NB, 2)), p_r=dma((NP, NB, 2)), x_s=dma((2, 2)), x_r=dma((2, T)), x_l=dma((2,)), x_f=dma((2, 2)),
        e_s=dma((4, NCH)), e_r=dma((4, NCH)), rs_s=dma((NP, NB, 2)), rs_r=dma((NP, NB, 2)), free=reg((NB, 2)), took=reg,
        rz_s=dma((NP, T - 1)), rz_r=dma((NP, T - 1)), f_s=dma((NP,)), f_r=dma((NP,)), z_f=dma((NP,)), rx=dma((NP, 2)),
        o_s=dma((2, T)), o_r=dma((2, 2)), o_l=dma((2,)), s_s=dma((small,)), s_r=dma((small,)),
    )
    names = tuple(ins) + tuple(outs) + tuple(scratch)
    got = pl.pallas_call(
        functools.partial(block_kernel, dm, names),
        out_shape=tuple(outs.values()),
        in_specs=[any_ if name in ("wqkv", "wup", "xb", "dyb") else vm for name in ins],
        out_specs=tuple(any_ if name in ("outd", "gind") else vm for name in outs),
        scratch_shapes=list(scratch.values()),
        compiler_params=pltpu.CompilerParams(
            collective_id=0, has_side_effects=True, vmem_limit_bytes=66 * 1024 * 1024
        ),
        cost_estimate=pl.CostEstimate(flops=30 * 10**9, bytes_accessed=10**7, transcendentals=10**7),
    )(*ins.values())
    return dict(zip(outs, got))


def local(
    dp, tensor,
    block_input, cotangent, class_ids, scale_ids, class_table, w_ada, b_ada, query_key_value_weight,
    qv_bias, q_gain, output_projection, up_weight, hidden_bias, down_weight, projection_bias,
):
    seqs, quarter, width = block_input.shape
    length = scale_ids.shape[1]
    assert seqs == 2 and tensor == 4
    rows = -(-quarter // 16) * 16
    head = q_gain.shape[1] * dp
    hidden = up_weight.shape[1] * tensor
    dm = Dims(dp, tensor, rows, width, head, hidden)
    T, R, hq, fu, NC, M = dm.T, dm.R, dm.hq, dm.fu, dm.NC, dm.M
    total = class_ids.shape[0]
    di, zi = lax.axis_index("dp"), lax.axis_index("tensor")
    core = di % 2

    pad_rows = ((0, 0), (0, 0), (0, rows - quarter))
    sid = jnp.pad(scale_ids.astype(F32).reshape(2, T, quarter), pad_rows, constant_values=127.0).reshape(2, M)
    sid = jnp.pad(sid, ((0, 6), (0, 0)))
    my_rows = class_table.shape[0]
    my_ids = di * my_rows + jnp.arange(my_rows, dtype=jnp.int32)

    if dm.inside:
        place = jnp.arange(dp, dtype=jnp.int32) == di

        def spread(w):
            return jnp.where(place[:, None], w[..., None, :], 0).reshape(w.shape[:-2] + (-1,)).astype(F32)

        def pad_lanes(w):
            return jnp.pad(w, ((0, 0), (0, width - w.shape[1])))

        hot = (class_ids[:, None] == my_ids[None, :]).astype(B16)
        cond = jnp.dot(hot, class_table, preferred_element_type=F32).reshape(NC, -1)
        tiny = [spread(hidden_bias)[None], spread(qv_bias), spread(q_gain)[None]]
        tiny = jnp.concatenate([pad_lanes(w) for w in tiny], axis=0)
        m1 = jnp.concatenate([jnp.pad(cond, ((0, 8 - NC), (0, 0))), jnp.pad(tiny, ((0, 4), (0, 0)))], axis=0)
        badd = jnp.concatenate([b_ada, projection_bias], axis=0).astype(F32).reshape(1, -1)
        extra = {"m1": m1, "wada": jnp.moveaxis(w_ada, 1, 0), "badd": badd}
    else:
        hot = (class_ids[:, None] == my_ids[None, :]).astype(B16)
        cond = lax.psum(jnp.dot(hot, class_table, preferred_element_type=F32), "dp")
        silu, silu_back = jax.vjp(jax.nn.silu, cond)
        silu_low = silu.astype(B16)
        parts = jnp.einsum("sc,cjd->sjd", silu_low, w_ada, preferred_element_type=F32)
        parts = parts.reshape((NC, T) + parts.shape[1:])
        mine = lax.psum_scatter(parts, "tensor", scatter_dimension=1, tiled=True)[:, 0] + b_ada.astype(F32)
        spread = lax.all_to_all(jnp.repeat(mine, 2, axis=0), "dp", 0, 0, tiled=True)
        modulation = jnp.moveaxis(spread, 0, 1).reshape(6, width)

        pieces = [qv_bias, q_gain, hidden_bias, projection_bias]
        flat = jnp.concatenate([p.reshape(-1) for p in pieces])
        everyone = lax.all_gather(lax.all_gather(flat, "tensor"), "dp")
        cut, at = [], 0
        for p in pieces:
            cut.append(everyone[:, :, at : at + p.size].reshape((dp, T) + p.shape).astype(F32))
            at += p.size
        qv_all = cut[0].transpose(2, 1, 3, 0, 4).reshape(2, T, 2, hq)[:, :, core]
        gain_all = cut[1].transpose(1, 2, 0, 3).reshape(T, 2, hq)[:, core]
        hidden_all = cut[2].transpose(1, 2, 0, 3).reshape(T, 2, fu)[:, core]
        out_bias = cut[3][:, 0].transpose(1, 0, 2).reshape(2, width)
        mods = jnp.concatenate([modulation, out_bias], axis=0)
        hp = jnp.stack([qv_all[0], qv_all[1], gain_all, 1.0 / gain_all], axis=1)
        hp = jnp.concatenate([hp, jnp.zeros_like(hp)], axis=1)
        hb = jnp.broadcast_to(hidden_all[:, None], (T, 8, fu))

        extra = {"mods": mods, "hp": hp, "hb": hb}

    weights = {"wqkv": query_key_value_weight, "wup": up_weight, "wproj": output_projection, "wdown": down_weight}
    pad = ((0, 0), (0, rows - quarter), (0, 0))
    xb = jnp.pad(block_input.astype(B16), pad)
    dyb = jnp.pad(cotangent.astype(B16), pad)

    got = block_call(dm, weights, xb, dyb, sid, extra)
    outd, gind = got["outd"], got["gind"]

    block_output = block_input + outd[:, :quarter].astype(F32)
    input_grad = cotangent + gind[:, :quarter].astype(F32)

    w_qkv_grad, w_proj_grad, w_fc1_grad, w_fc2_grad = (got[name] for name in ("g_qkv", "g_proj", "g_up", "g_down"))

    if dm.inside:
        cond = got["cond"][:NC].reshape(total, -1)
        silu, silu_back = jax.vjp(jax.nn.silu, cond)
        dmod = jnp.swapaxes(got["dmodf"][:, :NC], 0, 1).reshape(total, 8, R)[:, :6].astype(B16)
        b_ada_grad = jnp.sum(dmod.astype(F32), axis=0)
        w_ada_grad = jnp.einsum("sc,sjd->cjd", silu.astype(B16), dmod, preferred_element_type=F32)
        (d_cond,) = silu_back(got["dsil"][:NC].reshape(total, -1))
        pk = got["pk"]

        def own(w, n):
            return lax.dynamic_slice_in_dim(w, di * n, n, w.ndim - 1)

        heads = own(jnp.swapaxes(pk[:, :3, :hq], 0, 1).reshape(3, -1, head), head // dp)
        qv_bias_grad, q_gain_grad = heads[:2], heads[2]
        b_fc1_grad = own(pk[:, 0, hq : hq + fu].reshape(hidden_bias.shape[0], -1), hidden_bias.shape[1])
        b_out_grad = own(pk[0, 6:8, hq + fu :], R)
    else:
        sums, hsum, fsum = got["sums"], got["hsum"], got["fsum"]
        dmod = sums[:6].reshape(6, dp, R).astype(B16)
        dmod = lax.all_to_all(jnp.moveaxis(dmod, 1, 0), "dp", 0, 0, tiled=True)
        dmod = lax.all_gather(dmod[::2], "tensor", axis=1)
        dmod = dmod.reshape((total, 6, R))
        b_ada_grad = jnp.sum(dmod.astype(F32), axis=0)
        w_ada_grad = jnp.einsum("sc,sjd->cjd", silu_low, dmod, preferred_element_type=F32)
        d_silu = lax.psum(jnp.einsum("sjd,cjd->sc", dmod, w_ada, preferred_element_type=F32), "dp")
        (d_cond,) = silu_back(d_silu)

        vec = jnp.concatenate([hsum[:, :3].reshape(-1), fsum[:, 0].reshape(-1), sums[6:].reshape(-1) * 0.5])
        nh, nf = T * 3 * hq, T * fu
        place_ = jnp.arange(2, dtype=jnp.int32) == core
        by_core = jnp.where(place_[:, None], vec[None, : nh + nf], 0.0).reshape(-1)
        vec = lax.psum(jnp.concatenate([by_core, vec[nh + nf :]]), ("dp", "tensor"))
        by_core = vec[: 2 * (nh + nf)].reshape(2, nh + nf)
        heads = by_core[:, :nh].reshape(2, T, 3, hq)
        heads = lax.dynamic_index_in_dim(heads, zi, 1, keepdims=False)
        heads = jnp.moveaxis(heads, 0, 1).reshape(3, -1, head)
        step = head // dp
        heads = lax.dynamic_slice_in_dim(heads, di * step, step, 2)
        qv_bias_grad, q_gain_grad = heads[:2], heads[2]
        fc1 = lax.dynamic_index_in_dim(by_core[:, nh:].reshape(2, T, fu), zi, 1, keepdims=False)
        fc1 = fc1.reshape(-1, hidden_bias.shape[1] * dp)
        step = hidden_bias.shape[1]
        b_fc1_grad = lax.dynamic_slice_in_dim(fc1, di * step, step, 1)
        b_out_grad = lax.dynamic_slice_in_dim(vec[2 * (nh + nf) :].reshape(2, width), di * R, R, 1)

    table_grad = jnp.dot(hot.astype(F32).T, d_cond, precision=lax.Precision.HIGHEST, preferred_element_type=F32)

    return (
        block_output, input_grad, table_grad, w_ada_grad, b_ada_grad, w_qkv_grad, qv_bias_grad, q_gain_grad,
        w_proj_grad, w_fc1_grad, b_fc1_grad, w_fc2_grad, b_out_grad,
    )


def solution(mesh):
    dp, tensor = mesh.shape["dp"], mesh.shape["tensor"]
    return jax.shard_map(
        functools.partial(local, dp, tensor),
        mesh=mesh,
        in_specs=(
            P("dp", "tensor", None),
            P("dp", "tensor", None),
            P(),
            P("dp", None),
            P("dp", "tensor"),
            P("tensor", None, "dp"),
            P(None, "dp"),
            P(None, "dp", "tensor"),
            P(None, "tensor", "dp"),
            P("tensor", "dp"),
            P("tensor", "dp"),
            P("dp", "tensor"),
            P("tensor", "dp"),
            P("tensor", "dp"),
            P(None, "dp"),
        ),
        out_specs=(
            P("dp", "tensor", None),
            P("dp", "tensor", None),
            P("dp", "tensor"),
            P("tensor", None, "dp"),
            P(None, "dp"),
            P(None, "dp", "tensor"),
            P(None, "tensor", "dp"),
            P("tensor", "dp"),
            P("tensor", "dp"),
            P("dp", "tensor"),
            P("tensor", "dp"),
            P("tensor", "dp"),
            P(None, "dp"),
        ),
        check_vma=False,
    )
```

```python
import functools

import jax
import jax.numpy as jnp
from jax import lax
from jax.experimental import pallas as pl
from jax.experimental.layout import Layout, with_layout_constraint
from jax.experimental.pallas import tpu as pltpu
from jax.sharding import PartitionSpec as P

MESH = pl.DeviceIdType.MESH
F32, B16 = jnp.float32, jnp.bfloat16
FINS = 3
SLOTS = 3
PUMPS = (1, 0, 0, 0, 1, 1, 4, 0, 3, 2, 4, 5, 2, 1)
BEGIN = ((), ((2, 0),), ((1, 0),), ((2, 1), (1, 1), (0, 0), (0, 1)))
LEAN = 2.0
CHUNK = 256
EPS = 1e-06
FAR = 256.0


def dot(a, b):
    return lax.dot_general(a, b, (((1,), (0,)), ((), ())), preferred_element_type=F32)


def dot_nt(a, b):
    return lax.dot_general(a, b, (((1,), (1,)), ((), ())), preferred_element_type=F32)


def dot_tn(a, b):
    return lax.dot_general(a, b, (((0,), (0,)), ((), ())), preferred_element_type=F32)


def split_dot(a, b):
    high = a.astype(B16)
    low = (a - high.astype(F32)).astype(B16)
    return dot(high, b) + dot(low, b)


def row_sum(a):
    return jnp.sum(a, axis=0, keepdims=True)


class Dims:
    def __init__(self, dp, tensor, rows, width, head, hidden):
        self.T = tensor
        self.NC = dp // 2
        self.bits = self.NC.bit_length() - 1
        self.Q = rows
        self.M = rows * tensor
        self.D = width
        self.hd = head
        self.hq = width // tensor // 2
        self.fu = hidden // tensor // 2
        self.R = width // dp
        self.C = 4 * self.hq + 2 * self.fu
        self.NCH = width // CHUNK
        self.inside = self.R % 128 == 0 and self.NC <= tensor and hidden // tensor <= width
        self.W = self.hq + self.fu + width
        hq, fu, half = self.hq, self.fu, self.fu // 2
        up, down = 4 * hq, 4 * hq + fu
        self.up, self.down, self.half = up, down, half
        self.pieces = ((0, hq), (hq, hq), (2 * hq, hq), (3 * hq, hq), (up, half), (down, half), (up + half, half), (down + half, half))
        self.sums_order = (5, 4, 7, 6, 3, 2, 1, 0)
        assert 1 << self.bits == self.NC


class Refs:
    pass


def block_kernel(dm, names, *refs):
    m = Refs()
    for name, ref in zip(names, refs):
        if name[:2] in ("rb", "rf"):
            setattr(m, name[:2], getattr(m, name[:2], []) + [ref])
        else:
            setattr(m, name, ref)
    T, NC, NB, Q, M, D, R, C = dm.T, dm.NC, dm.bits, dm.Q, dm.M, dm.D, dm.R, dm.C
    hq, fu, NCH, half = dm.hq, dm.fu, dm.NCH, dm.half
    TH = T // 2
    NP = len(dm.pieces)
    wall, xs, dys, h1, h2 = m.wall, m.xs, m.dys, m.h1, m.h2
    mods, hp, hb, sums, hsum, fsum = m.mods, m.hp, m.hb, m.sums, m.hsum, m.fsum
    dpi = lax.axis_index("dp")
    me_z = lax.axis_index("tensor")
    core = lax.rem(dpi, 2)
    chip = dpi // 2
    mybit = [lax.rem(chip // (1 << b), 2) for b in range(NB)]
    partner = (dpi + 1 - 2 * core, me_z)

    def tag_z(dev):
        return dev

    def z_dev(off):
        return (dpi, lax.rem(me_z + off, T))

    def bit_dev(b):
        return (dpi + (1 - 2 * mybit[b]) * (2 << b), me_z)

    def chip_dev(k):
        return (lax.rem(chip + k, NC) * 2 + core, me_z)

    bar = pltpu.get_barrier_semaphore()
    friends = [partner] + [z_dev(k) for k in range(1, T)]
    friends += [chip_dev(k) for k in range(1, NC)] if dm.inside else [bit_dev(b) for b in range(NB)]
    for dev in friends:
        pl.semaphore_signal(bar, inc=1, device_id=dev, device_id_type=MESH)
    pl.semaphore_wait(bar, len(friends))

    def rdma(src, dst, ss, rs, dev):
        return pltpu.make_async_remote_copy(
            src_ref=src, dst_ref=dst, send_sem=ss, recv_sem=rs, device_id=dev, device_id_type=MESH
        )

    every = slice(None)

    def place(fixed):
        return tuple(fixed.get(b, every) for b in reversed(range(NB)))

    mine = place({b: mybit[b] for b in range(NB)})

    def cols(pc):
        return pl.ds(*dm.pieces[pc])

    def core_rows(c):
        return pl.ds(pl.multiple_of(c * R, R), R)

    def lanes_of(start, n):
        return pl.ds(pl.multiple_of(start, 128), n)

    def own_weight(pc, c):
        if pc < 3:
            return m.wqkv.at[pc, :, lanes_of(c * hq, hq)]
        if pc == 3:
            return m.gk.at[0, 128 : 128 + R, lanes_of(c * hq, hq)]
        k = (pc - 4) // 2
        if pc % 2 == 0:
            return m.wup.at[:, lanes_of(c * fu + k * half, half)]
        return m.gk.at[2 * c + k, 0:R, :]

    def transpose_own():
        m.gk[0, 128 : 128 + R, :] = m.wproj[...].T
        for i in range(4):
            m.gk[i, 0:R, :] = m.wdown[i * half : (i + 1) * half, :].T

    def core_copy(pc):
        dst = wall.at[(me_z,) + mine + (core_rows(core), cols(pc))]
        return rdma(own_weight(pc, 1 - core), dst, m.c_s.at[pc], m.c_r.at[pc], partner)

    def core_local(pc):
        dst = wall.at[(me_z,) + mine + (core_rows(core), cols(pc))]
        return pltpu.make_async_copy(own_weight(pc, core), dst, m.c_l.at[pc])

    def z_copy(pc, off):
        part = wall.at[(me_z,) + mine + (every, cols(pc))]
        return rdma(part, part, m.z_s.at[pc, off - 1], m.z_r.at[pc, off - 1], z_dev(off))

    inner = jnp.logical_and(me_z > 0, me_z < T - 1)
    line_sends = ((2, me_z >= 0), (1, me_z < T - 1), (3, me_z > 0))

    def z_landed(pc, off):
        part = wall.at[(lax.rem(me_z - off + T, T),) + mine + (every, cols(pc))]
        rdma(part, part, m.z_s.at[pc, off - 1], m.z_r.at[pc, off - 1], z_dev(off)).wait_recv()

    def z_forward(pc):
        part = wall.at[(lax.rem(me_z + 2, T),) + mine + (every, cols(pc))]
        up = lax.rem(me_z + 1, 2)
        return rdma(part, part, m.z_f.at[pc], m.z_r.at[pc, 2 * up], tag_z((dpi, me_z + 2 * up - 1)))

    order = [list(range(NB)), list(reversed(range(NB)))]

    def half_z(h):
        return pl.ds(h * TH, TH)

    def p_copy(pc, step, h, landing):
        b = order[h][step]
        fixed = {k: mybit[k] for k in order[h][step:]}
        if landing:
            fixed[b] = 1 - mybit[b]
        part = wall.at[(half_z(h),) + place(fixed) + (every, cols(pc))]
        return rdma(part, part, m.p_s.at[pc, step, h], m.p_r.at[pc, step, h], bit_dev(b))

    def gather_stage(pc, s):
        if not 0 <= pc < NP:
            return
        if s == 0:
            core_local(pc).wait()
            other = wall.at[(me_z,) + mine + (core_rows(1 - core), cols(pc))]
            rdma(other, other, m.c_s.at[pc], m.c_r.at[pc], partner).wait_recv()
            for off, allowed in line_sends:
                @pl.when(allowed)
                def _():
                    z_copy(pc, off).start()
            return
        if s == -1:
            @pl.when(inner)
            def _():
                z_landed(pc, 2)
                z_forward(pc).start()
            return
        if s == 1:
            z_landed(pc, 1)
            z_landed(pc, 3)

            @pl.when(jnp.logical_not(inner))
            def _():
                z_landed(pc, 2)
        for h in range(2):
            if s > 1:
                p_copy(pc, s - 2, h, True).wait_recv()
            if s <= NB:
                p_copy(pc, s - 1, h, False).start()

    starts = [(pc - 2.2, pc, 0) for pc in range(NP)] + [(pc - 1.1, pc, -1) for pc in range(NP)]
    starts += [(pc + 1.1 * (s - 1), pc, s) for pc in range(NP) for s in range(1, NB + 1)]
    if NB == 2:
        starts[starts.index((4 + 1.1, 4, 2))] = (4.95, 4, 2)
    starts.sort()

    here = [0]

    def gather_to(key):
        while starts and starts[0][0] <= key:
            gather_stage(*starts.pop(0)[1:])

    def gather_until(pc):
        gather_to(pc + 1.1 * NB)
        while here[0] <= pc:
            gather_stage(here[0], NB + 1)
            here[0] += 1

    def gather_sent(which):
        for pc in which:
            for off, allowed in line_sends:
                @pl.when(allowed)
                def _():
                    z_copy(pc, off).wait_send()

            @pl.when(inner)
            def _():
                z_forward(pc).wait_send()

            for step in range(NB):
                for h in range(2):
                    p_copy(pc, step, h, False).wait_send()

    owner = me_z // 2 == core

    def tok_copy(which, src, dst, i):
        zt = 2 * core + i
        return rdma(src.at[i], dst.at[me_z], m.x_s.at[which, i], m.x_r.at[which, me_z], (dpi, zt))

    def tok_start(which, src, dst):
        for i in range(2):
            @pl.when(2 * core + i != me_z)
            def _():
                tok_copy(which, src, dst, i).start()

            @pl.when(2 * core + i == me_z)
            def _():
                pltpu.make_async_copy(src.at[i], dst.at[me_z], m.x_l.at[which]).start()

    def tok_forward(which, dst):
        return rdma(dst, dst, m.x_f.at[which, 0], m.x_f.at[which, 1], partner)

    def tok_wait(which, src, dst):
        @pl.when(owner)
        def _():
            for off in range(1, T):
                zq = lax.rem(me_z + off, T)
                rdma(dst.at[zq], dst.at[zq], m.x_s.at[which, 0], m.x_r.at[which, zq], (dpi, zq)).wait_recv()
            pltpu.make_async_copy(src.at[0], dst.at[me_z], m.x_l.at[which]).wait()
            tok_forward(which, dst).start()

        @pl.when(jnp.logical_not(owner))
        def _():
            tok_forward(which, dst).wait_recv()

    def tok_sent(which, src, dst):
        for i in range(2):
            @pl.when(2 * core + i != me_z)
            def _():
                tok_copy(which, src, dst, i).wait_send()

        @pl.when(owner)
        def _():
            tok_forward(which, dst).wait_send()

    back_from = (m.n2, m.ab)

    def back_copy(which, dst, zq):
        i = lax.rem(me_z, 2)
        return rdma(back_from[which].at[zq], dst.at[i], m.o_s.at[which, zq], m.o_r.at[which, i], (dpi, zq))

    def back_start(which, dst):
        @pl.when(owner)
        def _():
            for off in range(1, T):
                back_copy(which, dst, lax.rem(me_z + off, T)).start()
            pltpu.make_async_copy(back_from[which].at[me_z], dst.at[lax.rem(me_z, 2)], m.o_l.at[which]).start()

    def back_wait(which, dst):
        @pl.when(owner)
        def _():
            for off in range(1, T):
                back_copy(which, dst, lax.rem(me_z + off, T)).wait_send()
            pltpu.make_async_copy(back_from[which].at[me_z], dst.at[lax.rem(me_z, 2)], m.o_l.at[which]).wait()

        for i in range(2):
            @pl.when(2 * core + i != me_z)
            def _():
                rdma(dst.at[i], dst.at[i], m.o_s.at[which, 0], m.o_r.at[which, i], (dpi, 2 * core + i)).wait_recv()

    def sender(k):
        return m.duk if k == 2 and m.duk.shape == m.send.shape else m.send

    def x_copy(k, n):
        return rdma(sender(k).at[n], m.recv.at[k % 2, n], m.e_s.at[k, n], m.e_r.at[k, n], partner)

    def exchange(k, n, value):
        sender(k)[n] = value.astype(B16)
        x_copy(k, n).start()

    def exchange_wait(k):
        for n in range(NCH):
            x_copy(k, n).wait_recv()

    def exchange_sent(k):
        for n in range(NCH):
            x_copy(k, n).wait_send()

    def both(k, t):
        rows = pl.ds(pl.multiple_of(t * Q, 16), Q)
        parts = [sender(k)[n, rows, :].astype(F32) + m.recv[k % 2, n, rows, :].astype(F32) for n in range(NCH)]
        return jnp.concatenate(parts, axis=-1)

    def wz(z, lo, n):
        return wall[(z,) + (every,) * NB + (every, pl.ds(lo, n))].reshape(D, n)

    def wrows(z, n, lo, width):
        per = CHUNK // (2 * R)
        low = per.bit_length() - 1
        top = n * per
        fixed = {b: (top >> b) & 1 for b in range(low, NB)}
        return wall[(z,) + place(fixed) + (every, pl.ds(lo, width))].reshape(CHUNK, width)

    def wrows_all(n, lo, width):
        return jnp.concatenate([wrows(z, n, lo, width) for z in range(T)], axis=-1)

    def wstore(z, lo, n, value):
        wall[(z,) + (every,) * NB + (every, pl.ds(lo, n))] = value.astype(B16).reshape(
            (2,) * NB + (2 * R, n)
        )

    def all_z(ref):
        return jnp.concatenate([ref[z] for z in range(T)], axis=-1)

    def whole(ref):
        return ref[...].reshape(M, D)

    def mod(r):
        return mods[r : r + 1, :]

    def transpose_into(dst, ref):
        for n in range(D // 128):
            block = ref[:, :, n * 128 : (n + 1) * 128].reshape(M, 128)
            dst[n * 128 : (n + 1) * 128, :] = block.T

    place_of = {pc: j for j, pc in enumerate(dm.sums_order)}

    def rs_fixed(step, h, away):
        order_r = order[h][::-1]
        fixed = {k: mybit[k] for k in order_r[: step + 1]}
        b = order_r[step]
        if away:
            fixed[b] = 1 - mybit[b]
        return b, fixed

    FIRST = 1 if dm.inside else 0

    def rf_copy(step, h):
        lo, width = dm.pieces[dm.sums_order[0]]
        b, fixed = rs_fixed(step, h, True)
        part = wall.at[(me_z,) + place(fixed) + (every, pl.ds(lo + h * (width // 2), width // 2))]
        return rdma(part, m.rf[step].at[h], m.rs_s.at[0, step, h], m.rs_r.at[0, step, h], bit_dev(b))

    def rf_add(step, h):
        rf_copy(step, h).wait_recv()
        lo, width = dm.pieces[dm.sums_order[0]]
        b, fixed = rs_fixed(step, h, False)
        where = (me_z,) + place(fixed) + (every, pl.ds(lo + h * (width // 2), width // 2))
        wall[where] = (wall[where].astype(F32) + m.rf[step][h].astype(F32)).astype(B16)

    def rs_copy(j, step, h):
        pc = dm.sums_order[j]
        b, fixed = rs_fixed(step, h, True)
        part = wall.at[(half_z(h),) + place(fixed) + (every, cols(pc))]
        buf = m.rb[step].at[((j - FIRST) % SLOTS, h) + (every,) * (NB - step) + (every, pl.ds(0, dm.pieces[pc][1]))]
        return rdma(part, buf, m.rs_s.at[j, step, h], m.rs_r.at[j, step, h], bit_dev(b))

    def rs_start(j, step, h):
        if j - FIRST >= SLOTS:
            pl.semaphore_wait(m.free.at[step, h], 1)
        rs_copy(j, step, h).start()

    def rs_add(j, step, h):
        pc = dm.sums_order[j]
        rs_copy(j, step, h).wait_recv()
        b, fixed = rs_fixed(step, h, False)
        rest = [k for k in reversed(range(NB)) if k not in fixed]
        slot, width = (j - FIRST) % SLOTS, dm.pieces[pc][1]

        def one(i, carry):
            zz, r = i // (1 << len(rest)), lax.rem(i, 1 << len(rest))
            at = dict(fixed)
            inner = ()
            for pos, k in enumerate(rest):
                v = lax.rem(r // (1 << (len(rest) - 1 - pos)), 2)
                at[k] = v
                inner += (v,)
            where = (h * TH + zz,) + place(at) + (every, cols(pc))
            got = m.rb[step][(slot, h, zz) + inner + (every, pl.ds(0, width))]
            wall[where] = (wall[where].astype(F32) + got.astype(F32)).astype(B16)
            return carry

        lax.fori_loop(0, TH << len(rest), one, 0)
        if j + SLOTS < NP:
            pl.semaphore_signal(m.free.at[step, h], inc=1, device_id=bit_dev(b), device_id_type=MESH)

    def rz_blocks(j):
        pc = dm.sums_order[j]
        if j >= FIRST:
            return [(mine, cols(pc))]
        width = dm.pieces[pc][1]
        return [(place({b: (p >> b) & 1 for b in range(NB)}), pl.ds(p * width, width)) for p in range(NC)]

    ends_here = jnp.logical_not(inner)

    def rz_copies(j, off):
        pc, out = dm.sums_order[j], []
        for i, (chip_at, at) in enumerate(rz_blocks(j)):
            part = wall.at[(lax.rem(me_z + off, T),) + chip_at + (every, cols(pc))]
            sems = m.rz_s.at[j, off - 1, i], m.rz_r.at[j, off - 1, i]
            out.append(rdma(part, m.zb.at[off - 1, :, at], *sems, z_dev(off)))
        return out

    def rz_specials(j):
        pc, out = dm.sums_order[j], []
        dev = tag_z((dpi, jnp.where(me_z == 0, 1, T - 2)))
        for i, (chip_at, at) in enumerate(rz_blocks(j)):
            part = wall.at[(T - 1 - me_z,) + chip_at + (every, cols(pc))]
            out.append(rdma(part, m.zx.at[:, at], m.rx_s.at[j, i], m.rx_r.at[j, i], dev))
        return out

    def each(copies, do):
        for copy in copies:
            getattr(copy, do)()

    def rz_begin(j):
        if j == FIRST and FIRST:
            pl.semaphore_wait(m.zfree, T - 1)

        @pl.when(ends_here)
        def _():
            each(rz_specials(j), "start")
            each(rz_copies(j, 2), "start")

        for off, allowed in line_sends[1:]:
            @pl.when(allowed)
            def _():
                each(rz_copies(j, off), "start")

    def rz_middle(j):
        pc = dm.sums_order[j]

        @pl.when(inner)
        def _():
            each(rz_specials(j), "wait_recv")
            for chip_at, at in rz_blocks(j):
                where = (lax.rem(me_z + 2, T),) + chip_at + (every, cols(pc))
                wall[where] = (wall[where].astype(F32) + m.zx[:, at].astype(F32)).astype(B16)
            each(rz_copies(j, 2), "start")

    def rz_wait(j):
        each(rz_copies(j, 2), "wait_recv")
        for off, came in ((1, me_z > 0), (3, me_z < T - 1)):
            @pl.when(came)
            def _():
                each(rz_copies(j, off), "wait_recv")

    def rz_sent(j):
        each(rz_copies(j, 2), "wait_send")
        for off, allowed in line_sends[1:]:
            @pl.when(allowed)
            def _():
                each(rz_copies(j, off), "wait_send")

        @pl.when(ends_here)
        def _():
            each(rz_specials(j), "wait_send")

    def final(pc, c):
        if pc < 3:
            return m.g_qkv, (pc, every, lanes_of(c * hq, hq))
        if pc == 3:
            return m.g_proj, (pl.ds(pl.multiple_of(c * hq, hq), hq), every)
        at = c * fu + (pc - 4) // 2 * half
        if pc % 2 == 0:
            return m.g_up, (every, lanes_of(at, half))
        return m.g_down, (pl.ds(pl.multiple_of(at, half), half), every)

    def turned(pc):
        return pc in (3, 5, 7)

    def fin_from(j):
        pc = dm.sums_order[j]
        width = dm.pieces[pc][1]
        if turned(pc):
            return m.fturn, (j // 2 % 2, pl.ds(0, width))
        return m.fbuf, (j % FINS, every, pl.ds(0, width))

    def fin_copy(j):
        pc = dm.sums_order[j]
        ref, at = fin_from(j)
        out, place_ = final(pc, core)
        return rdma(ref.at[at], out.at[place_], m.f_s.at[j], m.f_r.at[j], partner)

    def rz_sum(j, chip_at, at, rows):
        acc = wall[(me_z,) + chip_at + (rows, cols(dm.sums_order[j]))].astype(F32)
        for off in range(1, T):
            acc = acc + m.zb[off - 1, rows, at].astype(F32)
        return acc

    def finish(j, total):
        pc = dm.sums_order[j]
        if j >= FINS:
            fin_copy(j - FINS).wait_send()
        ref, at = fin_from(j)
        out, place_ = final(pc, core)
        away, kept = total(core_rows(1 - core)), total(core_rows(core))
        ref[at] = away.T if turned(pc) else away
        fin_copy(j).start()
        out[place_] = kept.T if turned(pc) else kept

    def rs_event(j, s):
        pc = dm.sums_order[j]
        if j < FIRST:
            if s == 1:
                rz_middle(j)
            elif s == 2:
                rz_wait(j)
                for chip_at, at in rz_blocks(j):
                    wall[(me_z,) + chip_at + (every, cols(pc))] = rz_sum(j, chip_at, at, every).astype(B16)
                for off in range(1, T):
                    pl.semaphore_signal(m.zfree, inc=1, device_id=z_dev(off), device_id_type=MESH)
            if s > 2:
                for h in range(2):
                    rf_add(s - 3, h)
            if 2 <= s < NB + 2:
                for h in range(2):
                    rf_copy(s - 2, h).start()
            if s == NB + 2:
                finish(j, lambda rows: wall[(me_z,) + mine + (rows, cols(pc))].astype(F32))
            return
        if s <= NB:
            for h in range(2):
                rs_add(j, s - 1, h)
                if s < NB:
                    rs_start(j, s, h)
            if s == NB:
                rz_begin(j)
            return
        if s == NB + 1:
            rz_middle(j)
            return
        rz_wait(j)
        finish(j, lambda rows: rz_sum(j, mine, cols(pc), rows))

    events = sorted(((j, s) for j in range(NP) for s in range(1, NB + 3)), key=lambda e: (e[0] + LEAN * e[1], e[0]))
    begun = set()

    def pump(count):
        while count and events and (events[0][0], 1) in begun:
            rs_event(*events.pop(0))
            count -= 1

    stops = list(PUMPS)

    def stop():
        pump(stops.pop(0) if stops else 0)

    def rs_begin(pc, h):
        j = place_of[pc]
        while j - SLOTS >= FIRST and (j - SLOTS, 1) in events:
            pump(1)
        if j >= FIRST:
            rs_start(j, 0, h)
        elif h == 1:
            rz_begin(j)
        begun.add((j, h))

    def rs_end():
        for j in range(NP):
            for step in range(NB):
                for h in range(2):
                    (rs_copy(j, step, h) if j >= FIRST else rf_copy(step, h)).wait_send()
            rz_sent(j)
            fin_copy(j).wait_recv()
            if j + FINS >= NP:
                fin_copy(j).wait_send()

    def small(src, dst, k, dev):
        return rdma(src, dst, m.s_s.at[k], m.s_r.at[k], dev)

    def sum_step(acc, got, i, base, sign, rows=None):
        dev = partner if i < sign else bit_dev(i - sign)
        n = acc.shape[1] if rows is None else rows
        return small(acc.at[i, pl.ds(0, n)], got.at[i, pl.ds(0, n)], base + i, dev)

    def sum_finish(acc, got, i, base, sign, rows=None):
        sum_step(acc, got, i, base, sign, rows).wait_recv()
        n = acc.shape[1] if rows is None else rows
        acc[i + 1, 0:n] = acc[i, 0:n] + got[i, 0:n]

    S_SID = 0
    S_M1 = 1
    S_M2 = S_M1 + NB + 1
    S_SM = S_M2 + T - 1
    S_M3 = S_SM + T - 1
    S_M4 = S_M3 + NC - 1
    S_B1 = S_M4 + 1
    S_B2 = S_B1 + NC - 1
    S_B3 = S_B2 + T - 1
    S_PZ = S_B3 + NB + 1
    S_PB = S_PZ + T - 1
    S_PC = S_PB + NB

    sid_copy = small(m.sid, m.sidr, S_SID, partner)
    sid_copy.start()
    if dm.inside:
        m.macc[0] = m.m1[...]
        sum_step(m.macc, m.mrec, 0, S_M1, 1).start()
    for pc in (0, 1, 2, 4, 6):
        core_copy(pc).start()
        core_local(pc).start()
    gather_to(-1.0)
    transpose_own()
    for pc in (3, 5, 7):
        core_copy(pc).start()
        core_local(pc).start()
    for z, slot in ((0, 0), (T - 1, T - 2)):
        @pl.when(me_z == z)
        def _():
            m.zb[slot] = jnp.zeros(m.zb.shape[1:], B16)

    sums[...] = jnp.zeros_like(sums)
    hsum[...] = jnp.zeros_like(hsum)
    fsum[...] = jnp.zeros_like(fsum)

    if dm.inside:
        for i in range(NB + 1):
            sum_finish(m.macc, m.mrec, i, S_M1, 1)
            if i < NB:
                sum_step(m.macc, m.mrec, i + 1, S_M1, 1).start()
        m.sm[me_z] = m.macc[NB + 1, 8:16, :]
        for off in range(1, T):
            small(m.sm.at[me_z], m.sm.at[me_z], S_SM + off - 1, z_dev(off)).start()
        m.cond[...] = m.macc[NB + 1, 0:8, :]
        width = D // T
        for zz in range(T):
            c = m.cond[:, zz * width : (zz + 1) * width]
            low = (c / (1.0 + jnp.exp(-c))).astype(B16)
            rows = [dot(low, m.wada[j]) for j in range(6)] + [jnp.zeros((8, 2 * R), F32)]
            m.m2s[zz] = jnp.concatenate(rows, axis=-1)
        for off in range(1, T):
            small(m.m2s.at[lax.rem(me_z + off, T)], m.m2r.at[off - 1], S_M2 + off - 1, z_dev(off)).start()

    gather_to(1.85)
    tok_start(0, m.xb, xs)

    if dm.inside:
        for off in range(1, T):
            small(m.m2s.at[0], m.m2r.at[off - 1], S_M2 + off - 1, z_dev(off)).wait_recv()
        m.m3c[core, chip] = m.m2s[me_z] + sum(m.m2r[k] for k in range(T - 1)) + m.badd[...]
        own = m.m3c.at[core, chip]
        for k in range(1, NC):
            small(own, own, S_M3 + k - 1, chip_dev(k)).start()
        gather_to(2.15)
        for off in range(1, T):
            got = m.sm.at[lax.rem(me_z - off + T, T)]
            small(got, got, S_SM + off - 1, z_dev(off)).wait_recv()
        head_cols = pl.ds(pl.multiple_of(core * hq, hq), hq)
        for z in range(T):
            for r in range(3):
                hp[z, r : r + 1, :] = m.sm[z, r + 1 : r + 2, head_cols]
            hp[z, 3:4, :] = 1.0 / hp[z, 2:3, :]
            hb[z, 0:1, :] = m.sm[z, 0:1, pl.ds(pl.multiple_of(core * fu, fu), fu)]
        for k in range(1, NC):
            got = m.m3c.at[core, lax.rem(chip - k + NC, NC)]
            small(got, got, S_M3 + k - 1, chip_dev(k)).wait_recv()
        small(m.m3c.at[core], m.m3c.at[core], S_M4, partner).start()

    got = small(m.sidr, m.sidr, S_SID, partner)
    got.wait_recv()
    pick = lax.rem(me_z, 2)
    ids = jnp.where(owner, m.sid[pl.ds(pick, 1), :], m.sidr[pl.ds(pick, 1), :])
    lanes = lax.broadcasted_iota(jnp.int32, (128, 1), 0).astype(F32)
    m.psi[...] = jnp.where(lanes > ids, FAR, 0.0).astype(B16).T
    m.phi[...] = jnp.where(lanes == ids, -1.0, 0.0).astype(B16).T

    if dm.inside:
        got = m.m3c.at[1 - core]
        small(got, got, S_M4, partner).wait_recv()
        for c in range(2):
            for p in range(NC):
                row = m.m3c[c, p, pl.ds(chip, 1), :]
                d = 2 * p + c
                for j in range(8):
                    mods[j : j + 1, d * R : (d + 1) * R] = row[:, j * R : (j + 1) * R]

    gather_to(4.1)
    tok_wait(0, m.xb, xs)

    def ln(rows):
        centred = rows - jnp.mean(rows, axis=-1, keepdims=True)
        inv = lax.rsqrt(jnp.mean(centred * centred, axis=-1, keepdims=True) + EPS)
        return centred * inv, inv

    def first_norm(t, carry):
        normed, _ = ln(xs[t].astype(F32))
        h1[t] = (normed * (1.0 + mod(2)) + mod(4)).astype(B16)
        return carry

    lax.fori_loop(0, T, first_norm, 0)
    gather_to(4.96)
    if dm.inside:
        for i in range(NB + 1):
            sum_step(m.macc, m.mrec, i, S_M1, 1).wait_send()
    gather_until(2)

    lane = lax.broadcasted_iota(jnp.int32, (1, hq), 1)
    halves = [(lane // dm.hd) == k for k in range(hq // dm.hd)]
    bi = lax.broadcasted_iota(jnp.int32, (hq, hq), 0) // dm.hd
    bj = lax.broadcasted_iota(jnp.int32, (hq, hq), 1) // dm.hd
    same_head = (bi == bj).astype(B16)

    def qkv(z, carry):
        t = dot(whole(h1), wz(z, 0, 3 * hq))
        q = t[:, :hq] + hp[z, 0:1, :]
        k = t[:, hq : 2 * hq]
        v = t[:, 2 * hq :] + hp[z, 1:2, :]
        qi = lax.rsqrt(split_dot(q * q, same_head) + EPS)
        ki = lax.rsqrt(split_dot(k * k, same_head) + EPS)
        m.qs[z] = (q * qi * hp[z, 2:3, :]).astype(B16)
        m.ks[z] = (k * ki).astype(B16)
        m.vs[z] = v.astype(B16)
        m.rq[z] = qi.astype(B16)
        m.rk[z] = ki.astype(B16)
        return carry

    lax.fori_loop(0, T, qkv, 0)
    zero16 = jnp.zeros((), B16)

    def expo(z, k, q_all, k_all):
        q_one = jnp.where(halves[k], q_all, zero16)
        left = jnp.concatenate([q_one, m.psi[...]], axis=1)
        right = jnp.concatenate([k_all, m.phi[...]], axis=1)
        return q_one, jnp.exp(dot_nt(left, right)).astype(B16)

    def attend(z, carry):
        q_all, k_all, v_all = m.qs[z], m.ks[z], m.vs[z]
        v_ones = jnp.concatenate([v_all, jnp.ones((M, hq), B16)], axis=1)
        mixed = inverse = None
        for k in range(hq // dm.hd):
            _, e = expo(z, k, q_all, k_all)
            both_ = dot(e, v_ones)
            inv = 1.0 / both_[:, hq:]
            one = both_[:, :hq] * inv
            mixed = one if mixed is None else jnp.where(halves[k], one, mixed)
            inverse = inv if inverse is None else jnp.where(halves[k], inv, inverse)
        m.o[z] = mixed.astype(B16)
        m.ol[z] = (mixed - mixed.astype(B16).astype(F32)).astype(B16)
        m.do[z] = inverse.astype(B16)
        return carry

    gather_to(5.0)
    for z in range(T):
        lax.fori_loop(z, z + 1, attend, 0)
        if z == 1:
            gather_to(5.9)
            tok_start(1, m.dyb, dys)

    gather_until(3)
    o_all = all_z(m.o)
    for n in range(NCH):
        exchange(0, n, dot_nt(o_all, wrows_all(n, 3 * hq, hq)))
    exchange_wait(0)

    def second_norm(t, carry):
        a = both(0, t) + mod(6)
        m.ab[t] = a.astype(B16)
        normed, inv = ln(xs[t].astype(F32) + mod(0) * a)
        h2[t] = (normed * (1.0 + mod(3)) + mod(5)).astype(B16)
        m.n2[t] = normed.astype(B16)
        m.r2[t] = jnp.broadcast_to(inv, (Q, 128))
        return carry

    lax.fori_loop(0, T, second_norm, 0)
    gather_to(7.05)
    exchange_sent(0)
    transpose_into(m.xt, h2)

    def out_grad(t, carry):
        d = (mod(1) * dys[t].astype(F32)).astype(B16)
        m.df[t] = d
        sums[7:8, :] += row_sum(d.astype(F32))
        return carry

    root = 0.7978845608028654

    def hidden(k):
        lo_u, lo_d = dm.up + k * half, dm.down + k * half

        def up(z, carry):
            u = dot(whole(h2), wz(z, lo_u, half)) + hb[z, 0:1, k * half : (k + 1) * half]
            uu = u * u
            th = jnp.tanh(root * u * (1.0 + 0.044715 * uu))
            m.gk[z] = (0.5 * u * (1.0 + th)).astype(B16)
            m.duk[z] = (0.5 * (1.0 + th) + (0.5 * root) * u * (1.0 - th * th) * (1.0 + 0.134145 * uu)).astype(B16)
            return carry

        def down(z, carry):
            dg = dot(whole(m.df), wz(z, lo_d, half))
            du = (dg * m.duk[z].astype(F32)).astype(B16)
            m.duk[z] = du
            fsum[z, 0:1, k * half : (k + 1) * half] = row_sum(du.astype(F32))
            return carry

        gather_until(4 + 2 * k)
        lax.fori_loop(0, T, up, 0)
        if k == 0:
            gather_to(7.15)
            tok_wait(1, m.dyb, dys)
            lax.fori_loop(0, T, out_grad, 0)
            transpose_into(m.xt2, m.df)
        gather_until(5 + 2 * k)
        lax.fori_loop(0, T, down, 0)

    def grads(k, begin):
        lo_u, lo_d = dm.up + k * half, dm.down + k * half

        def down_grad(z, carry):
            wstore(z, lo_d, half, dot(m.xt2[...], m.gk[z]))
            return carry

        def up_grad(z, carry):
            wstore(z, lo_u, half, dot(m.xt[...], m.duk[z]))
            return carry

        for pc, body in ((5 + 2 * k, down_grad), (4 + 2 * k, up_grad)):
            for h in range(2):
                lax.fori_loop(h * TH, (h + 1) * TH, body, 0)
                if pc in begin:
                    rs_begin(pc, h)

    for pc in range(NP):
        core_copy(pc).wait_send()
    hidden(0)
    du_all, g_all = all_z(m.duk), all_z(m.gk)
    for n in range(NCH):
        m.dacc[n] = dot_nt(du_all, wrows_all(n, dm.up, half))
        m.facc[n] = dot_nt(g_all, wrows_all(n, dm.down, half))
    gather_sent((4, 5))
    gather_to(99.0)
    grads(0, (5, 4))
    hidden(1)
    du_all, g_all = all_z(m.duk), all_z(m.gk)
    for n in range(NCH):
        exchange(1, n, m.dacc[n] + dot_nt(du_all, wrows_all(n, dm.up + half, half)))
    for n in range(NCH):
        m.facc[n] = m.facc[n] + dot_nt(g_all, wrows_all(n, dm.down + half, half))
    gather_sent((0, 1, 2, 3, 6, 7))
    grads(1, (7,))
    stop()
    transpose_into(m.xt, h1)
    tok_sent(1, m.dyb, dys)
    exchange_wait(1)
    if sender(2) is not m.send:
        for n in range(NCH):
            exchange(2, n, m.facc[n])

    def ln_back(e, normed, inv):
        return (e - jnp.mean(e, axis=-1, keepdims=True) - normed * jnp.mean(e * normed, axis=-1, keepdims=True)) * inv

    def mid_back(t, carry):
        dh = both(1, t)
        normed = m.n2[t].astype(F32)
        sums[3:4, :] += row_sum(dh * normed)
        sums[5:6, :] += row_sum(dh)
        step_back = ln_back(dh * (1.0 + mod(3)), normed, m.r2[t, :, 0:1])
        h2[t] = step_back.astype(B16)
        dx1 = dys[t].astype(F32) + step_back
        sums[0:1, :] += row_sum(dx1 * m.ab[t].astype(F32))
        da = (mod(0) * dx1).astype(B16)
        m.df[t] = da
        sums[6:7, :] += row_sum(da.astype(F32))
        return carry

    lax.fori_loop(0, T, mid_back, 0)
    pl.semaphore_signal(m.took, inc=1, device_id=partner, device_id_type=MESH)
    stop()
    for h in range(2):
        rs_begin(6, h)
    exchange_sent(1)
    if sender(2) is m.send:
        for n in range(NCH):
            exchange(2, n, m.facc[n])

    def last(t, carry):
        f = both(2, t) + mod(7)
        m.n2[t] = (mod(0) * m.ab[t].astype(F32) + mod(1) * f).astype(B16)
        sums[1:2, :] += row_sum(dys[t].astype(F32) * f)
        return carry

    exchange_wait(2)
    lax.fori_loop(0, T, last, 0)
    exchange_sent(2)
    back_start(0, m.outd)

    w_proj = jnp.concatenate([wz(z, 3 * hq, hq) for z in range(T)], axis=-1)
    do_all = dot(whole(m.df), w_proj).astype(B16)
    for z in range(T):
        m.do[z] = (do_all[:, z * hq : (z + 1) * hq].astype(F32) * m.do[z].astype(F32)).astype(B16)
    transpose_into(m.xt2, m.df)
    dw = dot(m.xt2[...], all_z(m.o))
    for z in range(T):
        wstore(z, 3 * hq, hq, dw[:, z * hq : (z + 1) * hq])
    for h in range(2):
        rs_begin(3, h)
    stop()

    ends = jnp.where(lane < 2, -1.0, 0.0).astype(B16)

    def attend_back(z, carry):
        q_all, k_all, v_all = m.qs[z], m.ks[z], m.vs[z]
        dob = m.do[z]
        prod = dob.astype(F32) * (m.o[z].astype(F32) + m.ol[z].astype(F32))
        v_ends = jnp.concatenate([v_all, jnp.broadcast_to(ends, (M, hq))], axis=1)
        dq = dk = dv = 0.0
        for k in range(hq // dm.hd):
            q_one, e = expo(z, k, q_all, k_all)
            to_all = (bi == k).astype(B16)
            total = split_dot(prod, to_all)
            high = total.astype(B16)
            low = (total - high.astype(F32)).astype(B16)
            extra = jnp.where(lane == 0, high, jnp.where(lane == 1, low, zero16))
            d_one = jnp.where(halves[k], dob, zero16)
            dp = dot_nt(jnp.concatenate([d_one, extra], axis=1), v_ends)
            ds = (e.astype(F32) * dp).astype(B16)
            dq = dq + dot(ds, jnp.where(halves[k], k_all, zero16))
            dk = dk + dot_tn(ds, q_one)
            dv = dv + dot_tn(e, d_one)
        gain = hp[z, 2:3, :]
        q_hat = q_all.astype(F32) * hp[z, 3:4, :]
        k_hat = k_all.astype(F32)
        hsum[z, 2:3, :] = row_sum(dq * q_hat)
        eq = dq * gain
        dq = ((eq - q_hat * split_dot(eq * q_hat, same_head)) * m.rq[z].astype(F32)).astype(B16)
        dk = ((dk - k_hat * split_dot(dk * k_hat, same_head)) * m.rk[z].astype(F32)).astype(B16)
        dv = dv.astype(B16)
        hsum[z, 0:1, :] = row_sum(dq.astype(F32))
        hsum[z, 1:2, :] = row_sum(dv.astype(F32))
        m.dqkv[...] = jnp.concatenate([dq, dk, dv], axis=1)
        return carry

    for z in range(T):
        lax.fori_loop(z, z + 1, attend_back, 0)
        if z == T - 1:
            pl.semaphore_wait(m.took, 1)
        d_one_z = m.dqkv[...]
        for n in range(NCH):
            part = dot_nt(d_one_z, wrows(z, n, 0, 3 * hq))
            if z == T - 1:
                exchange(3, n, m.facc[n] + part)
            else:
                m.facc[n] = part if z == 0 else m.facc[n] + part
        wstore(z, 0, 3 * hq, dot(m.xt[...], d_one_z))
        for pc, h in BEGIN[z]:
            rs_begin(pc, h)
        stop()

    if dm.inside:
        for z in range(T):
            m.pks[z] = jnp.concatenate([hsum[z], fsum[z], sums[...]], axis=-1)
        for off in range(1, T):
            small(m.pks.at[lax.rem(me_z + off, T)], m.pkr.at[off - 1], S_PZ + off - 1, z_dev(off)).start()
    exchange_wait(3)

    def first_back(t, carry):
        dh = both(3, t)
        normed, inv = ln(xs[t].astype(F32))
        sums[2:3, :] += row_sum(dh * normed)
        sums[4:5, :] += row_sum(dh)
        m.ab[t] = (h2[t].astype(F32) + ln_back(dh * (1.0 + mod(2)), normed, inv)).astype(B16)
        return carry

    for t in range(T):
        lax.fori_loop(t, t + 1, first_back, 0)
        if t % 2:
            stop()
    exchange_sent(3)
    if not dm.inside:
        back_start(1, m.gind)

    if dm.inside:
        for off in range(1, T):
            zt = lax.rem(me_z + off, T)
            small(m.m2s.at[zt], m.m2r.at[off - 1], S_M2 + off - 1, z_dev(off)).wait_send()
        for p in range(NC):
            d = pl.multiple_of((2 * p + core) * R, R)
            rows = [sums[j : j + 1, pl.ds(d, R)] for j in range(8)]
            m.m2s[p] = jnp.broadcast_to(jnp.concatenate(rows, axis=-1), (8, 8 * R))
        for k in range(1, NC):
            small(m.m2s.at[lax.rem(chip + k, NC)], m.b1r.at[k - 1], S_B1 + k - 1, chip_dev(k)).start()
        stop()
        stop()
        for k in range(1, NC):
            small(m.m2s.at[0], m.b1r.at[k - 1], S_B1 + k - 1, chip_dev(k)).wait_recv()
        row8 = lax.broadcasted_iota(jnp.int32, (8, 1), 0)
        packed = jnp.where(row8 == chip, m.m2s[chip], 0.0)
        for k in range(1, NC):
            packed = jnp.where(row8 == lax.rem(chip - k + NC, NC), m.b1r[k - 1], packed)
        m.dmodf[me_z] = packed
        for off in range(1, T):
            small(m.dmodf.at[me_z], m.dmodf.at[me_z], S_B2 + off - 1, z_dev(off)).start()
        stop()
        for off in range(1, T):
            small(m.pks.at[0], m.pkr.at[off - 1], S_PZ + off - 1, z_dev(off)).wait_recv()
        m.pka[0] = m.pks[me_z] + sum(m.pkr[k] for k in range(T - 1))
        if NB:
            sum_step(m.pka, m.pkb, 0, S_PB, 0).start()
        for off in range(1, T):
            got = m.dmodf.at[lax.rem(me_z - off + T, T)]
            small(got, got, S_B2 + off - 1, z_dev(off)).wait_recv()
        width = D // T
        for zz in range(T):
            acc = 0.0
            for j in range(6):
                acc = acc + dot_nt(m.dmodf[zz, :, j * R : (j + 1) * R].astype(B16), m.wada[j])
            m.macc[0, 0:8, zz * width : (zz + 1) * width] = acc
        sum_step(m.macc, m.mrec, 0, S_B3, 1, 8).start()
        for i in range(NB + 1):
            if i < NB:
                sum_finish(m.pka, m.pkb, i, S_PB, 0)
                if i + 1 < NB:
                    sum_step(m.pka, m.pkb, i + 1, S_PB, 0).start()
            if i == NB:
                m.pk[core] = m.pka[NB]
                small(m.pka.at[NB], m.pk.at[core], S_PC, partner).start()
            sum_finish(m.macc, m.mrec, i, S_B3, 1, 8)
            if i < NB:
                sum_step(m.macc, m.mrec, i + 1, S_B3, 1, 8).start()
            stop()
        m.dsil[...] = m.macc[NB + 1, 0:8]
    while (NP - 1, NB) in events:
        pump(1)
    if dm.inside:
        back_start(1, m.gind)
    pump(len(events))
    assert not events
    rs_end()
    tok_sent(0, m.xb, xs)
    back_wait(0, m.outd)
    back_wait(1, m.gind)
    sid_copy.wait_send()
    if dm.inside:
        for i in range(NB + 1):
            sum_step(m.macc, m.mrec, i, S_B3, 1, 8).wait_send()
        for i in range(NB):
            sum_step(m.pka, m.pkb, i, S_PB, 0).wait_send()
        for off in range(1, T):
            zt = lax.rem(me_z + off, T)
            small(m.sm.at[me_z], m.sm.at[me_z], S_SM + off - 1, z_dev(off)).wait_send()
            small(m.pks.at[zt], m.pkr.at[off - 1], S_PZ + off - 1, z_dev(off)).wait_send()
            small(m.dmodf.at[me_z], m.dmodf.at[me_z], S_B2 + off - 1, z_dev(off)).wait_send()
        for k in range(1, NC):
            small(m.m3c.at[core, chip], m.m3c.at[core, chip], S_M3 + k - 1, chip_dev(k)).wait_send()
            small(m.m2s.at[lax.rem(chip + k, NC)], m.b1r.at[k - 1], S_B1 + k - 1, chip_dev(k)).wait_send()
        small(m.m3c.at[core], m.m3c.at[core], S_M4, partner).wait_send()
        small(m.pka.at[NB], m.pk.at[core], S_PC, partner).wait_send()
        got = m.pk.at[1 - core]
        small(got, got, S_PC, partner).wait_recv()


def block_call(dm, weights, xb, dyb, sid, extra):
    T, NC, NB, Q, M, D, R, C, W = dm.T, dm.NC, dm.bits, dm.Q, dm.M, dm.D, dm.R, dm.C, dm.W
    hq, fu, NCH, half = dm.hq, dm.fu, dm.NCH, dm.half
    TH, NP = T // 2, len(dm.pieces)
    two = (2,) * NB
    v = pltpu.VMEM
    dma = pltpu.SemaphoreType.DMA
    any_, vm = pl.BlockSpec(memory_space=pl.ANY), pl.BlockSpec(memory_space=pltpu.VMEM)
    s = jax.ShapeDtypeStruct
    tok, heads, acc = (T, Q, D), (T, M, hq), (NCH, M, CHUNK)
    ins = {**weights, "xb": xb, "dyb": dyb, "sid": sid, **extra}
    outs = {"g_qkv": s((3, R, 2 * hq), F32), "g_proj": s((2 * hq, R), F32), "g_up": s((R, 2 * fu), F32), "g_down": s((2 * fu, R), F32), "outd": s((2, Q, D), B16), "gind": s((2, Q, D), B16)}
    totals = {"sums": (8, D), "hsum": (T, 8, hq), "fsum": (T, 8, fu)}
    scratch = {"wall": v((T,) + two + (2 * R, C), B16)}
    for name in "xs dys h1 h2 ab n2 df".split():
        scratch[name] = v(tok, B16)
    for name in "qs ks vs rq rk o ol do".split():
        scratch[name] = v(heads, B16)
    scratch.update(
        r2=v((T, Q, 128), F32), psi=v((M, 128), B16), phi=v((M, 128), B16), sidr=v((8, M), F32),
        gk=v((T, M, half), B16), duk=v((T, M, half), B16), facc=v(acc, F32), dacc=v(acc, F32),
        send=v((NCH, M, CHUNK), B16), recv=v((2, NCH, M, CHUNK), B16),
        xt=v((D, M), B16), xt2=v((D, M), B16), dqkv=v((M, 3 * hq), B16),
        zb=v((T - 1, 2 * R, C), B16), zx=v((2 * R, C), B16), fbuf=v((FINS, R, half), F32), fturn=v((2, half, R), F32),
    )
    for k in range(NB):
        scratch[f"rf{k}"] = v((2,) + (2,) * (NB - 1 - k) + (2 * R, half // 2), B16)
        scratch[f"rb{k}"] = v((SLOTS, 2, TH) + (2,) * (NB - 1 - k) + (2 * R, half), B16)
    if dm.inside:
        outs.update(dmodf=s((T, 8, 8 * R), F32), cond=s((8, D), F32), dsil=s((8, D), F32), pk=s((2, 8, W), F32))
        scratch.update({name: v(shape, F32) for name, shape in totals.items()})
        scratch.update(
            mods=v((8, D), F32), hp=v((T, 8, hq), F32), hb=v((T, 8, fu), F32),
            macc=v((NB + 2, 16, D), F32), mrec=v((NB + 1, 16, D), F32), sm=v((T, 8, D), F32),
            m2s=v((T, 8, 8 * R), F32), m2r=v((T - 1, 8, 8 * R), F32), m3c=v((2, NC, 8, 8 * R), F32),
            b1r=v((max(NC - 1, 1), 8, 8 * R), F32),
            pks=v((T, 8, W), F32), pkr=v((T - 1, 8, W), F32), pka=v((NB + 1, 8, W), F32), pkb=v((max(NB, 1), 8, W), F32),
        )
    else:
        outs.update({name: s(shape, F32) for name, shape in totals.items()})
    small = 4 * NB + 6 * T + 2 * NC + 8
    reg = pltpu.SemaphoreType.REGULAR
    scratch.update(
        c_s=dma((NP,)), c_r=dma((NP,)), c_l=dma((NP,)), z_s=dma((NP, T - 1)), z_r=dma((NP, T - 1)),
        p_s=dma((NP, NB, 2)), p_r=dma((NP, NB, 2)), x_s=dma((2, 2)), x_r=dma((2, T)), x_l=dma((2,)), x_f=dma((2, 2)),
        e_s=dma((4, NCH)), e_r=dma((4, NCH)), rs_s=dma((NP, NB, 2)), rs_r=dma((NP, NB, 2)), free=reg((NB, 2)), took=reg,
        rz_s=dma((NP, T - 1, NC)), rz_r=dma((NP, T - 1, NC)), rx_s=dma((NP, NC)), rx_r=dma((NP, NC)), zfree=reg, f_s=dma((NP,)), f_r=dma((NP,)), z_f=dma((NP,)),
        o_s=dma((2, T)), o_r=dma((2, 2)), o_l=dma((2,)), s_s=dma((small,)), s_r=dma((small,)),
    )
    names = tuple(ins) + tuple(outs) + tuple(scratch)
    got = pl.pallas_call(
        functools.partial(block_kernel, dm, names),
        out_shape=tuple(outs.values()),
        in_specs=[any_ if name in ("wqkv", "wup", "xb", "dyb") else vm for name in ins],
        out_specs=tuple(any_ if name in ("outd", "gind") else vm for name in outs),
        scratch_shapes=list(scratch.values()),
        compiler_params=pltpu.CompilerParams(
            collective_id=0, has_side_effects=True, vmem_limit_bytes=66 * 1024 * 1024
        ),
        cost_estimate=pl.CostEstimate(flops=30 * 10**9, bytes_accessed=10**7, transcendentals=10**7),
    )(*ins.values())
    return dict(zip(outs, got))


def local(
    dp, tensor,
    block_input, cotangent, class_ids, scale_ids, class_table, w_ada, b_ada, query_key_value_weight,
    qv_bias, q_gain, output_projection, up_weight, hidden_bias, down_weight, projection_bias,
):
    seqs, quarter, width = block_input.shape
    length = scale_ids.shape[1]
    assert seqs == 2 and tensor == 4
    rows = -(-quarter // 16) * 16
    head = q_gain.shape[1] * dp
    hidden = up_weight.shape[1] * tensor
    dm = Dims(dp, tensor, rows, width, head, hidden)
    T, R, hq, fu, NC, M = dm.T, dm.R, dm.hq, dm.fu, dm.NC, dm.M
    total = class_ids.shape[0]
    di, zi = lax.axis_index("dp"), lax.axis_index("tensor")
    core = di % 2

    pad_rows = ((0, 0), (0, 0), (0, rows - quarter))
    sid = jnp.pad(scale_ids.astype(F32).reshape(2, T, quarter), pad_rows, constant_values=127.0).reshape(2, M)
    sid = jnp.pad(sid, ((0, 6), (0, 0)))
    my_rows = class_table.shape[0]
    my_ids = di * my_rows + jnp.arange(my_rows, dtype=jnp.int32)

    if dm.inside:
        place = jnp.arange(dp, dtype=jnp.int32) == di

        def spread(w):
            return jnp.where(place[:, None], w[..., None, :], 0).reshape(w.shape[:-2] + (-1,)).astype(F32)

        def pad_lanes(w):
            return jnp.pad(w, ((0, 0), (0, width - w.shape[1])))

        hot = (class_ids[:, None] == my_ids[None, :]).astype(B16)
        cond = jnp.dot(hot, class_table, preferred_element_type=F32).reshape(NC, -1)
        tiny = [spread(hidden_bias)[None], spread(qv_bias), spread(q_gain)[None]]
        tiny = jnp.concatenate([pad_lanes(w) for w in tiny], axis=0)
        m1 = jnp.concatenate([jnp.pad(cond, ((0, 8 - NC), (0, 0))), jnp.pad(tiny, ((0, 4), (0, 0)))], axis=0)
        badd = jnp.concatenate([b_ada, projection_bias], axis=0).astype(F32).reshape(1, -1)
        extra = {"m1": m1, "wada": jnp.moveaxis(w_ada, 1, 0), "badd": badd}
    else:
        hot = (class_ids[:, None] == my_ids[None, :]).astype(B16)
        cond = lax.psum(jnp.dot(hot, class_table, preferred_element_type=F32), "dp")
        silu, silu_back = jax.vjp(jax.nn.silu, cond)
        silu_low = silu.astype(B16)
        parts = jnp.einsum("sc,cjd->sjd", silu_low, w_ada, preferred_element_type=F32)
        parts = parts.reshape((NC, T) + parts.shape[1:])
        mine = lax.psum_scatter(parts, "tensor", scatter_dimension=1, tiled=True)[:, 0] + b_ada.astype(F32)
        spread = lax.all_to_all(jnp.repeat(mine, 2, axis=0), "dp", 0, 0, tiled=True)
        modulation = jnp.moveaxis(spread, 0, 1).reshape(6, width)

        pieces = [qv_bias, q_gain, hidden_bias, projection_bias]
        flat = jnp.concatenate([p.reshape(-1) for p in pieces])
        everyone = lax.all_gather(lax.all_gather(flat, "tensor"), "dp")
        cut, at = [], 0
        for p in pieces:
            cut.append(everyone[:, :, at : at + p.size].reshape((dp, T) + p.shape).astype(F32))
            at += p.size
        qv_all = cut[0].transpose(2, 1, 3, 0, 4).reshape(2, T, 2, hq)[:, :, core]
        gain_all = cut[1].transpose(1, 2, 0, 3).reshape(T, 2, hq)[:, core]
        hidden_all = cut[2].transpose(1, 2, 0, 3).reshape(T, 2, fu)[:, core]
        out_bias = cut[3][:, 0].transpose(1, 0, 2).reshape(2, width)
        mods = jnp.concatenate([modulation, out_bias], axis=0)
        hp = jnp.stack([qv_all[0], qv_all[1], gain_all, 1.0 / gain_all], axis=1)
        hp = jnp.concatenate([hp, jnp.zeros_like(hp)], axis=1)
        hb = jnp.broadcast_to(hidden_all[:, None], (T, 8, fu))

        extra = {"mods": mods, "hp": hp, "hb": hb}

    weights = {"wqkv": query_key_value_weight, "wup": up_weight, "wproj": output_projection, "wdown": down_weight}
    pad = ((0, 0), (0, rows - quarter), (0, 0))
    xb = jnp.pad(block_input.astype(B16), pad)
    dyb = jnp.pad(cotangent.astype(B16), pad)

    got = block_call(dm, weights, xb, dyb, sid, extra)
    outd, gind = got["outd"], got["gind"]

    outermost = Layout(major_to_minor=(0, 1, 2))

    def added(base, step):
        step = with_layout_constraint(jnp.swapaxes(step, 0, 1), outermost)
        out = with_layout_constraint(jnp.swapaxes(base, 0, 1) + step[:quarter].astype(F32), outermost)
        return jnp.swapaxes(out, 0, 1)

    block_output, input_grad = added(block_input, outd), added(cotangent, gind)

    w_qkv_grad, w_proj_grad, w_fc1_grad, w_fc2_grad = (got[name] for name in ("g_qkv", "g_proj", "g_up", "g_down"))

    if dm.inside:
        cond = got["cond"][:NC].reshape(total, -1)
        silu, silu_back = jax.vjp(jax.nn.silu, cond)
        dmod = jnp.swapaxes(got["dmodf"][:, :NC], 0, 1).reshape(total, 8, R)[:, :6].astype(B16)
        b_ada_grad = jnp.sum(dmod.astype(F32), axis=0)
        w_ada_grad = jnp.einsum("sc,sjd->cjd", silu.astype(B16), dmod, preferred_element_type=F32)
        (d_cond,) = silu_back(got["dsil"][:NC].reshape(total, -1))
        pk = got["pk"]

        def own(w, n):
            return lax.dynamic_slice_in_dim(w, di * n, n, w.ndim - 1)

        heads = own(jnp.swapaxes(pk[:, :3, :hq], 0, 1).reshape(3, -1, head), head // dp)
        qv_bias_grad, q_gain_grad = heads[:2], heads[2]
        b_fc1_grad = own(pk[:, 0, hq : hq + fu].reshape(hidden_bias.shape[0], -1), hidden_bias.shape[1])
        b_out_grad = own(pk[0, 6:8, hq + fu :], R)
    else:
        sums, hsum, fsum = got["sums"], got["hsum"], got["fsum"]
        dmod = sums[:6].reshape(6, dp, R).astype(B16)
        dmod = lax.all_to_all(jnp.moveaxis(dmod, 1, 0), "dp", 0, 0, tiled=True)
        dmod = lax.all_gather(dmod[::2], "tensor", axis=1)
        dmod = dmod.reshape((total, 6, R))
        b_ada_grad = jnp.sum(dmod.astype(F32), axis=0)
        w_ada_grad = jnp.einsum("sc,sjd->cjd", silu_low, dmod, preferred_element_type=F32)
        d_silu = lax.psum(jnp.einsum("sjd,cjd->sc", dmod, w_ada, preferred_element_type=F32), "dp")
        (d_cond,) = silu_back(d_silu)

        vec = jnp.concatenate([hsum[:, :3].reshape(-1), fsum[:, 0].reshape(-1), sums[6:].reshape(-1) * 0.5])
        nh, nf = T * 3 * hq, T * fu
        place_ = jnp.arange(2, dtype=jnp.int32) == core
        by_core = jnp.where(place_[:, None], vec[None, : nh + nf], 0.0).reshape(-1)
        vec = lax.psum(jnp.concatenate([by_core, vec[nh + nf :]]), ("dp", "tensor"))
        by_core = vec[: 2 * (nh + nf)].reshape(2, nh + nf)
        heads = by_core[:, :nh].reshape(2, T, 3, hq)
        heads = lax.dynamic_index_in_dim(heads, zi, 1, keepdims=False)
        heads = jnp.moveaxis(heads, 0, 1).reshape(3, -1, head)
        step = head // dp
        heads = lax.dynamic_slice_in_dim(heads, di * step, step, 2)
        qv_bias_grad, q_gain_grad = heads[:2], heads[2]
        fc1 = lax.dynamic_index_in_dim(by_core[:, nh:].reshape(2, T, fu), zi, 1, keepdims=False)
        fc1 = fc1.reshape(-1, hidden_bias.shape[1] * dp)
        step = hidden_bias.shape[1]
        b_fc1_grad = lax.dynamic_slice_in_dim(fc1, di * step, step, 1)
        b_out_grad = lax.dynamic_slice_in_dim(vec[2 * (nh + nf) :].reshape(2, width), di * R, R, 1)

    table_grad = jnp.dot(hot.astype(F32).T, d_cond, precision=lax.Precision.HIGHEST, preferred_element_type=F32)

    return (
        block_output, input_grad, table_grad, w_ada_grad, b_ada_grad, w_qkv_grad, qv_bias_grad, q_gain_grad,
        w_proj_grad, w_fc1_grad, b_fc1_grad, w_fc2_grad, b_out_grad,
    )


def solution(mesh):
    dp, tensor = mesh.shape["dp"], mesh.shape["tensor"]
    return jax.shard_map(
        functools.partial(local, dp, tensor),
        mesh=mesh,
        in_specs=(
            P("dp", "tensor", None),
            P("dp", "tensor", None),
            P(),
            P("dp", None),
            P("dp", "tensor"),
            P("tensor", None, "dp"),
            P(None, "dp"),
            P(None, "dp", "tensor"),
            P(None, "tensor", "dp"),
            P("tensor", "dp"),
            P("tensor", "dp"),
            P("dp", "tensor"),
            P("tensor", "dp"),
            P("tensor", "dp"),
            P(None, "dp"),
        ),
        out_specs=(
            P("dp", "tensor", None),
            P("dp", "tensor", None),
            P("dp", "tensor"),
            P("tensor", None, "dp"),
            P(None, "dp"),
            P(None, "dp", "tensor"),
            P(None, "tensor", "dp"),
            P("tensor", "dp"),
            P("tensor", "dp"),
            P("dp", "tensor"),
            P("tensor", "dp"),
            P("tensor", "dp"),
            P(None, "dp"),
        ),
        check_vma=False,
    )
```

```python
import functools

import jax
import jax.numpy as jnp
from jax import lax
from jax.experimental import pallas as pl
from jax.experimental.layout import Layout, with_layout_constraint
from jax.experimental.pallas import tpu as pltpu
from jax.sharding import PartitionSpec as P

MESH = pl.DeviceIdType.MESH
F32, B16 = jnp.float32, jnp.bfloat16
FINS = 2
SLOTS = 3
PUMPS = (1, 0, 0, 0, 1, 1, 4, 0, 3, 2, 4, 5, 2, 1)
BEGIN = ((), ((2, 0),), ((1, 0),), ((2, 1), (1, 1), (0, 0), (0, 1)))
LEAN = 2.0
CHUNK = 256
EPS = 1e-06
FAR = 256.0


def dot(a, b):
    return lax.dot_general(a, b, (((1,), (0,)), ((), ())), preferred_element_type=F32)


def dot_nt(a, b):
    return lax.dot_general(a, b, (((1,), (1,)), ((), ())), preferred_element_type=F32)


def dot_tn(a, b):
    return lax.dot_general(a, b, (((0,), (0,)), ((), ())), preferred_element_type=F32)


def split_dot(a, b):
    high = a.astype(B16)
    low = (a - high.astype(F32)).astype(B16)
    return dot(high, b) + dot(low, b)


def row_sum(a):
    return jnp.sum(a, axis=0, keepdims=True)


class Dims:
    def __init__(self, dp, tensor, rows, width, head, hidden):
        self.T = tensor
        self.NC = dp // 2
        self.bits = self.NC.bit_length() - 1
        self.Q = rows
        self.M = rows * tensor
        self.D = width
        self.hd = head
        self.hq = width // tensor // 2
        self.fu = hidden // tensor // 2
        self.R = width // dp
        self.C = 4 * self.hq + 2 * self.fu
        self.NCH = width // CHUNK
        self.inside = self.R % 128 == 0 and self.NC <= tensor and hidden // tensor <= width
        self.W = self.hq + self.fu + width
        hq, fu, half = self.hq, self.fu, self.fu // 2
        up, down = 4 * hq, 4 * hq + fu
        self.up, self.down, self.half = up, down, half
        self.pieces = ((0, hq), (hq, hq), (2 * hq, hq), (3 * hq, hq), (up, half), (down, half), (up + half, half), (down + half, half))
        self.sums_order = (5, 4, 7, 6, 3, 2, 1, 0)
        assert 1 << self.bits == self.NC


class Refs:
    pass


def block_kernel(dm, names, *refs):
    m = Refs()
    for name, ref in zip(names, refs):
        if name[:2] in ("rb", "rf"):
            setattr(m, name[:2], getattr(m, name[:2], []) + [ref])
        else:
            setattr(m, name, ref)
    T, NC, NB, Q, M, D, R, C = dm.T, dm.NC, dm.bits, dm.Q, dm.M, dm.D, dm.R, dm.C
    hq, fu, NCH, half = dm.hq, dm.fu, dm.NCH, dm.half
    TH = T // 2
    NP = len(dm.pieces)
    wall, xs, dys, h1, h2 = m.wall, m.xs, m.dys, m.h1, m.h2
    mods, hp, hb, sums, hsum, fsum = m.mods, m.hp, m.hb, m.sums, m.hsum, m.fsum
    dpi = lax.axis_index("dp")
    me_z = lax.axis_index("tensor")
    core = lax.rem(dpi, 2)
    chip = dpi // 2
    mybit = [lax.rem(chip // (1 << b), 2) for b in range(NB)]
    partner = (dpi + 1 - 2 * core, me_z)

    def tag_z(dev):
        return dev

    def z_dev(off):
        return (dpi, lax.rem(me_z + off, T))

    def bit_dev(b):
        return (dpi + (1 - 2 * mybit[b]) * (2 << b), me_z)

    def chip_dev(k):
        return (lax.rem(chip + k, NC) * 2 + core, me_z)

    bar = pltpu.get_barrier_semaphore()
    friends = [partner] + [z_dev(k) for k in range(1, T)]
    friends += [chip_dev(k) for k in range(1, NC)] if dm.inside else [bit_dev(b) for b in range(NB)]
    for dev in friends:
        pl.semaphore_signal(bar, inc=1, device_id=dev, device_id_type=MESH)
    pl.semaphore_wait(bar, len(friends))

    def rdma(src, dst, ss, rs, dev):
        return pltpu.make_async_remote_copy(
            src_ref=src, dst_ref=dst, send_sem=ss, recv_sem=rs, device_id=dev, device_id_type=MESH
        )

    every = slice(None)

    def place(fixed):
        return tuple(fixed.get(b, every) for b in reversed(range(NB)))

    mine = place({b: mybit[b] for b in range(NB)})

    def cols(pc):
        return pl.ds(*dm.pieces[pc])

    def core_rows(c):
        return pl.ds(pl.multiple_of(c * R, R), R)

    def lanes_of(start, n):
        return pl.ds(pl.multiple_of(start, 128), n)

    def own_weight(pc, c):
        if pc < 3:
            return m.wqkv.at[pc, :, lanes_of(c * hq, hq)]
        if pc == 3:
            return m.gk.at[0, 128 : 128 + R, lanes_of(c * hq, hq)]
        k = (pc - 4) // 2
        if pc % 2 == 0:
            return m.wup.at[:, lanes_of(c * fu + k * half, half)]
        return m.gk.at[2 * c + k, 0:R, :]

    def transpose_own():
        m.gk[0, 128 : 128 + R, :] = m.wproj[...].T
        for i in range(4):
            m.gk[i, 0:R, :] = m.wdown[i * half : (i + 1) * half, :].T

    def core_copy(pc):
        dst = wall.at[(me_z,) + mine + (core_rows(core), cols(pc))]
        return rdma(own_weight(pc, 1 - core), dst, m.c_s.at[pc], m.c_r.at[pc], partner)

    def core_local(pc):
        dst = wall.at[(me_z,) + mine + (core_rows(core), cols(pc))]
        return pltpu.make_async_copy(own_weight(pc, core), dst, m.c_l.at[pc])

    def z_copy(pc, off):
        part = wall.at[(me_z,) + mine + (every, cols(pc))]
        return rdma(part, part, m.z_s.at[pc, off - 1], m.z_r.at[pc, off - 1], z_dev(off))

    inner = jnp.logical_and(me_z > 0, me_z < T - 1)
    line_sends = ((2, me_z >= 0), (1, me_z < T - 1), (3, me_z > 0))

    def z_landed(pc, off):
        part = wall.at[(lax.rem(me_z - off + T, T),) + mine + (every, cols(pc))]
        rdma(part, part, m.z_s.at[pc, off - 1], m.z_r.at[pc, off - 1], z_dev(off)).wait_recv()

    def z_forward(pc):
        part = wall.at[(lax.rem(me_z + 2, T),) + mine + (every, cols(pc))]
        up = lax.rem(me_z + 1, 2)
        return rdma(part, part, m.z_f.at[pc], m.z_r.at[pc, 2 * up], tag_z((dpi, me_z + 2 * up - 1)))

    order = [list(range(NB)), list(reversed(range(NB)))]

    def half_z(h):
        return pl.ds(h * TH, TH)

    def p_copy(pc, step, h, landing):
        b = order[h][step]
        fixed = {k: mybit[k] for k in order[h][step:]}
        if landing:
            fixed[b] = 1 - mybit[b]
        part = wall.at[(half_z(h),) + place(fixed) + (every, cols(pc))]
        return rdma(part, part, m.p_s.at[pc, step, h], m.p_r.at[pc, step, h], bit_dev(b))

    def gather_stage(pc, s):
        if not 0 <= pc < NP:
            return
        if s == 0:
            core_local(pc).wait()
            other = wall.at[(me_z,) + mine + (core_rows(1 - core), cols(pc))]
            rdma(other, other, m.c_s.at[pc], m.c_r.at[pc], partner).wait_recv()
            for off, allowed in line_sends:
                @pl.when(allowed)
                def _():
                    z_copy(pc, off).start()
            return
        if s == -1:
            @pl.when(inner)
            def _():
                z_landed(pc, 2)
                z_forward(pc).start()
            return
        if s == 1:
            z_landed(pc, 1)
            z_landed(pc, 3)

            @pl.when(jnp.logical_not(inner))
            def _():
                z_landed(pc, 2)
        for h in range(2):
            if s > 1:
                p_copy(pc, s - 2, h, True).wait_recv()
            if s <= NB:
                p_copy(pc, s - 1, h, False).start()

    starts = [(pc - 2.2, pc, 0) for pc in range(NP)] + [(pc - 1.1, pc, -1) for pc in range(NP)]
    starts += [(pc + 1.1 * (s - 1), pc, s) for pc in range(NP) for s in range(1, NB + 1)]
    if NB == 2:
        starts[starts.index((4 + 1.1, 4, 2))] = (4.95, 4, 2)
    starts.sort()

    here = [0]

    def gather_to(key):
        while starts and starts[0][0] <= key:
            gather_stage(*starts.pop(0)[1:])

    def gather_until(pc):
        gather_to(pc + 1.1 * NB)
        while here[0] <= pc:
            gather_stage(here[0], NB + 1)
            here[0] += 1

    def gather_sent(which):
        for pc in which:
            for off, allowed in line_sends:
                @pl.when(allowed)
                def _():
                    z_copy(pc, off).wait_send()

            @pl.when(inner)
            def _():
                z_forward(pc).wait_send()

            for step in range(NB):
                for h in range(2):
                    p_copy(pc, step, h, False).wait_send()

    owner = me_z // 2 == core

    def tok_copy(which, src, dst, i):
        zt = 2 * core + i
        return rdma(src.at[i], dst.at[me_z], m.x_s.at[which, i], m.x_r.at[which, me_z], (dpi, zt))

    def tok_start(which, src, dst):
        for i in range(2):
            @pl.when(2 * core + i != me_z)
            def _():
                tok_copy(which, src, dst, i).start()

            @pl.when(2 * core + i == me_z)
            def _():
                pltpu.make_async_copy(src.at[i], dst.at[me_z], m.x_l.at[which]).start()

    def tok_forward(which, dst):
        return rdma(dst, dst, m.x_f.at[which, 0], m.x_f.at[which, 1], partner)

    def tok_wait(which, src, dst):
        @pl.when(owner)
        def _():
            for off in range(1, T):
                zq = lax.rem(me_z + off, T)
                rdma(dst.at[zq], dst.at[zq], m.x_s.at[which, 0], m.x_r.at[which, zq], (dpi, zq)).wait_recv()
            pltpu.make_async_copy(src.at[0], dst.at[me_z], m.x_l.at[which]).wait()
            tok_forward(which, dst).start()

        @pl.when(jnp.logical_not(owner))
        def _():
            tok_forward(which, dst).wait_recv()

    def tok_sent(which, src, dst):
        for i in range(2):
            @pl.when(2 * core + i != me_z)
            def _():
                tok_copy(which, src, dst, i).wait_send()

        @pl.when(owner)
        def _():
            tok_forward(which, dst).wait_send()

    back_from = (m.n2, m.ab)

    def back_copy(which, dst, zq):
        i = lax.rem(me_z, 2)
        return rdma(back_from[which].at[zq], dst.at[i], m.o_s.at[which, zq], m.o_r.at[which, i], (dpi, zq))

    def back_start(which, dst):
        @pl.when(owner)
        def _():
            for off in range(1, T):
                back_copy(which, dst, lax.rem(me_z + off, T)).start()
            pltpu.make_async_copy(back_from[which].at[me_z], dst.at[lax.rem(me_z, 2)], m.o_l.at[which]).start()

    def back_wait(which, dst):
        @pl.when(owner)
        def _():
            for off in range(1, T):
                back_copy(which, dst, lax.rem(me_z + off, T)).wait_send()
            pltpu.make_async_copy(back_from[which].at[me_z], dst.at[lax.rem(me_z, 2)], m.o_l.at[which]).wait()

        for i in range(2):
            @pl.when(2 * core + i != me_z)
            def _():
                rdma(dst.at[i], dst.at[i], m.o_s.at[which, 0], m.o_r.at[which, i], (dpi, 2 * core + i)).wait_recv()

    def sender(k):
        return m.duk if k == 2 and m.duk.shape == m.send.shape else m.send

    def x_copy(k, n):
        return rdma(sender(k).at[n], m.recv.at[k % 2, n], m.e_s.at[k, n], m.e_r.at[k, n], partner)

    def exchange(k, n, value):
        sender(k)[n] = value.astype(B16)
        x_copy(k, n).start()

    def exchange_wait(k):
        for n in range(NCH):
            x_copy(k, n).wait_recv()

    def exchange_sent(k):
        for n in range(NCH):
            x_copy(k, n).wait_send()

    def both(k, t):
        rows = pl.ds(pl.multiple_of(t * Q, 16), Q)
        parts = [sender(k)[n, rows, :].astype(F32) + m.recv[k % 2, n, rows, :].astype(F32) for n in range(NCH)]
        return jnp.concatenate(parts, axis=-1)

    def wz(z, lo, n):
        return wall[(z,) + (every,) * NB + (every, pl.ds(lo, n))].reshape(D, n)

    def wrows(z, n, lo, width):
        per = CHUNK // (2 * R)
        low = per.bit_length() - 1
        top = n * per
        fixed = {b: (top >> b) & 1 for b in range(low, NB)}
        return wall[(z,) + place(fixed) + (every, pl.ds(lo, width))].reshape(CHUNK, width)

    def wrows_all(n, lo, width):
        return jnp.concatenate([wrows(z, n, lo, width) for z in range(T)], axis=-1)

    def wstore(z, lo, n, value):
        wall[(z,) + (every,) * NB + (every, pl.ds(lo, n))] = value.astype(B16).reshape(
            (2,) * NB + (2 * R, n)
        )

    def all_z(ref):
        return jnp.concatenate([ref[z] for z in range(T)], axis=-1)

    def whole(ref):
        return ref[...].reshape(M, D)

    def mod(r):
        return mods[r : r + 1, :]

    def transpose_into(dst, ref):
        for n in range(D // 128):
            block = ref[:, :, n * 128 : (n + 1) * 128].reshape(M, 128)
            dst[n * 128 : (n + 1) * 128, :] = block.T

    place_of = {pc: j for j, pc in enumerate(dm.sums_order)}

    def rs_fixed(step, h, away):
        order_r = order[h][::-1]
        fixed = {k: mybit[k] for k in order_r[: step + 1]}
        b = order_r[step]
        if away:
            fixed[b] = 1 - mybit[b]
        return b, fixed

    FIRST = 1 if dm.inside else 0

    def rf_copy(step, h):
        lo, width = dm.pieces[dm.sums_order[0]]
        b, fixed = rs_fixed(step, h, True)
        part = wall.at[(me_z,) + place(fixed) + (every, pl.ds(lo + h * (width // 2), width // 2))]
        return rdma(part, m.rf[step].at[h], m.rs_s.at[0, step, h], m.rs_r.at[0, step, h], bit_dev(b))

    def rf_add(step, h):
        rf_copy(step, h).wait_recv()
        lo, width = dm.pieces[dm.sums_order[0]]
        b, fixed = rs_fixed(step, h, False)
        where = (me_z,) + place(fixed) + (every, pl.ds(lo + h * (width // 2), width // 2))
        wall[where] = (wall[where].astype(F32) + m.rf[step][h].astype(F32)).astype(B16)

    def rs_copy(j, step, h):
        pc = dm.sums_order[j]
        b, fixed = rs_fixed(step, h, True)
        part = wall.at[(half_z(h),) + place(fixed) + (every, cols(pc))]
        buf = m.rb[step].at[((j - FIRST) % SLOTS, h) + (every,) * (NB - step) + (every, pl.ds(0, dm.pieces[pc][1]))]
        return rdma(part, buf, m.rs_s.at[j, step, h], m.rs_r.at[j, step, h], bit_dev(b))

    def rs_start(j, step, h):
        if j - FIRST >= SLOTS:
            pl.semaphore_wait(m.free.at[step, h], 1)
        rs_copy(j, step, h).start()

    def rs_add(j, step, h):
        pc = dm.sums_order[j]
        rs_copy(j, step, h).wait_recv()
        b, fixed = rs_fixed(step, h, False)
        rest = [k for k in reversed(range(NB)) if k not in fixed]
        slot, width = (j - FIRST) % SLOTS, dm.pieces[pc][1]

        def one(i, carry):
            zz, r = i // (1 << len(rest)), lax.rem(i, 1 << len(rest))
            at = dict(fixed)
            inner = ()
            for pos, k in enumerate(rest):
                v = lax.rem(r // (1 << (len(rest) - 1 - pos)), 2)
                at[k] = v
                inner += (v,)
            where = (h * TH + zz,) + place(at) + (every, cols(pc))
            got = m.rb[step][(slot, h, zz) + inner + (every, pl.ds(0, width))]
            wall[where] = (wall[where].astype(F32) + got.astype(F32)).astype(B16)
            return carry

        lax.fori_loop(0, TH << len(rest), one, 0)
        if j + SLOTS < NP:
            pl.semaphore_signal(m.free.at[step, h], inc=1, device_id=bit_dev(b), device_id_type=MESH)

    def rz_blocks(j):
        pc = dm.sums_order[j]
        if j >= FIRST:
            return [(mine, cols(pc))]
        width = dm.pieces[pc][1]
        return [(place({b: (p >> b) & 1 for b in range(NB)}), pl.ds(p * width, width)) for p in range(NC)]

    ends_here = jnp.logical_not(inner)

    def rz_copies(j, off):
        pc, out = dm.sums_order[j], []
        for i, (chip_at, at) in enumerate(rz_blocks(j)):
            part = wall.at[(lax.rem(me_z + off, T),) + chip_at + (every, cols(pc))]
            sems = m.rz_s.at[j, off - 1, i], m.rz_r.at[j, off - 1, i]
            out.append(rdma(part, m.zb.at[off - 1, :, at], *sems, z_dev(off)))
        return out

    def rz_specials(j):
        pc, out = dm.sums_order[j], []
        dev = tag_z((dpi, jnp.where(me_z == 0, 1, T - 2)))
        for i, (chip_at, at) in enumerate(rz_blocks(j)):
            part = wall.at[(T - 1 - me_z,) + chip_at + (every, cols(pc))]
            out.append(rdma(part, m.zx.at[:, at], m.rx_s.at[j, i], m.rx_r.at[j, i], dev))
        return out

    def each(copies, do):
        for copy in copies:
            getattr(copy, do)()

    def rz_begin(j):
        if j == FIRST and FIRST:
            pl.semaphore_wait(m.zfree, T - 1)

        @pl.when(ends_here)
        def _():
            each(rz_specials(j), "start")
            each(rz_copies(j, 2), "start")

        for off, allowed in line_sends[1:]:
            @pl.when(allowed)
            def _():
                each(rz_copies(j, off), "start")

    def rz_middle(j):
        pc = dm.sums_order[j]

        @pl.when(inner)
        def _():
            each(rz_specials(j), "wait_recv")
            for chip_at, at in rz_blocks(j):
                where = (lax.rem(me_z + 2, T),) + chip_at + (every, cols(pc))
                wall[where] = (wall[where].astype(F32) + m.zx[:, at].astype(F32)).astype(B16)
            each(rz_copies(j, 2), "start")

    def rz_wait(j):
        each(rz_copies(j, 2), "wait_recv")
        for off, came in ((1, me_z > 0), (3, me_z < T - 1)):
            @pl.when(came)
            def _():
                each(rz_copies(j, off), "wait_recv")

    def rz_sent(j):
        each(rz_copies(j, 2), "wait_send")
        for off, allowed in line_sends[1:]:
            @pl.when(allowed)
            def _():
                each(rz_copies(j, off), "wait_send")

        @pl.when(ends_here)
        def _():
            each(rz_specials(j), "wait_send")

    def final(pc, c):
        if pc < 3:
            return m.g_qkv, (pc, every, lanes_of(c * hq, hq))
        if pc == 3:
            return m.g_proj, (pl.ds(pl.multiple_of(c * hq, hq), hq), every)
        at = c * fu + (pc - 4) // 2 * half
        if pc % 2 == 0:
            return m.g_up, (every, lanes_of(at, half))
        return m.g_down, (pl.ds(pl.multiple_of(at, half), half), every)

    def turned(pc):
        return pc in (3, 5, 7)

    def fin_from(j):
        pc = dm.sums_order[j]
        width = dm.pieces[pc][1]
        if turned(pc):
            return m.fturn, (j // 2 % 2, pl.ds(0, width))
        return m.fbuf, (j % FINS, every, pl.ds(0, width))

    def fin_copy(j):
        pc = dm.sums_order[j]
        ref, at = fin_from(j)
        out, place_ = final(pc, core)
        return rdma(ref.at[at], out.at[place_], m.f_s.at[j], m.f_r.at[j], partner)

    def rz_sum(j, chip_at, at, rows):
        acc = wall[(me_z,) + chip_at + (rows, cols(dm.sums_order[j]))].astype(F32)
        for off in range(1, T):
            acc = acc + m.zb[off - 1, rows, at].astype(F32)
        return acc

    def finish(j, total):
        pc = dm.sums_order[j]
        if j >= FINS:
            fin_copy(j - FINS).wait_send()
        ref, at = fin_from(j)
        out, place_ = final(pc, core)
        away, kept = total(core_rows(1 - core)), total(core_rows(core))
        ref[at] = away.T if turned(pc) else away
        fin_copy(j).start()
        out[place_] = kept.T if turned(pc) else kept

    def rs_event(j, s):
        pc = dm.sums_order[j]
        if j < FIRST:
            if s == 1:
                rz_middle(j)
            elif s == 2:
                rz_wait(j)
                for chip_at, at in rz_blocks(j):
                    wall[(me_z,) + chip_at + (every, cols(pc))] = rz_sum(j, chip_at, at, every).astype(B16)
                for off in range(1, T):
                    pl.semaphore_signal(m.zfree, inc=1, device_id=z_dev(off), device_id_type=MESH)
            if s > 2:
                for h in range(2):
                    rf_add(s - 3, h)
            if 2 <= s < NB + 2:
                for h in range(2):
                    rf_copy(s - 2, h).start()
            if s == NB + 2:
                finish(j, lambda rows: wall[(me_z,) + mine + (rows, cols(pc))].astype(F32))
            return
        if s <= NB:
            for h in range(2):
                rs_add(j, s - 1, h)
                if s < NB:
                    rs_start(j, s, h)
            if s == NB:
                rz_begin(j)
            return
        if s == NB + 1:
            rz_middle(j)
            return
        rz_wait(j)
        finish(j, lambda rows: rz_sum(j, mine, cols(pc), rows))

    events = sorted(((j, s) for j in range(NP) for s in range(1, NB + 3)), key=lambda e: (e[0] + LEAN * e[1], e[0]))
    begun = set()

    def pump(count):
        while count and events and (events[0][0], 1) in begun:
            rs_event(*events.pop(0))
            count -= 1

    stops = list(PUMPS)

    def stop():
        pump(stops.pop(0) if stops else 0)

    def rs_begin(pc, h):
        j = place_of[pc]
        while j - SLOTS >= FIRST and (j - SLOTS, 1) in events:
            pump(1)
        if j >= FIRST:
            rs_start(j, 0, h)
        elif h == 1:
            rz_begin(j)
        begun.add((j, h))

    def rs_end():
        for j in range(NP):
            for step in range(NB):
                for h in range(2):
                    (rs_copy(j, step, h) if j >= FIRST else rf_copy(step, h)).wait_send()
            rz_sent(j)
            fin_copy(j).wait_recv()
            if j + FINS >= NP:
                fin_copy(j).wait_send()

    def small(src, dst, k, dev):
        return rdma(src, dst, m.s_s.at[k], m.s_r.at[k], dev)

    def sum_step(acc, got, i, base, sign, rows=None):
        dev = partner if i < sign else bit_dev(i - sign)
        n = acc.shape[1] if rows is None else rows
        return small(acc.at[i, pl.ds(0, n)], got.at[i, pl.ds(0, n)], base + i, dev)

    def sum_finish(acc, got, i, base, sign, rows=None):
        sum_step(acc, got, i, base, sign, rows).wait_recv()
        n = acc.shape[1] if rows is None else rows
        acc[i + 1, 0:n] = acc[i, 0:n] + got[i, 0:n]

    S_SID = 0
    S_M1 = 1
    S_M2 = S_M1 + NB + 1
    S_SM = S_M2 + T - 1
    S_M3 = S_SM + T - 1
    S_M4 = S_M3 + NC - 1
    S_B1 = S_M4 + 1
    S_B2 = S_B1 + NC - 1
    S_B3 = S_B2 + T - 1
    S_PZ = S_B3 + NB + 1
    S_PB = S_PZ + T - 1
    S_PC = S_PB + NB

    sid_copy = small(m.sid, m.sidr, S_SID, partner)
    sid_copy.start()
    if dm.inside:
        m.macc[0] = m.m1[...]
        sum_step(m.macc, m.mrec, 0, S_M1, 1).start()
    for pc in (0, 1, 2, 4, 6):
        core_copy(pc).start()
        core_local(pc).start()
    gather_to(-1.0)
    transpose_own()
    for pc in (3, 5, 7):
        core_copy(pc).start()
        core_local(pc).start()
    for z, slot in ((0, 0), (T - 1, T - 2)):
        @pl.when(me_z == z)
        def _():
            m.zb[slot] = jnp.zeros(m.zb.shape[1:], B16)

    sums[...] = jnp.zeros_like(sums)
    hsum[...] = jnp.zeros_like(hsum)
    fsum[...] = jnp.zeros_like(fsum)

    if dm.inside:
        for i in range(NB + 1):
            sum_finish(m.macc, m.mrec, i, S_M1, 1)
            if i < NB:
                sum_step(m.macc, m.mrec, i + 1, S_M1, 1).start()
        m.sm[me_z] = m.macc[NB + 1, 8:16, :]
        for off in range(1, T):
            small(m.sm.at[me_z], m.sm.at[me_z], S_SM + off - 1, z_dev(off)).start()
        width = D // T
        for zz in range(T):
            c = m.macc[NB + 1, 0:8, zz * width : (zz + 1) * width]
            m.cond[8 * zz : 8 * zz + 8, :] = c
            low = (c / (1.0 + jnp.exp(-c))).astype(B16)
            rows = [dot(low, m.wada[j]) for j in range(6)] + [jnp.zeros((8, 2 * R), F32)]
            m.m2s[zz] = jnp.concatenate(rows, axis=-1)
        for off in range(1, T):
            small(m.m2s.at[lax.rem(me_z + off, T)], m.m2r.at[off - 1], S_M2 + off - 1, z_dev(off)).start()

    gather_to(1.85)
    tok_start(0, m.xb, xs)

    if dm.inside:
        for off in range(1, T):
            small(m.m2s.at[0], m.m2r.at[off - 1], S_M2 + off - 1, z_dev(off)).wait_recv()
        m.m3c[core, chip] = m.m2s[me_z] + sum(m.m2r[k] for k in range(T - 1)) + m.badd[...]
        own = m.m3c.at[core, chip]
        for k in range(1, NC):
            small(own, own, S_M3 + k - 1, chip_dev(k)).start()
        gather_to(2.15)
        for off in range(1, T):
            got = m.sm.at[lax.rem(me_z - off + T, T)]
            small(got, got, S_SM + off - 1, z_dev(off)).wait_recv()
        head_cols = pl.ds(pl.multiple_of(core * hq, hq), hq)
        for z in range(T):
            for r in range(3):
                hp[z, r : r + 1, :] = m.sm[z, r + 1 : r + 2, head_cols]
            hp[z, 3:4, :] = 1.0 / hp[z, 2:3, :]
            hb[z, 0:1, :] = m.sm[z, 0:1, pl.ds(pl.multiple_of(core * fu, fu), fu)]
        for k in range(1, NC):
            got = m.m3c.at[core, lax.rem(chip - k + NC, NC)]
            small(got, got, S_M3 + k - 1, chip_dev(k)).wait_recv()
        small(m.m3c.at[core], m.m3c.at[core], S_M4, partner).start()

    got = small(m.sidr, m.sidr, S_SID, partner)
    got.wait_recv()
    pick = lax.rem(me_z, 2)
    ids = jnp.where(owner, m.sid[pl.ds(pick, 1), :], m.sidr[pl.ds(pick, 1), :])
    lanes = lax.broadcasted_iota(jnp.int32, (128, 1), 0).astype(F32)
    m.psi[...] = jnp.where(lanes > ids, FAR, 0.0).astype(B16).T
    m.phi[...] = jnp.where(lanes == ids, -1.0, 0.0).astype(B16).T

    if dm.inside:
        got = m.m3c.at[1 - core]
        small(got, got, S_M4, partner).wait_recv()
        for c in range(2):
            for p in range(NC):
                row = m.m3c[c, p, pl.ds(chip, 1), :]
                d = 2 * p + c
                for j in range(8):
                    mods[j : j + 1, d * R : (d + 1) * R] = row[:, j * R : (j + 1) * R]

    gather_to(4.1)
    tok_wait(0, m.xb, xs)

    def ln(rows):
        centred = rows - jnp.mean(rows, axis=-1, keepdims=True)
        inv = lax.rsqrt(jnp.mean(centred * centred, axis=-1, keepdims=True) + EPS)
        return centred * inv, inv

    def first_norm(t, carry):
        normed, _ = ln(xs[t].astype(F32))
        h1[t] = (normed * (1.0 + mod(2)) + mod(4)).astype(B16)
        return carry

    lax.fori_loop(0, T, first_norm, 0)
    gather_to(4.96)
    if dm.inside:
        for i in range(NB + 1):
            sum_step(m.macc, m.mrec, i, S_M1, 1).wait_send()
    gather_until(2)

    lane = lax.broadcasted_iota(jnp.int32, (1, hq), 1)
    halves = [(lane // dm.hd) == k for k in range(hq // dm.hd)]
    bi = lax.broadcasted_iota(jnp.int32, (hq, hq), 0) // dm.hd
    bj = lax.broadcasted_iota(jnp.int32, (hq, hq), 1) // dm.hd
    same_head = (bi == bj).astype(B16)

    def qkv(z, carry):
        t = dot(whole(h1), wz(z, 0, 3 * hq))
        q = t[:, :hq] + hp[z, 0:1, :]
        k = t[:, hq : 2 * hq]
        v = t[:, 2 * hq :] + hp[z, 1:2, :]
        qi = lax.rsqrt(split_dot(q * q, same_head) + EPS)
        ki = lax.rsqrt(split_dot(k * k, same_head) + EPS)
        m.qs[z] = (q * qi * hp[z, 2:3, :]).astype(B16)
        m.ks[z] = (k * ki).astype(B16)
        m.vs[z] = v.astype(B16)
        m.rq[z] = qi.astype(B16)
        m.rk[z] = ki.astype(B16)
        return carry

    lax.fori_loop(0, T, qkv, 0)
    zero16 = jnp.zeros((), B16)

    def expo(z, k, q_all, k_all, rows=slice(None)):
        q_one = jnp.where(halves[k], q_all[rows], zero16)
        left = jnp.concatenate([q_one, m.psi[rows, :]], axis=1)
        right = jnp.concatenate([k_all, m.phi[...]], axis=1)
        return q_one, jnp.exp(dot_nt(left, right))

    def attend(z, carry):
        q_all, k_all, v_all = m.qs[z], m.ks[z], m.vs[z]
        v_ones = jnp.concatenate([v_all, jnp.ones((M, hq), B16)], axis=1)
        mixed = inverse = None
        for k in range(hq // dm.hd):
            _, e = expo(z, k, q_all, k_all)
            both_ = dot(e.astype(B16), v_ones)
            inv = 1.0 / both_[:, hq:]
            one = both_[:, :hq] * inv
            mixed = one if mixed is None else jnp.where(halves[k], one, mixed)
            inverse = inv if inverse is None else jnp.where(halves[k], inv, inverse)
        m.o[z] = mixed.astype(B16)
        m.ol[z] = (mixed - mixed.astype(B16).astype(F32)).astype(B16)
        m.do[z] = inverse.astype(B16)
        return carry

    gather_to(5.0)
    for z in range(T):
        lax.fori_loop(z, z + 1, attend, 0)
        if z == 1:
            gather_to(5.9)
            tok_start(1, m.dyb, dys)

    gather_until(3)
    o_all = all_z(m.o)
    for n in range(NCH):
        exchange(0, n, dot_nt(o_all, wrows_all(n, 3 * hq, hq)))
    exchange_wait(0)

    def second_norm(t, carry):
        a = both(0, t) + mod(6)
        m.ab[t] = a.astype(B16)
        normed, inv = ln(xs[t].astype(F32) + mod(0) * a)
        h2[t] = (normed * (1.0 + mod(3)) + mod(5)).astype(B16)
        m.n2[t] = normed.astype(B16)
        m.r2[t] = jnp.broadcast_to(inv, (Q, 128))
        return carry

    lax.fori_loop(0, T, second_norm, 0)
    gather_to(7.05)
    exchange_sent(0)
    transpose_into(m.xt, h2)

    def out_grad(t, carry):
        d = (mod(1) * dys[t].astype(F32)).astype(B16)
        m.df[t] = d
        sums[7:8, :] += row_sum(d.astype(F32))
        return carry

    root = 0.7978845608028654

    def hidden(k):
        lo_u, lo_d = dm.up + k * half, dm.down + k * half

        def up(z, carry):
            u = dot(whole(h2), wz(z, lo_u, half)) + hb[z, 0:1, k * half : (k + 1) * half]
            uu = u * u
            th = jnp.tanh(root * u * (1.0 + 0.044715 * uu))
            m.gk[z] = (0.5 * u * (1.0 + th)).astype(B16)
            m.duk[z] = (0.5 * (1.0 + th) + (0.5 * root) * u * (1.0 - th * th) * (1.0 + 0.134145 * uu)).astype(B16)
            return carry

        def down(z, carry):
            dg = dot(whole(m.df), wz(z, lo_d, half))
            du = (dg * m.duk[z].astype(F32)).astype(B16)
            m.duk[z] = du
            fsum[z, 0:1, k * half : (k + 1) * half] = row_sum(du.astype(F32))
            return carry

        gather_until(4 + 2 * k)
        lax.fori_loop(0, T, up, 0)
        if k == 0:
            gather_to(7.15)
            tok_wait(1, m.dyb, dys)
            lax.fori_loop(0, T, out_grad, 0)
            transpose_into(m.xt2, m.df)
        gather_until(5 + 2 * k)
        lax.fori_loop(0, T, down, 0)

    def grads(k, begin):
        lo_u, lo_d = dm.up + k * half, dm.down + k * half

        def down_grad(z, carry):
            wstore(z, lo_d, half, dot(m.xt2[...], m.gk[z]))
            return carry

        def up_grad(z, carry):
            wstore(z, lo_u, half, dot(m.xt[...], m.duk[z]))
            return carry

        for pc, body in ((5 + 2 * k, down_grad), (4 + 2 * k, up_grad)):
            for h in range(2):
                lax.fori_loop(h * TH, (h + 1) * TH, body, 0)
                if pc in begin:
                    rs_begin(pc, h)

    for pc in range(NP):
        core_copy(pc).wait_send()
    hidden(0)
    du_all, g_all = all_z(m.duk), all_z(m.gk)
    for n in range(NCH):
        m.dacc[n] = dot_nt(du_all, wrows_all(n, dm.up, half))
        m.facc[n] = dot_nt(g_all, wrows_all(n, dm.down, half))
    gather_sent((4, 5))
    gather_to(99.0)
    grads(0, (5, 4))
    hidden(1)
    du_all, g_all = all_z(m.duk), all_z(m.gk)
    for n in range(NCH):
        exchange(1, n, m.dacc[n] + dot_nt(du_all, wrows_all(n, dm.up + half, half)))
    for n in range(NCH):
        m.facc[n] = m.facc[n] + dot_nt(g_all, wrows_all(n, dm.down + half, half))
    gather_sent((0, 1, 2, 3, 6, 7))
    grads(1, (7,))
    stop()
    transpose_into(m.xt, h1)
    tok_sent(1, m.dyb, dys)
    exchange_wait(1)
    if sender(2) is not m.send:
        for n in range(NCH):
            exchange(2, n, m.facc[n])

    def ln_back(e, normed, inv):
        return (e - jnp.mean(e, axis=-1, keepdims=True) - normed * jnp.mean(e * normed, axis=-1, keepdims=True)) * inv

    def mid_back(t, carry):
        dh = both(1, t)
        normed = m.n2[t].astype(F32)
        sums[3:4, :] += row_sum(dh * normed)
        sums[5:6, :] += row_sum(dh)
        step_back = ln_back(dh * (1.0 + mod(3)), normed, m.r2[t, :, 0:1])
        h2[t] = step_back.astype(B16)
        dx1 = dys[t].astype(F32) + step_back
        sums[0:1, :] += row_sum(dx1 * m.ab[t].astype(F32))
        da = (mod(0) * dx1).astype(B16)
        m.df[t] = da
        sums[6:7, :] += row_sum(da.astype(F32))
        return carry

    lax.fori_loop(0, T, mid_back, 0)
    pl.semaphore_signal(m.took, inc=1, device_id=partner, device_id_type=MESH)
    stop()
    for h in range(2):
        rs_begin(6, h)
    exchange_sent(1)
    if sender(2) is m.send:
        for n in range(NCH):
            exchange(2, n, m.facc[n])

    def last(t, carry):
        f = both(2, t) + mod(7)
        m.n2[t] = (mod(0) * m.ab[t].astype(F32) + mod(1) * f).astype(B16)
        sums[1:2, :] += row_sum(dys[t].astype(F32) * f)
        return carry

    exchange_wait(2)
    lax.fori_loop(0, T, last, 0)
    exchange_sent(2)
    back_start(0, m.outd)

    w_proj = jnp.concatenate([wz(z, 3 * hq, hq) for z in range(T)], axis=-1)
    do_all = dot(whole(m.df), w_proj).astype(B16)
    for z in range(T):
        m.do[z] = (do_all[:, z * hq : (z + 1) * hq].astype(F32) * m.do[z].astype(F32)).astype(B16)
    transpose_into(m.xt2, m.df)
    dw = dot(m.xt2[...], all_z(m.o))
    for z in range(T):
        wstore(z, 3 * hq, hq, dw[:, z * hq : (z + 1) * hq])
    for h in range(2):
        rs_begin(3, h)
    stop()

    ends = jnp.where(lane < 2, -1.0, 0.0).astype(B16)

    def attend_back(z, carry):
        q_all, k_all, v_all = m.qs[z], m.ks[z], m.vs[z]
        dob = m.do[z]
        prod = dob.astype(F32) * (m.o[z].astype(F32) + m.ol[z].astype(F32))
        v_ends = jnp.concatenate([v_all, jnp.broadcast_to(ends, (M, hq))], axis=1)
        dq = dk = dv = 0.0
        for k in range(hq // dm.hd):
            to_all = (bi == k).astype(B16)
            total = split_dot(prod, to_all)
            high = total.astype(B16)
            low = (total - high.astype(F32)).astype(B16)
            extra = jnp.where(lane == 0, high, jnp.where(lane == 1, low, zero16))
            d_one = jnp.where(halves[k], dob, zero16)
            d_ext = jnp.concatenate([d_one, extra], axis=1)
            k_one = jnp.where(halves[k], k_all, zero16)
            dq_rows = []
            for rows in (slice(0, 256), slice(256, M)):
                q_one, e = expo(z, k, q_all, k_all, rows)
                dp = dot_nt(d_ext[rows], v_ends)
                ds = (e * dp).astype(B16)
                dq_rows.append(dot(ds, k_one))
                dk = dk + dot_tn(ds, q_one)
                dv = dv + dot_tn(e.astype(B16), d_one[rows])
            dq = dq + jnp.concatenate(dq_rows, axis=0)
        gain = hp[z, 2:3, :]
        q_hat = q_all.astype(F32) * hp[z, 3:4, :]
        k_hat = k_all.astype(F32)
        hsum[z, 2:3, :] = row_sum(dq * q_hat)
        eq = dq * gain
        dq = ((eq - q_hat * split_dot(eq * q_hat, same_head)) * m.rq[z].astype(F32)).astype(B16)
        dk = ((dk - k_hat * split_dot(dk * k_hat, same_head)) * m.rk[z].astype(F32)).astype(B16)
        dv = dv.astype(B16)
        hsum[z, 0:1, :] = row_sum(dq.astype(F32))
        hsum[z, 1:2, :] = row_sum(dv.astype(F32))
        m.dqkv[...] = jnp.concatenate([dq, dk, dv], axis=1)
        return carry

    for z in range(T):
        lax.fori_loop(z, z + 1, attend_back, 0)
        if z == T - 1:
            pl.semaphore_wait(m.took, 1)
        d_one_z = m.dqkv[...]
        for n in range(NCH):
            part = dot_nt(d_one_z, wrows(z, n, 0, 3 * hq))
            if z == T - 1:
                exchange(3, n, m.facc[n] + part)
            else:
                m.facc[n] = part if z == 0 else m.facc[n] + part
        wstore(z, 0, 3 * hq, dot(m.xt[...], d_one_z))
        for pc, h in BEGIN[z]:
            rs_begin(pc, h)
        stop()

    if dm.inside:
        for z in range(T):
            m.pks[z] = jnp.concatenate([hsum[z], fsum[z], sums[...]], axis=-1)
        for off in range(1, T):
            small(m.pks.at[lax.rem(me_z + off, T)], m.pkr.at[off - 1], S_PZ + off - 1, z_dev(off)).start()
    exchange_wait(3)

    def first_back(t, carry):
        dh = both(3, t)
        normed, inv = ln(xs[t].astype(F32))
        sums[2:3, :] += row_sum(dh * normed)
        sums[4:5, :] += row_sum(dh)
        m.ab[t] = (h2[t].astype(F32) + ln_back(dh * (1.0 + mod(2)), normed, inv)).astype(B16)
        return carry

    for t in range(T):
        lax.fori_loop(t, t + 1, first_back, 0)
        if t % 2:
            stop()
    exchange_sent(3)
    if not dm.inside:
        back_start(1, m.gind)

    if dm.inside:
        for off in range(1, T):
            zt = lax.rem(me_z + off, T)
            small(m.m2s.at[zt], m.m2r.at[off - 1], S_M2 + off - 1, z_dev(off)).wait_send()
        for p in range(NC):
            d = pl.multiple_of((2 * p + core) * R, R)
            rows = [sums[j : j + 1, pl.ds(d, R)] for j in range(8)]
            m.m2s[p] = jnp.broadcast_to(jnp.concatenate(rows, axis=-1), (8, 8 * R))
        for k in range(1, NC):
            small(m.m2s.at[lax.rem(chip + k, NC)], m.b1r.at[k - 1], S_B1 + k - 1, chip_dev(k)).start()
        stop()
        stop()
        for k in range(1, NC):
            small(m.m2s.at[0], m.b1r.at[k - 1], S_B1 + k - 1, chip_dev(k)).wait_recv()
        row8 = lax.broadcasted_iota(jnp.int32, (8, 1), 0)
        packed = jnp.where(row8 == chip, m.m2s[chip], 0.0)
        for k in range(1, NC):
            packed = jnp.where(row8 == lax.rem(chip - k + NC, NC), m.b1r[k - 1], packed)
        m.dmodf[me_z] = packed
        for off in range(1, T):
            small(m.dmodf.at[me_z], m.dmodf.at[me_z], S_B2 + off - 1, z_dev(off)).start()
        stop()
        for off in range(1, T):
            small(m.pks.at[0], m.pkr.at[off - 1], S_PZ + off - 1, z_dev(off)).wait_recv()
        m.pka[0] = m.pks[me_z] + sum(m.pkr[k] for k in range(T - 1))
        if NB:
            sum_step(m.pka, m.pkb, 0, S_PB, 0).start()
        for off in range(1, T):
            got = m.dmodf.at[lax.rem(me_z - off + T, T)]
            small(got, got, S_B2 + off - 1, z_dev(off)).wait_recv()
        width = D // T
        for zz in range(T):
            acc = 0.0
            for j in range(8):
                m.dmod[j, 8 * zz : 8 * zz + 8, :] = m.dmodf[zz, :, j * R : (j + 1) * R]
            for j in range(6):
                acc = acc + dot_nt(m.dmodf[zz, :, j * R : (j + 1) * R].astype(B16), m.wada[j])
            m.macc[0, 0:8, zz * width : (zz + 1) * width] = acc
        sum_step(m.macc, m.mrec, 0, S_B3, 1, 8).start()
        for i in range(NB + 1):
            if i < NB:
                sum_finish(m.pka, m.pkb, i, S_PB, 0)
                if i + 1 < NB:
                    sum_step(m.pka, m.pkb, i + 1, S_PB, 0).start()
            if i == NB:
                m.pk[core] = m.pka[NB]
                small(m.pka.at[NB], m.pk.at[core], S_PC, partner).start()
            sum_finish(m.macc, m.mrec, i, S_B3, 1, 8)
            if i < NB:
                sum_step(m.macc, m.mrec, i + 1, S_B3, 1, 8).start()
            stop()
        for zz in range(T):
            m.dsil[8 * zz : 8 * zz + 8, :] = m.macc[NB + 1, 0:8, zz * width : (zz + 1) * width]
    while (NP - 1, NB) in events:
        pump(1)
    if dm.inside:
        back_start(1, m.gind)
    pump(len(events))
    assert not events
    rs_end()
    tok_sent(0, m.xb, xs)
    back_wait(0, m.outd)
    back_wait(1, m.gind)
    sid_copy.wait_send()
    if dm.inside:
        for i in range(NB + 1):
            sum_step(m.macc, m.mrec, i, S_B3, 1, 8).wait_send()
        for i in range(NB):
            sum_step(m.pka, m.pkb, i, S_PB, 0).wait_send()
        for off in range(1, T):
            zt = lax.rem(me_z + off, T)
            small(m.sm.at[me_z], m.sm.at[me_z], S_SM + off - 1, z_dev(off)).wait_send()
            small(m.pks.at[zt], m.pkr.at[off - 1], S_PZ + off - 1, z_dev(off)).wait_send()
            small(m.dmodf.at[me_z], m.dmodf.at[me_z], S_B2 + off - 1, z_dev(off)).wait_send()
        for k in range(1, NC):
            small(m.m3c.at[core, chip], m.m3c.at[core, chip], S_M3 + k - 1, chip_dev(k)).wait_send()
            small(m.m2s.at[lax.rem(chip + k, NC)], m.b1r.at[k - 1], S_B1 + k - 1, chip_dev(k)).wait_send()
        small(m.m3c.at[core], m.m3c.at[core], S_M4, partner).wait_send()
        small(m.pka.at[NB], m.pk.at[core], S_PC, partner).wait_send()
        got = m.pk.at[1 - core]
        small(got, got, S_PC, partner).wait_recv()


def block_call(dm, weights, xb, dyb, sid, extra):
    T, NC, NB, Q, M, D, R, C, W = dm.T, dm.NC, dm.bits, dm.Q, dm.M, dm.D, dm.R, dm.C, dm.W
    hq, fu, NCH, half = dm.hq, dm.fu, dm.NCH, dm.half
    TH, NP = T // 2, len(dm.pieces)
    two = (2,) * NB
    v = pltpu.VMEM
    dma = pltpu.SemaphoreType.DMA
    any_, vm = pl.BlockSpec(memory_space=pl.ANY), pl.BlockSpec(memory_space=pltpu.VMEM)
    s = jax.ShapeDtypeStruct
    tok, heads, acc = (T, Q, D), (T, M, hq), (NCH, M, CHUNK)
    ins = {**weights, "xb": xb, "dyb": dyb, "sid": sid, **extra}
    outs = {"g_qkv": s((3, R, 2 * hq), F32), "g_proj": s((2 * hq, R), F32), "g_up": s((R, 2 * fu), F32), "g_down": s((2 * fu, R), F32), "outd": s((2, Q, D), B16), "gind": s((2, Q, D), B16)}
    totals = {"sums": (8, D), "hsum": (T, 8, hq), "fsum": (T, 8, fu)}
    scratch = {"wall": v((T,) + two + (2 * R, C), B16)}
    for name in "xs dys h1 h2 ab n2 df".split():
        scratch[name] = v(tok, B16)
    for name in "qs ks vs rq rk o ol do".split():
        scratch[name] = v(heads, B16)
    scratch.update(
        r2=v((T, Q, 128), F32), psi=v((M, 128), B16), phi=v((M, 128), B16), sidr=v((8, M), F32),
        gk=v((T, M, half), B16), duk=v((T, M, half), B16), facc=v(acc, F32), dacc=v(acc, F32),
        send=v((NCH, M, CHUNK), B16), recv=v((2, NCH, M, CHUNK), B16),
        xt=v((D, M), B16), xt2=v((D, M), B16), dqkv=v((M, 3 * hq), B16),
        zb=v((T - 1, 2 * R, C), B16), zx=v((2 * R, C), B16), fbuf=v((FINS, R, half), F32), fturn=v((2, half, R), F32),
    )
    for k in range(NB):
        scratch[f"rf{k}"] = v((2,) + (2,) * (NB - 1 - k) + (2 * R, half // 2), B16)
        scratch[f"rb{k}"] = v((SLOTS, 2, TH) + (2,) * (NB - 1 - k) + (2 * R, half), B16)
    if dm.inside:
        outs.update(dmod=s((8, 8 * T, R), F32), cond=s((8 * T, D // T), F32), dsil=s((8 * T, D // T), F32), pk=s((2, 8, W), F32))
        scratch.update({name: v(shape, F32) for name, shape in totals.items()})
        scratch.update(
            dmodf=v((T, 8, 8 * R), F32), mods=v((8, D), F32), hp=v((T, 8, hq), F32), hb=v((T, 8, fu), F32),
            macc=v((NB + 2, 16, D), F32), mrec=v((NB + 1, 16, D), F32), sm=v((T, 8, D), F32),
            m2s=v((T, 8, 8 * R), F32), m2r=v((T - 1, 8, 8 * R), F32), m3c=v((2, NC, 8, 8 * R), F32),
            b1r=v((max(NC - 1, 1), 8, 8 * R), F32),
            pks=v((T, 8, W), F32), pkr=v((T - 1, 8, W), F32), pka=v((NB + 1, 8, W), F32), pkb=v((max(NB, 1), 8, W), F32),
        )
    else:
        outs.update({name: s(shape, F32) for name, shape in totals.items()})
    small = 4 * NB + 6 * T + 2 * NC + 8
    reg = pltpu.SemaphoreType.REGULAR
    scratch.update(
        c_s=dma((NP,)), c_r=dma((NP,)), c_l=dma((NP,)), z_s=dma((NP, T - 1)), z_r=dma((NP, T - 1)),
        p_s=dma((NP, NB, 2)), p_r=dma((NP, NB, 2)), x_s=dma((2, 2)), x_r=dma((2, T)), x_l=dma((2,)), x_f=dma((2, 2)),
        e_s=dma((4, NCH)), e_r=dma((4, NCH)), rs_s=dma((NP, NB, 2)), rs_r=dma((NP, NB, 2)), free=reg((NB, 2)), took=reg,
        rz_s=dma((NP, T - 1, NC)), rz_r=dma((NP, T - 1, NC)), rx_s=dma((NP, NC)), rx_r=dma((NP, NC)), zfree=reg, f_s=dma((NP,)), f_r=dma((NP,)), z_f=dma((NP,)),
        o_s=dma((2, T)), o_r=dma((2, 2)), o_l=dma((2,)), s_s=dma((small,)), s_r=dma((small,)),
    )
    names = tuple(ins) + tuple(outs) + tuple(scratch)
    got = pl.pallas_call(
        functools.partial(block_kernel, dm, names),
        out_shape=tuple(outs.values()),
        in_specs=[any_ if name in ("wqkv", "wup", "xb", "dyb") else vm for name in ins],
        out_specs=tuple(any_ if name in ("outd", "gind") else vm for name in outs),
        scratch_shapes=list(scratch.values()),
        compiler_params=pltpu.CompilerParams(
            collective_id=0, has_side_effects=True, vmem_limit_bytes=66 * 1024 * 1024
        ),
        cost_estimate=pl.CostEstimate(flops=30 * 10**9, bytes_accessed=10**7, transcendentals=10**7),
    )(*ins.values())
    return dict(zip(outs, got))


def local(
    dp, tensor,
    block_input, cotangent, class_ids, scale_ids, class_table, w_ada, b_ada, query_key_value_weight,
    qv_bias, q_gain, output_projection, up_weight, hidden_bias, down_weight, projection_bias,
):
    seqs, quarter, width = block_input.shape
    length = scale_ids.shape[1]
    assert seqs == 2 and tensor == 4
    rows = -(-quarter // 16) * 16
    head = q_gain.shape[1] * dp
    hidden = up_weight.shape[1] * tensor
    dm = Dims(dp, tensor, rows, width, head, hidden)
    T, R, hq, fu, NC, M = dm.T, dm.R, dm.hq, dm.fu, dm.NC, dm.M
    total = class_ids.shape[0]
    di, zi = lax.axis_index("dp"), lax.axis_index("tensor")
    core = di % 2

    pad_rows = ((0, 0), (0, 0), (0, rows - quarter))
    sid = jnp.pad(scale_ids.astype(F32).reshape(2, T, quarter), pad_rows, constant_values=127.0).reshape(2, M)
    sid = jnp.pad(sid, ((0, 6), (0, 0)))
    my_rows = class_table.shape[0]
    my_ids = di * my_rows + jnp.arange(my_rows, dtype=jnp.int32)

    if dm.inside:
        place = jnp.arange(dp, dtype=jnp.int32) == di

        def spread(w):
            return jnp.where(place[:, None], w[..., None, :], 0).reshape(w.shape[:-2] + (-1,)).astype(F32)

        def pad_lanes(w):
            return jnp.pad(w, ((0, 0), (0, width - w.shape[1])))

        hot = (class_ids[:, None] == my_ids[None, :]).astype(B16)
        cond = jnp.dot(hot, class_table, preferred_element_type=F32).reshape(NC, -1)
        tiny = [spread(hidden_bias)[None], spread(qv_bias), spread(q_gain)[None]]
        tiny = jnp.concatenate([pad_lanes(w) for w in tiny], axis=0)
        m1 = jnp.concatenate([jnp.pad(cond, ((0, 8 - NC), (0, 0))), jnp.pad(tiny, ((0, 4), (0, 0)))], axis=0)
        badd = jnp.concatenate([b_ada, projection_bias], axis=0).astype(F32).reshape(1, -1)
        extra = {"m1": m1, "wada": jnp.moveaxis(w_ada, 1, 0), "badd": badd}
    else:
        hot = (class_ids[:, None] == my_ids[None, :]).astype(B16)
        cond = lax.psum(jnp.dot(hot, class_table, preferred_element_type=F32), "dp")
        silu, silu_back = jax.vjp(jax.nn.silu, cond)
        silu_low = silu.astype(B16)
        parts = jnp.einsum("sc,cjd->sjd", silu_low, w_ada, preferred_element_type=F32)
        parts = parts.reshape((NC, T) + parts.shape[1:])
        mine = lax.psum_scatter(parts, "tensor", scatter_dimension=1, tiled=True)[:, 0] + b_ada.astype(F32)
        spread = lax.all_to_all(jnp.repeat(mine, 2, axis=0), "dp", 0, 0, tiled=True)
        modulation = jnp.moveaxis(spread, 0, 1).reshape(6, width)

        pieces = [qv_bias, q_gain, hidden_bias, projection_bias]
        flat = jnp.concatenate([p.reshape(-1) for p in pieces])
        everyone = lax.all_gather(lax.all_gather(flat, "tensor"), "dp")
        cut, at = [], 0
        for p in pieces:
            cut.append(everyone[:, :, at : at + p.size].reshape((dp, T) + p.shape).astype(F32))
            at += p.size
        qv_all = cut[0].transpose(2, 1, 3, 0, 4).reshape(2, T, 2, hq)[:, :, core]
        gain_all = cut[1].transpose(1, 2, 0, 3).reshape(T, 2, hq)[:, core]
        hidden_all = cut[2].transpose(1, 2, 0, 3).reshape(T, 2, fu)[:, core]
        out_bias = cut[3][:, 0].transpose(1, 0, 2).reshape(2, width)
        mods = jnp.concatenate([modulation, out_bias], axis=0)
        hp = jnp.stack([qv_all[0], qv_all[1], gain_all, 1.0 / gain_all], axis=1)
        hp = jnp.concatenate([hp, jnp.zeros_like(hp)], axis=1)
        hb = jnp.broadcast_to(hidden_all[:, None], (T, 8, fu))

        extra = {"mods": mods, "hp": hp, "hb": hb}

    weights = {"wqkv": query_key_value_weight, "wup": up_weight, "wproj": output_projection, "wdown": down_weight}
    pad = ((0, 0), (0, rows - quarter), (0, 0))
    xb = jnp.pad(block_input.astype(B16), pad)
    dyb = jnp.pad(cotangent.astype(B16), pad)

    got = block_call(dm, weights, xb, dyb, sid, extra)
    outd, gind = got["outd"], got["gind"]

    outermost = Layout(major_to_minor=(0, 1, 2))

    def added(base, step):
        step = with_layout_constraint(jnp.swapaxes(step, 0, 1), outermost)
        out = with_layout_constraint(jnp.swapaxes(base, 0, 1) + step[:quarter].astype(F32), outermost)
        return jnp.swapaxes(out, 0, 1)

    block_output, input_grad = added(block_input, outd), added(cotangent, gind)

    w_qkv_grad, w_proj_grad, w_fc1_grad, w_fc2_grad = (got[name] for name in ("g_qkv", "g_proj", "g_up", "g_down"))

    if dm.inside:
        silu, silu_back = jax.vjp(jax.nn.silu, got["cond"])
        dmod = got["dmod"][:6].astype(B16)
        b_ada_grad = jnp.sum(dmod.astype(F32), axis=1)
        w_ada_grad = jnp.einsum("sc,jsd->cjd", silu.astype(B16), dmod, preferred_element_type=F32)
        (d_cond,) = silu_back(got["dsil"])
        ids = jnp.pad(class_ids.reshape(NC, T).T, ((0, 0), (0, 8 - NC)), constant_values=-1).reshape(-1)
        hot = ids[:, None] == my_ids[None, :]
        pk = got["pk"]

        def own(w, n):
            return lax.dynamic_slice_in_dim(w, di * n, n, w.ndim - 1)

        heads = own(jnp.swapaxes(pk[:, :3, :hq], 0, 1).reshape(3, -1, head), head // dp)
        qv_bias_grad, q_gain_grad = heads[:2], heads[2]
        b_fc1_grad = own(pk[:, 0, hq : hq + fu].reshape(hidden_bias.shape[0], -1), hidden_bias.shape[1])
        b_out_grad = lax.dynamic_slice(pk, (0, 6, hq + fu + di * R), (1, 2, R))[0]
    else:
        sums, hsum, fsum = got["sums"], got["hsum"], got["fsum"]
        dmod = sums[:6].reshape(6, dp, R).astype(B16)
        dmod = lax.all_to_all(jnp.moveaxis(dmod, 1, 0), "dp", 0, 0, tiled=True)
        dmod = lax.all_gather(dmod[::2], "tensor", axis=1)
        dmod = dmod.reshape((total, 6, R))
        b_ada_grad = jnp.sum(dmod.astype(F32), axis=0)
        w_ada_grad = jnp.einsum("sc,sjd->cjd", silu_low, dmod, preferred_element_type=F32)
        d_silu = lax.psum(jnp.einsum("sjd,cjd->sc", dmod, w_ada, preferred_element_type=F32), "dp")
        (d_cond,) = silu_back(d_silu)

        vec = jnp.concatenate([hsum[:, :3].reshape(-1), fsum[:, 0].reshape(-1), sums[6:].reshape(-1) * 0.5])
        nh, nf = T * 3 * hq, T * fu
        place_ = jnp.arange(2, dtype=jnp.int32) == core
        by_core = jnp.where(place_[:, None], vec[None, : nh + nf], 0.0).reshape(-1)
        vec = lax.psum(jnp.concatenate([by_core, vec[nh + nf :]]), ("dp", "tensor"))
        by_core = vec[: 2 * (nh + nf)].reshape(2, nh + nf)
        heads = by_core[:, :nh].reshape(2, T, 3, hq)
        heads = lax.dynamic_index_in_dim(heads, zi, 1, keepdims=False)
        heads = jnp.moveaxis(heads, 0, 1).reshape(3, -1, head)
        step = head // dp
        heads = lax.dynamic_slice_in_dim(heads, di * step, step, 2)
        qv_bias_grad, q_gain_grad = heads[:2], heads[2]
        fc1 = lax.dynamic_index_in_dim(by_core[:, nh:].reshape(2, T, fu), zi, 1, keepdims=False)
        fc1 = fc1.reshape(-1, hidden_bias.shape[1] * dp)
        step = hidden_bias.shape[1]
        b_fc1_grad = lax.dynamic_slice_in_dim(fc1, di * step, step, 1)
        b_out_grad = lax.dynamic_slice_in_dim(vec[2 * (nh + nf) :].reshape(2, width), di * R, R, 1)

    table_grad = jnp.dot(hot.astype(F32).T, d_cond, precision=lax.Precision.HIGHEST, preferred_element_type=F32)

    return (
        block_output, input_grad, table_grad, w_ada_grad, b_ada_grad, w_qkv_grad, qv_bias_grad, q_gain_grad,
        w_proj_grad, w_fc1_grad, b_fc1_grad, w_fc2_grad, b_out_grad,
    )


def solution(mesh):
    dp, tensor = mesh.shape["dp"], mesh.shape["tensor"]
    return jax.shard_map(
        functools.partial(local, dp, tensor),
        mesh=mesh,
        in_specs=(
            P("dp", "tensor", None),
            P("dp", "tensor", None),
            P(),
            P("dp", None),
            P("dp", "tensor"),
            P("tensor", None, "dp"),
            P(None, "dp"),
            P(None, "dp", "tensor"),
            P(None, "tensor", "dp"),
            P("tensor", "dp"),
            P("tensor", "dp"),
            P("dp", "tensor"),
            P("tensor", "dp"),
            P("tensor", "dp"),
            P(None, "dp"),
        ),
        out_specs=(
            P("dp", "tensor", None),
            P("dp", "tensor", None),
            P("dp", "tensor"),
            P("tensor", None, "dp"),
            P(None, "dp"),
            P(None, "dp", "tensor"),
            P(None, "tensor", "dp"),
            P("tensor", "dp"),
            P("tensor", "dp"),
            P("dp", "tensor"),
            P("tensor", "dp"),
            P("tensor", "dp"),
            P(None, "dp"),
        ),
        check_vma=False,
    )
```

```python
import functools

import jax
import jax.numpy as jnp
from jax import lax
from jax.experimental import pallas as pl
from jax.experimental.layout import Layout, with_layout_constraint
from jax.experimental.pallas import tpu as pltpu
from jax.sharding import PartitionSpec as P

MESH = pl.DeviceIdType.MESH
F32, B16 = jnp.float32, jnp.bfloat16
FINS = 2
SLOTS = 3
PUMPS = (1, 0, 0, 0, 1, 1, 4, 0, 3, 2, 4, 5, 2, 1)
BEGIN = ((), ((2, 0),), ((1, 0),), ((2, 1), (1, 1), (0, 0), (0, 1)))
LEAN = 2.0
CHUNK = 256
EPS = 1e-06
FAR = 256.0


def dot(a, b):
    return lax.dot_general(a, b, (((1,), (0,)), ((), ())), preferred_element_type=F32)


def dot_nt(a, b):
    return lax.dot_general(a, b, (((1,), (1,)), ((), ())), preferred_element_type=F32)


def dot_tn(a, b):
    return lax.dot_general(a, b, (((0,), (0,)), ((), ())), preferred_element_type=F32)


def split_dot(a, b):
    high = a.astype(B16)
    low = (a - high.astype(F32)).astype(B16)
    return dot(high, b) + dot(low, b)


def row_sum(a):
    return jnp.sum(a, axis=0, keepdims=True)


class Dims:
    def __init__(self, dp, tensor, rows, width, head, hidden):
        self.T = tensor
        self.NC = dp // 2
        self.bits = self.NC.bit_length() - 1
        self.Q = rows
        self.M = rows * tensor
        self.D = width
        self.hd = head
        self.hq = width // tensor // 2
        self.fu = hidden // tensor // 2
        self.R = width // dp
        self.C = 4 * self.hq + 2 * self.fu
        self.NCH = width // CHUNK
        self.inside = self.R % 128 == 0 and self.NC <= tensor and hidden // tensor <= width
        self.W = self.hq + self.fu + width
        hq, fu, half = self.hq, self.fu, self.fu // 2
        up, down = 4 * hq, 4 * hq + fu
        self.up, self.down, self.half = up, down, half
        self.pieces = ((0, hq), (hq, hq), (2 * hq, hq), (3 * hq, hq), (up, half), (down, half), (up + half, half), (down + half, half))
        self.sums_order = (5, 4, 7, 6, 3, 2, 1, 0)
        assert 1 << self.bits == self.NC


class Refs:
    pass


def block_kernel(dm, names, *refs):
    m = Refs()
    for name, ref in zip(names, refs):
        if name[:2] in ("rb", "rf"):
            setattr(m, name[:2], getattr(m, name[:2], []) + [ref])
        else:
            setattr(m, name, ref)
    T, NC, NB, Q, M, D, R, C = dm.T, dm.NC, dm.bits, dm.Q, dm.M, dm.D, dm.R, dm.C
    hq, fu, NCH, half = dm.hq, dm.fu, dm.NCH, dm.half
    TH = T // 2
    NP = len(dm.pieces)
    wall, xs, dys, h1, h2 = m.wall, m.xs, m.dys, m.h1, m.h2
    mods, hp, hb, sums, hsum, fsum = m.mods, m.hp, m.hb, m.sums, m.hsum, m.fsum
    dpi = lax.axis_index("dp")
    me_z = lax.axis_index("tensor")
    core = lax.rem(dpi, 2)
    chip = dpi // 2
    mybit = [lax.rem(chip // (1 << b), 2) for b in range(NB)]
    partner = (dpi + 1 - 2 * core, me_z)

    def tag_z(dev):
        return dev

    def z_dev(off):
        return (dpi, lax.rem(me_z + off, T))

    def bit_dev(b):
        return (dpi + (1 - 2 * mybit[b]) * (2 << b), me_z)

    def chip_dev(k):
        return (lax.rem(chip + k, NC) * 2 + core, me_z)

    bar = pltpu.get_barrier_semaphore()
    friends = [partner] + [z_dev(k) for k in range(1, T)]
    friends += [chip_dev(k) for k in range(1, NC)] if dm.inside else [bit_dev(b) for b in range(NB)]
    for dev in friends:
        pl.semaphore_signal(bar, inc=1, device_id=dev, device_id_type=MESH)
    pl.semaphore_wait(bar, len(friends))

    def rdma(src, dst, ss, rs, dev):
        return pltpu.make_async_remote_copy(
            src_ref=src, dst_ref=dst, send_sem=ss, recv_sem=rs, device_id=dev, device_id_type=MESH
        )

    every = slice(None)

    def place(fixed):
        return tuple(fixed.get(b, every) for b in reversed(range(NB)))

    mine = place({b: mybit[b] for b in range(NB)})

    def cols(pc):
        return pl.ds(*dm.pieces[pc])

    def core_rows(c):
        return pl.ds(pl.multiple_of(c * R, R), R)

    def lanes_of(start, n):
        return pl.ds(pl.multiple_of(start, 128), n)

    def own_weight(pc, c):
        if pc < 3:
            return m.wqkv.at[pc, :, lanes_of(c * hq, hq)]
        if pc == 3:
            return m.gk.at[0, 128 : 128 + R, lanes_of(c * hq, hq)]
        k = (pc - 4) // 2
        if pc % 2 == 0:
            return m.wup.at[:, lanes_of(c * fu + k * half, half)]
        return m.gk.at[2 * c + k, 0:R, :]

    def transpose_own():
        m.gk[0, 128 : 128 + R, :] = m.wproj[...].T
        for i in range(4):
            m.gk[i, 0:R, :] = m.wdown[i * half : (i + 1) * half, :].T

    def core_copy(pc):
        dst = wall.at[(me_z,) + mine + (core_rows(core), cols(pc))]
        return rdma(own_weight(pc, 1 - core), dst, m.c_s.at[pc], m.c_r.at[pc], partner)

    def core_local(pc):
        dst = wall.at[(me_z,) + mine + (core_rows(core), cols(pc))]
        return pltpu.make_async_copy(own_weight(pc, core), dst, m.c_l.at[pc])

    mixed = (NP - 1,) if dm.inside and NB == 2 else ()

    def half_rows(h):
        return pl.ds(h * R, R)

    def z_parts(pc, z):
        if pc not in mixed:
            return [wall.at[(z,) + mine + (every, cols(pc))]]
        known = [place({order[h][1]: mybit[order[h][1]]}) for h in range(2)]
        return [wall.at[(z,) + known[h] + (half_rows(h), cols(pc))] for h in range(2)]

    def z_copies(pc, off):
        parts = z_parts(pc, me_z)
        return [rdma(p, p, m.z_s.at[pc, off - 1, i], m.z_r.at[pc, off - 1, i], z_dev(off)) for i, p in enumerate(parts)]

    def all_do(copies, do):
        for copy in copies:
            getattr(copy, do)()

    order = [list(range(NB)), list(reversed(range(NB)))]

    inner = jnp.logical_and(me_z > 0, me_z < T - 1)
    line_sends = ((2, me_z >= 0), (1, me_z < T - 1), (3, me_z > 0))

    def z_landed(pc, off):
        for i, p in enumerate(z_parts(pc, lax.rem(me_z - off + T, T))):
            rdma(p, p, m.z_s.at[pc, off - 1, i], m.z_r.at[pc, off - 1, i], z_dev(off)).wait_recv()

    def z_forward(pc):
        up = lax.rem(me_z + 1, 2)
        dev = tag_z((dpi, me_z + 2 * up - 1))
        parts = z_parts(pc, lax.rem(me_z + 2, T))
        return [rdma(p, p, m.z_f.at[pc, i], m.z_r.at[pc, 2 * up, i], dev) for i, p in enumerate(parts)]

    def half_z(h):
        return pl.ds(h * TH, TH)

    def p_copy(pc, step, h, landing):
        b = order[h][step]
        fixed = {k: mybit[k] for k in order[h][step:]}
        if landing:
            fixed[b] = 1 - mybit[b]
        if pc in mixed:
            part = wall.at[(every if step else me_z,) + place(fixed) + (half_rows(h), cols(pc))]
        else:
            part = wall.at[(half_z(h),) + place(fixed) + (every, cols(pc))]
        return rdma(part, part, m.p_s.at[pc, step, h], m.p_r.at[pc, step, h], bit_dev(b))

    def z_begin(pc):
        for off, allowed in line_sends:
            @pl.when(allowed)
            def _():
                all_do(z_copies(pc, off), "start")

    def z_pass(pc):
        @pl.when(inner)
        def _():
            z_landed(pc, 2)
            all_do(z_forward(pc), "start")

    def gather_stage(pc, s):
        if not 0 <= pc < NP:
            return
        if s == 0:
            core_local(pc).wait()
            other = wall.at[(me_z,) + mine + (core_rows(1 - core), cols(pc))]
            rdma(other, other, m.c_s.at[pc], m.c_r.at[pc], partner).wait_recv()
            if pc in mixed:
                for h in range(2):
                    p_copy(pc, 0, h, False).start()
            else:
                z_begin(pc)
            return
        if pc in mixed and s < NB:
            if s == -1:
                for h in range(2):
                    p_copy(pc, 0, h, True).wait_recv()
                z_begin(pc)
            else:
                z_pass(pc)
            return
        if s == -1:
            z_pass(pc)
            return
        if s == (NB if pc in mixed else 1):
            z_landed(pc, 1)
            z_landed(pc, 3)

            @pl.when(jnp.logical_not(inner))
            def _():
                z_landed(pc, 2)

            if pc in mixed:
                for h in range(2):
                    p_copy(pc, 1, h, False).start()
                return
        for h in range(2):
            if s > 1:
                p_copy(pc, s - 2, h, True).wait_recv()
            if s <= NB:
                p_copy(pc, s - 1, h, False).start()

    starts = [(pc - 2.2, pc, 0) for pc in range(NP)] + [(pc - 1.1, pc, -1) for pc in range(NP)]
    starts += [(pc + 1.1 * (s - 1), pc, s) for pc in range(NP) for s in range(1, NB + 1)]
    if NB == 2:
        starts[starts.index((4 + 1.1, 4, 2))] = (4.95, 4, 2)
    keys = {0: -3.2, -1: -2.2, 1: 0.06, 2: 1.05}
    starts = [(pc + keys[s], pc, s) if pc in mixed else (key, pc, s) for key, pc, s in starts]
    starts.sort()

    here = [0]

    def gather_to(key):
        while starts and starts[0][0] <= key:
            gather_stage(*starts.pop(0)[1:])

    def gather_until(pc):
        gather_to(pc + 1.1 * NB)
        while here[0] <= pc:
            gather_stage(here[0], NB + 1)
            here[0] += 1

    def gather_sent(which):
        for pc in which:
            for off, allowed in line_sends:
                @pl.when(allowed)
                def _():
                    all_do(z_copies(pc, off), "wait_send")

            @pl.when(inner)
            def _():
                all_do(z_forward(pc), "wait_send")

            for step in range(NB):
                for h in range(2):
                    p_copy(pc, step, h, False).wait_send()

    owner = me_z // 2 == core

    def tok_copy(which, src, dst, i):
        zt = 2 * core + i
        return rdma(src.at[i], dst.at[me_z], m.x_s.at[which, i], m.x_r.at[which, me_z], (dpi, zt))

    def tok_start(which, src, dst):
        for i in range(2):
            @pl.when(2 * core + i != me_z)
            def _():
                tok_copy(which, src, dst, i).start()

            @pl.when(2 * core + i == me_z)
            def _():
                pltpu.make_async_copy(src.at[i], dst.at[me_z], m.x_l.at[which]).start()

    def tok_forward(which, dst):
        return rdma(dst, dst, m.x_f.at[which, 0], m.x_f.at[which, 1], partner)

    def tok_wait(which, src, dst):
        @pl.when(owner)
        def _():
            for off in range(1, T):
                zq = lax.rem(me_z + off, T)
                rdma(dst.at[zq], dst.at[zq], m.x_s.at[which, 0], m.x_r.at[which, zq], (dpi, zq)).wait_recv()
            pltpu.make_async_copy(src.at[0], dst.at[me_z], m.x_l.at[which]).wait()
            tok_forward(which, dst).start()

        @pl.when(jnp.logical_not(owner))
        def _():
            tok_forward(which, dst).wait_recv()

    def tok_sent(which, src, dst):
        for i in range(2):
            @pl.when(2 * core + i != me_z)
            def _():
                tok_copy(which, src, dst, i).wait_send()

        @pl.when(owner)
        def _():
            tok_forward(which, dst).wait_send()

    back_from = (m.n2, m.ab)

    def back_copy(which, dst, zq):
        i = lax.rem(me_z, 2)
        return rdma(back_from[which].at[zq], dst.at[i], m.o_s.at[which, zq], m.o_r.at[which, i], (dpi, zq))

    def back_start(which, dst):
        @pl.when(owner)
        def _():
            for off in range(1, T):
                back_copy(which, dst, lax.rem(me_z + off, T)).start()
            pltpu.make_async_copy(back_from[which].at[me_z], dst.at[lax.rem(me_z, 2)], m.o_l.at[which]).start()

    def back_wait(which, dst):
        @pl.when(owner)
        def _():
            for off in range(1, T):
                back_copy(which, dst, lax.rem(me_z + off, T)).wait_send()
            pltpu.make_async_copy(back_from[which].at[me_z], dst.at[lax.rem(me_z, 2)], m.o_l.at[which]).wait()

        for i in range(2):
            @pl.when(2 * core + i != me_z)
            def _():
                rdma(dst.at[i], dst.at[i], m.o_s.at[which, 0], m.o_r.at[which, i], (dpi, 2 * core + i)).wait_recv()

    def sender(k):
        return m.duk if k == 2 and m.duk.shape == m.send.shape else m.send

    def x_copy(k, n):
        return rdma(sender(k).at[n], m.recv.at[k % 2, n], m.e_s.at[k, n], m.e_r.at[k, n], partner)

    def exchange(k, n, value):
        sender(k)[n] = value.astype(B16)
        x_copy(k, n).start()

    def exchange_wait(k):
        for n in range(NCH):
            x_copy(k, n).wait_recv()

    def exchange_sent(k):
        for n in range(NCH):
            x_copy(k, n).wait_send()

    def both(k, t):
        rows = pl.ds(pl.multiple_of(t * Q, 16), Q)
        parts = [sender(k)[n, rows, :].astype(F32) + m.recv[k % 2, n, rows, :].astype(F32) for n in range(NCH)]
        return jnp.concatenate(parts, axis=-1)

    def wz(z, lo, n):
        return wall[(z,) + (every,) * NB + (every, pl.ds(lo, n))].reshape(D, n)

    def wrows(z, n, lo, width):
        per = CHUNK // (2 * R)
        low = per.bit_length() - 1
        top = n * per
        fixed = {b: (top >> b) & 1 for b in range(low, NB)}
        return wall[(z,) + place(fixed) + (every, pl.ds(lo, width))].reshape(CHUNK, width)

    def wrows_all(n, lo, width):
        return jnp.concatenate([wrows(z, n, lo, width) for z in range(T)], axis=-1)

    def wstore(z, lo, n, value):
        wall[(z,) + (every,) * NB + (every, pl.ds(lo, n))] = value.astype(B16).reshape(
            (2,) * NB + (2 * R, n)
        )

    def all_z(ref):
        return jnp.concatenate([ref[z] for z in range(T)], axis=-1)

    def whole(ref):
        return ref[...].reshape(M, D)

    def mod(r):
        return mods[r : r + 1, :]

    def transpose_into(dst, ref):
        for n in range(D // 128):
            block = ref[:, :, n * 128 : (n + 1) * 128].reshape(M, 128)
            dst[n * 128 : (n + 1) * 128, :] = block.T

    place_of = {pc: j for j, pc in enumerate(dm.sums_order)}

    def rs_fixed(step, h, away):
        order_r = order[h][::-1]
        fixed = {k: mybit[k] for k in order_r[: step + 1]}
        b = order_r[step]
        if away:
            fixed[b] = 1 - mybit[b]
        return b, fixed

    FIRST = 1 if dm.inside else 0

    def rf_copy(step, h):
        lo, width = dm.pieces[dm.sums_order[0]]
        b, fixed = rs_fixed(step, h, True)
        part = wall.at[(me_z,) + place(fixed) + (every, pl.ds(lo + h * (width // 2), width // 2))]
        return rdma(part, m.rf[step].at[h], m.rs_s.at[0, step, h], m.rs_r.at[0, step, h], bit_dev(b))

    def rf_add(step, h):
        rf_copy(step, h).wait_recv()
        lo, width = dm.pieces[dm.sums_order[0]]
        b, fixed = rs_fixed(step, h, False)
        where = (me_z,) + place(fixed) + (every, pl.ds(lo + h * (width // 2), width // 2))
        wall[where] = (wall[where].astype(F32) + m.rf[step][h].astype(F32)).astype(B16)

    def rs_copy(j, step, h):
        pc = dm.sums_order[j]
        b, fixed = rs_fixed(step, h, True)
        part = wall.at[(half_z(h),) + place(fixed) + (every, cols(pc))]
        buf = m.rb[step].at[((j - FIRST) % SLOTS, h) + (every,) * (NB - step) + (every, pl.ds(0, dm.pieces[pc][1]))]
        return rdma(part, buf, m.rs_s.at[j, step, h], m.rs_r.at[j, step, h], bit_dev(b))

    def rs_start(j, step, h):
        if j - FIRST >= SLOTS:
            pl.semaphore_wait(m.free.at[step, h], 1)
        rs_copy(j, step, h).start()

    def rs_add(j, step, h):
        pc = dm.sums_order[j]
        rs_copy(j, step, h).wait_recv()
        b, fixed = rs_fixed(step, h, False)
        rest = [k for k in reversed(range(NB)) if k not in fixed]
        slot, width = (j - FIRST) % SLOTS, dm.pieces[pc][1]

        def one(i, carry):
            zz, r = i // (1 << len(rest)), lax.rem(i, 1 << len(rest))
            at = dict(fixed)
            inner = ()
            for pos, k in enumerate(rest):
                v = lax.rem(r // (1 << (len(rest) - 1 - pos)), 2)
                at[k] = v
                inner += (v,)
            where = (h * TH + zz,) + place(at) + (every, cols(pc))
            got = m.rb[step][(slot, h, zz) + inner + (every, pl.ds(0, width))]
            wall[where] = (wall[where].astype(F32) + got.astype(F32)).astype(B16)
            return carry

        lax.fori_loop(0, TH << len(rest), one, 0)
        if j + SLOTS < NP:
            pl.semaphore_signal(m.free.at[step, h], inc=1, device_id=bit_dev(b), device_id_type=MESH)

    def rz_blocks(j):
        pc = dm.sums_order[j]
        if j >= FIRST:
            return [(mine, cols(pc))]
        width = dm.pieces[pc][1]
        return [(place({b: (p >> b) & 1 for b in range(NB)}), pl.ds(p * width, width)) for p in range(NC)]

    ends_here = jnp.logical_not(inner)

    def rz_copies(j, off):
        pc, out = dm.sums_order[j], []
        for i, (chip_at, at) in enumerate(rz_blocks(j)):
            part = wall.at[(lax.rem(me_z + off, T),) + chip_at + (every, cols(pc))]
            sems = m.rz_s.at[j, off - 1, i], m.rz_r.at[j, off - 1, i]
            out.append(rdma(part, m.zb.at[off - 1, :, at], *sems, z_dev(off)))
        return out

    def rz_specials(j):
        pc, out = dm.sums_order[j], []
        dev = tag_z((dpi, jnp.where(me_z == 0, 1, T - 2)))
        for i, (chip_at, at) in enumerate(rz_blocks(j)):
            part = wall.at[(T - 1 - me_z,) + chip_at + (every, cols(pc))]
            out.append(rdma(part, m.zx.at[:, at], m.rx_s.at[j, i], m.rx_r.at[j, i], dev))
        return out

    def each(copies, do):
        for copy in copies:
            getattr(copy, do)()

    def rz_begin(j):
        if j == FIRST and FIRST:
            pl.semaphore_wait(m.zfree, T - 1)

        @pl.when(ends_here)
        def _():
            each(rz_specials(j), "start")
            each(rz_copies(j, 2), "start")

        for off, allowed in line_sends[1:]:
            @pl.when(allowed)
            def _():
                each(rz_copies(j, off), "start")

    def rz_middle(j):
        pc = dm.sums_order[j]

        @pl.when(inner)
        def _():
            each(rz_specials(j), "wait_recv")
            for chip_at, at in rz_blocks(j):
                where = (lax.rem(me_z + 2, T),) + chip_at + (every, cols(pc))
                wall[where] = (wall[where].astype(F32) + m.zx[:, at].astype(F32)).astype(B16)
            each(rz_copies(j, 2), "start")

    def rz_wait(j):
        each(rz_copies(j, 2), "wait_recv")
        for off, came in ((1, me_z > 0), (3, me_z < T - 1)):
            @pl.when(came)
            def _():
                each(rz_copies(j, off), "wait_recv")

    def rz_sent(j):
        each(rz_copies(j, 2), "wait_send")
        for off, allowed in line_sends[1:]:
            @pl.when(allowed)
            def _():
                each(rz_copies(j, off), "wait_send")

        @pl.when(ends_here)
        def _():
            each(rz_specials(j), "wait_send")

    def final(pc, c):
        if pc < 3:
            return m.g_qkv, (pc, every, lanes_of(c * hq, hq))
        if pc == 3:
            return m.g_proj, (pl.ds(pl.multiple_of(c * hq, hq), hq), every)
        at = c * fu + (pc - 4) // 2 * half
        if pc % 2 == 0:
            return m.g_up, (every, lanes_of(at, half))
        return m.g_down, (pl.ds(pl.multiple_of(at, half), half), every)

    def turned(pc):
        return pc in (3, 5, 7)

    def fin_from(j):
        pc = dm.sums_order[j]
        width = dm.pieces[pc][1]
        if turned(pc):
            return m.fturn, (j // 2 % 2, pl.ds(0, width))
        return m.fbuf, (j % FINS, every, pl.ds(0, width))

    def fin_copy(j):
        pc = dm.sums_order[j]
        ref, at = fin_from(j)
        out, place_ = final(pc, core)
        return rdma(ref.at[at], out.at[place_], m.f_s.at[j], m.f_r.at[j], partner)

    def rz_sum(j, chip_at, at, rows):
        acc = wall[(me_z,) + chip_at + (rows, cols(dm.sums_order[j]))].astype(F32)
        for off in range(1, T):
            acc = acc + m.zb[off - 1, rows, at].astype(F32)
        return acc

    def finish(j, total):
        pc = dm.sums_order[j]
        if j >= FINS:
            fin_copy(j - FINS).wait_send()
        ref, at = fin_from(j)
        out, place_ = final(pc, core)
        away, kept = total(core_rows(1 - core)), total(core_rows(core))
        ref[at] = away.T if turned(pc) else away
        fin_copy(j).start()
        out[place_] = kept.T if turned(pc) else kept

    def rs_event(j, s):
        pc = dm.sums_order[j]
        if j < FIRST:
            if s == 1:
                rz_middle(j)
            elif s == 2:
                rz_wait(j)
                for chip_at, at in rz_blocks(j):
                    wall[(me_z,) + chip_at + (every, cols(pc))] = rz_sum(j, chip_at, at, every).astype(B16)
                for off in range(1, T):
                    pl.semaphore_signal(m.zfree, inc=1, device_id=z_dev(off), device_id_type=MESH)
            if s > 2:
                for h in range(2):
                    rf_add(s - 3, h)
            if 2 <= s < NB + 2:
                for h in range(2):
                    rf_copy(s - 2, h).start()
            if s == NB + 2:
                finish(j, lambda rows: wall[(me_z,) + mine + (rows, cols(pc))].astype(F32))
            return
        if s <= NB:
            for h in range(2):
                rs_add(j, s - 1, h)
                if s < NB:
                    rs_start(j, s, h)
            if s == NB:
                rz_begin(j)
            return
        if s == NB + 1:
            rz_middle(j)
            return
        rz_wait(j)
        finish(j, lambda rows: rz_sum(j, mine, cols(pc), rows))

    events = sorted(((j, s) for j in range(NP) for s in range(1, NB + 3)), key=lambda e: (e[0] + LEAN * e[1], e[0]))
    begun = set()

    def pump(count):
        while count and events and (events[0][0], 1) in begun:
            rs_event(*events.pop(0))
            count -= 1

    stops = list(PUMPS)

    def stop():
        pump(stops.pop(0) if stops else 0)

    def rs_begin(pc, h):
        j = place_of[pc]
        while j - SLOTS >= FIRST and (j - SLOTS, 1) in events:
            pump(1)
        if j >= FIRST:
            rs_start(j, 0, h)
        elif h == 1:
            rz_begin(j)
        begun.add((j, h))

    def rs_end():
        for j in range(NP):
            for step in range(NB):
                for h in range(2):
                    (rs_copy(j, step, h) if j >= FIRST else rf_copy(step, h)).wait_send()
            rz_sent(j)
            fin_copy(j).wait_recv()
            if j + FINS >= NP:
                fin_copy(j).wait_send()

    def small(src, dst, k, dev):
        return rdma(src, dst, m.s_s.at[k], m.s_r.at[k], dev)

    def sum_step(acc, got, i, base, sign, rows=None):
        dev = partner if i < sign else bit_dev(i - sign)
        n = acc.shape[1] if rows is None else rows
        return small(acc.at[i, pl.ds(0, n)], got.at[i, pl.ds(0, n)], base + i, dev)

    def sum_finish(acc, got, i, base, sign, rows=None):
        sum_step(acc, got, i, base, sign, rows).wait_recv()
        n = acc.shape[1] if rows is None else rows
        acc[i + 1, 0:n] = acc[i, 0:n] + got[i, 0:n]

    S_SID = 0
    S_M1 = 1
    S_M2 = S_M1 + NB + 1
    S_SM = S_M2 + T - 1
    S_M3 = S_SM + T - 1
    S_M4 = S_M3 + NC - 1
    S_B1 = S_M4 + 1
    S_B2 = S_B1 + NC - 1
    S_B3 = S_B2 + T - 1
    S_PZ = S_B3 + NB + 1
    S_PB = S_PZ + T - 1
    S_PC = S_PB + NB

    sid_copy = small(m.sid, m.sidr, S_SID, partner)
    sid_copy.start()
    if dm.inside:
        m.macc[0] = m.m1[...]
        sum_step(m.macc, m.mrec, 0, S_M1, 1).start()
    for pc in (0, 1, 2, 4, 6):
        core_copy(pc).start()
        core_local(pc).start()
    gather_to(-1.0)
    transpose_own()
    for pc in (3, 5, 7):
        core_copy(pc).start()
        core_local(pc).start()
    for z, slot in ((0, 0), (T - 1, T - 2)):
        @pl.when(me_z == z)
        def _():
            m.zb[slot] = jnp.zeros(m.zb.shape[1:], B16)

    sums[...] = jnp.zeros_like(sums)
    hsum[...] = jnp.zeros_like(hsum)
    fsum[...] = jnp.zeros_like(fsum)

    if dm.inside:
        for i in range(NB + 1):
            sum_finish(m.macc, m.mrec, i, S_M1, 1)
            if i < NB:
                sum_step(m.macc, m.mrec, i + 1, S_M1, 1).start()
        m.sm[me_z] = m.macc[NB + 1, 8:16, :]
        for off in range(1, T):
            small(m.sm.at[me_z], m.sm.at[me_z], S_SM + off - 1, z_dev(off)).start()
        width = D // T
        for zz in range(T):
            c = m.macc[NB + 1, 0:8, zz * width : (zz + 1) * width]
            m.cond[8 * zz : 8 * zz + 8, :] = c
            low = (c / (1.0 + jnp.exp(-c))).astype(B16)
            rows = [dot(low, m.wada[j]) for j in range(6)] + [jnp.zeros((8, 2 * R), F32)]
            m.m2s[zz] = jnp.concatenate(rows, axis=-1)
        for off in range(1, T):
            small(m.m2s.at[lax.rem(me_z + off, T)], m.m2r.at[off - 1], S_M2 + off - 1, z_dev(off)).start()

    gather_to(1.85)
    tok_start(0, m.xb, xs)

    if dm.inside:
        for off in range(1, T):
            small(m.m2s.at[0], m.m2r.at[off - 1], S_M2 + off - 1, z_dev(off)).wait_recv()
        m.m3c[core, chip] = m.m2s[me_z] + sum(m.m2r[k] for k in range(T - 1)) + m.badd[...]
        own = m.m3c.at[core, chip]
        for k in range(1, NC):
            small(own, own, S_M3 + k - 1, chip_dev(k)).start()
        gather_to(2.15)
        for off in range(1, T):
            got = m.sm.at[lax.rem(me_z - off + T, T)]
            small(got, got, S_SM + off - 1, z_dev(off)).wait_recv()
        head_cols = pl.ds(pl.multiple_of(core * hq, hq), hq)
        for z in range(T):
            for r in range(3):
                hp[z, r : r + 1, :] = m.sm[z, r + 1 : r + 2, head_cols]
            hp[z, 3:4, :] = 1.0 / hp[z, 2:3, :]
            hb[z, 0:1, :] = m.sm[z, 0:1, pl.ds(pl.multiple_of(core * fu, fu), fu)]
        for k in range(1, NC):
            got = m.m3c.at[core, lax.rem(chip - k + NC, NC)]
            small(got, got, S_M3 + k - 1, chip_dev(k)).wait_recv()
        small(m.m3c.at[core], m.m3c.at[core], S_M4, partner).start()

    got = small(m.sidr, m.sidr, S_SID, partner)
    got.wait_recv()
    pick = lax.rem(me_z, 2)
    ids = jnp.where(owner, m.sid[pl.ds(pick, 1), :], m.sidr[pl.ds(pick, 1), :])
    lanes = lax.broadcasted_iota(jnp.int32, (128, 1), 0).astype(F32)
    m.psi[...] = jnp.where(lanes > ids, FAR, 0.0).astype(B16).T
    m.phi[...] = jnp.where(lanes == ids, -1.0, 0.0).astype(B16).T

    if dm.inside:
        got = m.m3c.at[1 - core]
        small(got, got, S_M4, partner).wait_recv()
        for c in range(2):
            for p in range(NC):
                row = m.m3c[c, p, pl.ds(chip, 1), :]
                d = 2 * p + c
                for j in range(8):
                    mods[j : j + 1, d * R : (d + 1) * R] = row[:, j * R : (j + 1) * R]

    gather_to(4.1)
    tok_wait(0, m.xb, xs)

    def ln(rows):
        centred = rows - jnp.mean(rows, axis=-1, keepdims=True)
        inv = lax.rsqrt(jnp.mean(centred * centred, axis=-1, keepdims=True) + EPS)
        return centred * inv, inv

    def first_norm(t, carry):
        normed, _ = ln(xs[t].astype(F32))
        h1[t] = (normed * (1.0 + mod(2)) + mod(4)).astype(B16)
        return carry

    lax.fori_loop(0, T, first_norm, 0)
    gather_to(4.96)
    if dm.inside:
        for i in range(NB + 1):
            sum_step(m.macc, m.mrec, i, S_M1, 1).wait_send()
    gather_until(2)

    lane = lax.broadcasted_iota(jnp.int32, (1, hq), 1)
    halves = [(lane // dm.hd) == k for k in range(hq // dm.hd)]
    bi = lax.broadcasted_iota(jnp.int32, (hq, hq), 0) // dm.hd
    bj = lax.broadcasted_iota(jnp.int32, (hq, hq), 1) // dm.hd
    same_head = (bi == bj).astype(B16)

    def qkv(z, carry):
        t = dot(whole(h1), wz(z, 0, 3 * hq))
        q = t[:, :hq] + hp[z, 0:1, :]
        k = t[:, hq : 2 * hq]
        v = t[:, 2 * hq :] + hp[z, 1:2, :]
        qi = lax.rsqrt(split_dot(q * q, same_head) + EPS)
        ki = lax.rsqrt(split_dot(k * k, same_head) + EPS)
        m.qs[z] = (q * qi * hp[z, 2:3, :]).astype(B16)
        m.ks[z] = (k * ki).astype(B16)
        m.vs[z] = v.astype(B16)
        m.rq[z] = qi.astype(B16)
        m.rk[z] = ki.astype(B16)
        return carry

    lax.fori_loop(0, T, qkv, 0)
    zero16 = jnp.zeros((), B16)

    def expo(z, k, q_all, k_all, rows=slice(None)):
        q_one = jnp.where(halves[k], q_all[rows], zero16)
        left = jnp.concatenate([q_one, m.psi[rows, :]], axis=1)
        right = jnp.concatenate([k_all, m.phi[...]], axis=1)
        return q_one, jnp.exp(dot_nt(left, right))

    def attend(z, carry):
        q_all, k_all, v_all = m.qs[z], m.ks[z], m.vs[z]
        v_ones = jnp.concatenate([v_all, jnp.ones((M, hq), B16)], axis=1)
        mixed = inverse = None
        for k in range(hq // dm.hd):
            _, e = expo(z, k, q_all, k_all)
            both_ = dot(e.astype(B16), v_ones)
            inv = 1.0 / both_[:, hq:]
            one = both_[:, :hq] * inv
            mixed = one if mixed is None else jnp.where(halves[k], one, mixed)
            inverse = inv if inverse is None else jnp.where(halves[k], inv, inverse)
        m.o[z] = mixed.astype(B16)
        m.ol[z] = (mixed - mixed.astype(B16).astype(F32)).astype(B16)
        m.do[z] = inverse.astype(B16)
        return carry

    gather_to(5.0)
    for z in range(T):
        lax.fori_loop(z, z + 1, attend, 0)
        if z == 1:
            gather_to(5.9)
            tok_start(1, m.dyb, dys)

    gather_until(3)
    o_all = all_z(m.o)
    for n in range(NCH):
        exchange(0, n, dot_nt(o_all, wrows_all(n, 3 * hq, hq)))
    exchange_wait(0)

    def second_norm(t, carry):
        a = both(0, t) + mod(6)
        m.ab[t] = a.astype(B16)
        normed, inv = ln(xs[t].astype(F32) + mod(0) * a)
        h2[t] = (normed * (1.0 + mod(3)) + mod(5)).astype(B16)
        m.n2[t] = normed.astype(B16)
        m.r2[t] = jnp.broadcast_to(inv, (Q, 128))
        return carry

    lax.fori_loop(0, T, second_norm, 0)
    gather_to(7.05)
    exchange_sent(0)
    transpose_into(m.xt, h2)

    def out_grad(t, carry):
        d = (mod(1) * dys[t].astype(F32)).astype(B16)
        m.df[t] = d
        sums[7:8, :] += row_sum(d.astype(F32))
        return carry

    root = 0.7978845608028654

    def hidden(k):
        lo_u, lo_d = dm.up + k * half, dm.down + k * half

        def up(z, carry):
            u = dot(whole(h2), wz(z, lo_u, half)) + hb[z, 0:1, k * half : (k + 1) * half]
            uu = u * u
            th = jnp.tanh(root * u * (1.0 + 0.044715 * uu))
            m.gk[z] = (0.5 * u * (1.0 + th)).astype(B16)
            m.duk[z] = (0.5 * (1.0 + th) + (0.5 * root) * u * (1.0 - th * th) * (1.0 + 0.134145 * uu)).astype(B16)
            return carry

        def down(z, carry):
            dg = dot(whole(m.df), wz(z, lo_d, half))
            du = (dg * m.duk[z].astype(F32)).astype(B16)
            m.duk[z] = du
            fsum[z, 0:1, k * half : (k + 1) * half] = row_sum(du.astype(F32))
            return carry

        gather_until(4 + 2 * k)
        lax.fori_loop(0, T, up, 0)
        if k == 0:
            gather_to(7.15)
            tok_wait(1, m.dyb, dys)
            lax.fori_loop(0, T, out_grad, 0)
            transpose_into(m.xt2, m.df)
        gather_until(5 + 2 * k)
        lax.fori_loop(0, T, down, 0)

    def grads(k, begin):
        lo_u, lo_d = dm.up + k * half, dm.down + k * half

        def down_grad(z, carry):
            wstore(z, lo_d, half, dot(m.xt2[...], m.gk[z]))
            return carry

        def up_grad(z, carry):
            wstore(z, lo_u, half, dot(m.xt[...], m.duk[z]))
            return carry

        for pc, body in ((5 + 2 * k, down_grad), (4 + 2 * k, up_grad)):
            for h in range(2):
                lax.fori_loop(h * TH, (h + 1) * TH, body, 0)
                if pc in begin:
                    rs_begin(pc, h)

    for pc in range(NP):
        core_copy(pc).wait_send()
    hidden(0)
    du_all, g_all = all_z(m.duk), all_z(m.gk)
    for n in range(NCH):
        m.dacc[n] = dot_nt(du_all, wrows_all(n, dm.up, half))
        m.facc[n] = dot_nt(g_all, wrows_all(n, dm.down, half))
    gather_sent((4, 5))
    gather_to(99.0)
    grads(0, (5, 4))
    hidden(1)
    du_all, g_all = all_z(m.duk), all_z(m.gk)
    for n in range(NCH):
        exchange(1, n, m.dacc[n] + dot_nt(du_all, wrows_all(n, dm.up + half, half)))
    for n in range(NCH):
        m.facc[n] = m.facc[n] + dot_nt(g_all, wrows_all(n, dm.down + half, half))
    gather_sent((0, 1, 2, 3, 6, 7))
    grads(1, (7,))
    stop()
    transpose_into(m.xt, h1)
    tok_sent(1, m.dyb, dys)
    exchange_wait(1)
    if sender(2) is not m.send:
        for n in range(NCH):
            exchange(2, n, m.facc[n])

    def ln_back(e, normed, inv):
        return (e - jnp.mean(e, axis=-1, keepdims=True) - normed * jnp.mean(e * normed, axis=-1, keepdims=True)) * inv

    def mid_back(t, carry):
        dh = both(1, t)
        normed = m.n2[t].astype(F32)
        sums[3:4, :] += row_sum(dh * normed)
        sums[5:6, :] += row_sum(dh)
        step_back = ln_back(dh * (1.0 + mod(3)), normed, m.r2[t, :, 0:1])
        h2[t] = step_back.astype(B16)
        dx1 = dys[t].astype(F32) + step_back
        sums[0:1, :] += row_sum(dx1 * m.ab[t].astype(F32))
        da = (mod(0) * dx1).astype(B16)
        m.df[t] = da
        sums[6:7, :] += row_sum(da.astype(F32))
        return carry

    lax.fori_loop(0, T, mid_back, 0)
    pl.semaphore_signal(m.took, inc=1, device_id=partner, device_id_type=MESH)
    stop()
    for h in range(2):
        rs_begin(6, h)
    exchange_sent(1)
    if sender(2) is m.send:
        for n in range(NCH):
            exchange(2, n, m.facc[n])

    def last(t, carry):
        f = both(2, t) + mod(7)
        m.n2[t] = (mod(0) * m.ab[t].astype(F32) + mod(1) * f).astype(B16)
        sums[1:2, :] += row_sum(dys[t].astype(F32) * f)
        return carry

    exchange_wait(2)
    lax.fori_loop(0, T, last, 0)
    exchange_sent(2)
    back_start(0, m.outd)

    w_proj = jnp.concatenate([wz(z, 3 * hq, hq) for z in range(T)], axis=-1)
    do_all = dot(whole(m.df), w_proj).astype(B16)
    for z in range(T):
        m.do[z] = (do_all[:, z * hq : (z + 1) * hq].astype(F32) * m.do[z].astype(F32)).astype(B16)
    transpose_into(m.xt2, m.df)
    dw = dot(m.xt2[...], all_z(m.o))
    for z in range(T):
        wstore(z, 3 * hq, hq, dw[:, z * hq : (z + 1) * hq])
    for h in range(2):
        rs_begin(3, h)
    stop()

    ends = jnp.where(lane < 2, -1.0, 0.0).astype(B16)

    def attend_back(z, carry):
        q_all, k_all, v_all = m.qs[z], m.ks[z], m.vs[z]
        dob = m.do[z]
        prod = dob.astype(F32) * (m.o[z].astype(F32) + m.ol[z].astype(F32))
        v_ends = jnp.concatenate([v_all, jnp.broadcast_to(ends, (M, hq))], axis=1)
        dq = dk = dv = 0.0
        for k in range(hq // dm.hd):
            to_all = (bi == k).astype(B16)
            total = split_dot(prod, to_all)
            high = total.astype(B16)
            low = (total - high.astype(F32)).astype(B16)
            extra = jnp.where(lane == 0, high, jnp.where(lane == 1, low, zero16))
            d_one = jnp.where(halves[k], dob, zero16)
            d_ext = jnp.concatenate([d_one, extra], axis=1)
            k_one = jnp.where(halves[k], k_all, zero16)
            dq_rows = []
            for rows in (slice(0, 256), slice(256, M)):
                q_one, e = expo(z, k, q_all, k_all, rows)
                dp = dot_nt(d_ext[rows], v_ends)
                ds = (e * dp).astype(B16)
                dq_rows.append(dot(ds, k_one))
                dk = dk + dot_tn(ds, q_one)
                dv = dv + dot_tn(e.astype(B16), d_one[rows])
            dq = dq + jnp.concatenate(dq_rows, axis=0)
        gain = hp[z, 2:3, :]
        q_hat = q_all.astype(F32) * hp[z, 3:4, :]
        k_hat = k_all.astype(F32)
        hsum[z, 2:3, :] = row_sum(dq * q_hat)
        eq = dq * gain
        dq = ((eq - q_hat * split_dot(eq * q_hat, same_head)) * m.rq[z].astype(F32)).astype(B16)
        dk = ((dk - k_hat * split_dot(dk * k_hat, same_head)) * m.rk[z].astype(F32)).astype(B16)
        dv = dv.astype(B16)
        hsum[z, 0:1, :] = row_sum(dq.astype(F32))
        hsum[z, 1:2, :] = row_sum(dv.astype(F32))
        m.dqkv[...] = jnp.concatenate([dq, dk, dv], axis=1)
        return carry

    for z in range(T):
        lax.fori_loop(z, z + 1, attend_back, 0)
        if z == T - 1:
            pl.semaphore_wait(m.took, 1)
        d_one_z = m.dqkv[...]
        for n in range(NCH):
            part = dot_nt(d_one_z, wrows(z, n, 0, 3 * hq))
            if z == T - 1:
                exchange(3, n, m.facc[n] + part)
            else:
                m.facc[n] = part if z == 0 else m.facc[n] + part
        wstore(z, 0, 3 * hq, dot(m.xt[...], d_one_z))
        for pc, h in BEGIN[z]:
            rs_begin(pc, h)
        stop()

    if dm.inside:
        for z in range(T):
            m.pks[z] = jnp.concatenate([hsum[z], fsum[z], sums[...]], axis=-1)
        for off in range(1, T):
            small(m.pks.at[lax.rem(me_z + off, T)], m.pkr.at[off - 1], S_PZ + off - 1, z_dev(off)).start()
    exchange_wait(3)

    def first_back(t, carry):
        dh = both(3, t)
        normed, inv = ln(xs[t].astype(F32))
        sums[2:3, :] += row_sum(dh * normed)
        sums[4:5, :] += row_sum(dh)
        m.ab[t] = (h2[t].astype(F32) + ln_back(dh * (1.0 + mod(2)), normed, inv)).astype(B16)
        return carry

    for t in range(T):
        lax.fori_loop(t, t + 1, first_back, 0)
        if t % 2:
            stop()
    exchange_sent(3)
    if not dm.inside:
        back_start(1, m.gind)

    if dm.inside:
        for off in range(1, T):
            zt = lax.rem(me_z + off, T)
            small(m.m2s.at[zt], m.m2r.at[off - 1], S_M2 + off - 1, z_dev(off)).wait_send()
        for p in range(NC):
            d = pl.multiple_of((2 * p + core) * R, R)
            rows = [sums[j : j + 1, pl.ds(d, R)] for j in range(8)]
            m.m2s[p] = jnp.broadcast_to(jnp.concatenate(rows, axis=-1), (8, 8 * R))
        for k in range(1, NC):
            small(m.m2s.at[lax.rem(chip + k, NC)], m.b1r.at[k - 1], S_B1 + k - 1, chip_dev(k)).start()
        stop()
        stop()
        for k in range(1, NC):
            small(m.m2s.at[0], m.b1r.at[k - 1], S_B1 + k - 1, chip_dev(k)).wait_recv()
        row8 = lax.broadcasted_iota(jnp.int32, (8, 1), 0)
        packed = jnp.where(row8 == chip, m.m2s[chip], 0.0)
        for k in range(1, NC):
            packed = jnp.where(row8 == lax.rem(chip - k + NC, NC), m.b1r[k - 1], packed)
        m.dmodf[me_z] = packed
        for off in range(1, T):
            small(m.dmodf.at[me_z], m.dmodf.at[me_z], S_B2 + off - 1, z_dev(off)).start()
        stop()
        for off in range(1, T):
            small(m.pks.at[0], m.pkr.at[off - 1], S_PZ + off - 1, z_dev(off)).wait_recv()
        m.pka[0] = m.pks[me_z] + sum(m.pkr[k] for k in range(T - 1))
        if NB:
            sum_step(m.pka, m.pkb, 0, S_PB, 0).start()
        for off in range(1, T):
            got = m.dmodf.at[lax.rem(me_z - off + T, T)]
            small(got, got, S_B2 + off - 1, z_dev(off)).wait_recv()
        width = D // T
        for zz in range(T):
            acc = 0.0
            for j in range(8):
                m.dmod[j, 8 * zz : 8 * zz + 8, :] = m.dmodf[zz, :, j * R : (j + 1) * R]
            for j in range(6):
                acc = acc + dot_nt(m.dmodf[zz, :, j * R : (j + 1) * R].astype(B16), m.wada[j])
            m.macc[0, 0:8, zz * width : (zz + 1) * width] = acc
        sum_step(m.macc, m.mrec, 0, S_B3, 1, 8).start()
        for i in range(NB + 1):
            if i < NB:
                sum_finish(m.pka, m.pkb, i, S_PB, 0)
                if i + 1 < NB:
                    sum_step(m.pka, m.pkb, i + 1, S_PB, 0).start()
            if i == NB:
                m.pk[core] = m.pka[NB]
                small(m.pka.at[NB], m.pk.at[core], S_PC, partner).start()
            sum_finish(m.macc, m.mrec, i, S_B3, 1, 8)
            if i < NB:
                sum_step(m.macc, m.mrec, i + 1, S_B3, 1, 8).start()
            stop()
        for zz in range(T):
            m.dsil[8 * zz : 8 * zz + 8, :] = m.macc[NB + 1, 0:8, zz * width : (zz + 1) * width]
    while (NP - 1, NB) in events:
        pump(1)
    if dm.inside:
        back_start(1, m.gind)
    pump(len(events))
    assert not events
    rs_end()
    tok_sent(0, m.xb, xs)
    back_wait(0, m.outd)
    back_wait(1, m.gind)
    sid_copy.wait_send()
    if dm.inside:
        for i in range(NB + 1):
            sum_step(m.macc, m.mrec, i, S_B3, 1, 8).wait_send()
        for i in range(NB):
            sum_step(m.pka, m.pkb, i, S_PB, 0).wait_send()
        for off in range(1, T):
            zt = lax.rem(me_z + off, T)
            small(m.sm.at[me_z], m.sm.at[me_z], S_SM + off - 1, z_dev(off)).wait_send()
            small(m.pks.at[zt], m.pkr.at[off - 1], S_PZ + off - 1, z_dev(off)).wait_send()
            small(m.dmodf.at[me_z], m.dmodf.at[me_z], S_B2 + off - 1, z_dev(off)).wait_send()
        for k in range(1, NC):
            small(m.m3c.at[core, chip], m.m3c.at[core, chip], S_M3 + k - 1, chip_dev(k)).wait_send()
            small(m.m2s.at[lax.rem(chip + k, NC)], m.b1r.at[k - 1], S_B1 + k - 1, chip_dev(k)).wait_send()
        small(m.m3c.at[core], m.m3c.at[core], S_M4, partner).wait_send()
        small(m.pka.at[NB], m.pk.at[core], S_PC, partner).wait_send()
        got = m.pk.at[1 - core]
        small(got, got, S_PC, partner).wait_recv()


def block_call(dm, weights, xb, dyb, sid, extra):
    T, NC, NB, Q, M, D, R, C, W = dm.T, dm.NC, dm.bits, dm.Q, dm.M, dm.D, dm.R, dm.C, dm.W
    hq, fu, NCH, half = dm.hq, dm.fu, dm.NCH, dm.half
    TH, NP = T // 2, len(dm.pieces)
    two = (2,) * NB
    v = pltpu.VMEM
    dma = pltpu.SemaphoreType.DMA
    any_, vm = pl.BlockSpec(memory_space=pl.ANY), pl.BlockSpec(memory_space=pltpu.VMEM)
    s = jax.ShapeDtypeStruct
    tok, heads, acc = (T, Q, D), (T, M, hq), (NCH, M, CHUNK)
    ins = {**weights, "xb": xb, "dyb": dyb, "sid": sid, **extra}
    outs = {"g_qkv": s((3, R, 2 * hq), F32), "g_proj": s((2 * hq, R), F32), "g_up": s((R, 2 * fu), F32), "g_down": s((2 * fu, R), F32), "outd": s((2, Q, D), B16), "gind": s((2, Q, D), B16)}
    totals = {"sums": (8, D), "hsum": (T, 8, hq), "fsum": (T, 8, fu)}
    scratch = {"wall": v((T,) + two + (2 * R, C), B16)}
    for name in "xs dys h1 h2 ab n2 df".split():
        scratch[name] = v(tok, B16)
    for name in "qs ks vs rq rk o ol do".split():
        scratch[name] = v(heads, B16)
    scratch.update(
        r2=v((T, Q, 128), F32), psi=v((M, 128), B16), phi=v((M, 128), B16), sidr=v((8, M), F32),
        gk=v((T, M, half), B16), duk=v((T, M, half), B16), facc=v(acc, F32), dacc=v(acc, F32),
        send=v((NCH, M, CHUNK), B16), recv=v((2, NCH, M, CHUNK), B16),
        xt=v((D, M), B16), xt2=v((D, M), B16), dqkv=v((M, 3 * hq), B16),
        zb=v((T - 1, 2 * R, C), B16), zx=v((2 * R, C), B16), fbuf=v((FINS, R, half), F32), fturn=v((2, half, R), F32),
    )
    for k in range(NB):
        scratch[f"rf{k}"] = v((2,) + (2,) * (NB - 1 - k) + (2 * R, half // 2), B16)
        scratch[f"rb{k}"] = v((SLOTS, 2, TH) + (2,) * (NB - 1 - k) + (2 * R, half), B16)
    if dm.inside:
        outs.update(dmod=s((8, 8 * T, R), F32), cond=s((8 * T, D // T), F32), dsil=s((8 * T, D // T), F32), pk=s((2, 8, W), F32))
        scratch.update({name: v(shape, F32) for name, shape in totals.items()})
        scratch.update(
            dmodf=v((T, 8, 8 * R), F32), mods=v((8, D), F32), hp=v((T, 8, hq), F32), hb=v((T, 8, fu), F32),
            macc=v((NB + 2, 16, D), F32), mrec=v((NB + 1, 16, D), F32), sm=v((T, 8, D), F32),
            m2s=v((T, 8, 8 * R), F32), m2r=v((T - 1, 8, 8 * R), F32), m3c=v((2, NC, 8, 8 * R), F32),
            b1r=v((max(NC - 1, 1), 8, 8 * R), F32),
            pks=v((T, 8, W), F32), pkr=v((T - 1, 8, W), F32), pka=v((NB + 1, 8, W), F32), pkb=v((max(NB, 1), 8, W), F32),
        )
    else:
        outs.update({name: s(shape, F32) for name, shape in totals.items()})
    small = 4 * NB + 6 * T + 2 * NC + 8
    reg = pltpu.SemaphoreType.REGULAR
    scratch.update(
        c_s=dma((NP,)), c_r=dma((NP,)), c_l=dma((NP,)), z_s=dma((NP, T - 1, 2)), z_r=dma((NP, T - 1, 2)),
        p_s=dma((NP, NB, 2)), p_r=dma((NP, NB, 2)), x_s=dma((2, 2)), x_r=dma((2, T)), x_l=dma((2,)), x_f=dma((2, 2)),
        e_s=dma((4, NCH)), e_r=dma((4, NCH)), rs_s=dma((NP, NB, 2)), rs_r=dma((NP, NB, 2)), free=reg((NB, 2)), took=reg,
        rz_s=dma((NP, T - 1, NC)), rz_r=dma((NP, T - 1, NC)), rx_s=dma((NP, NC)), rx_r=dma((NP, NC)), zfree=reg, f_s=dma((NP,)), f_r=dma((NP,)), z_f=dma((NP, 2)),
        o_s=dma((2, T)), o_r=dma((2, 2)), o_l=dma((2,)), s_s=dma((small,)), s_r=dma((small,)),
    )
    names = tuple(ins) + tuple(outs) + tuple(scratch)
    got = pl.pallas_call(
        functools.partial(block_kernel, dm, names),
        out_shape=tuple(outs.values()),
        in_specs=[any_ if name in ("wqkv", "wup", "xb", "dyb") else vm for name in ins],
        out_specs=tuple(any_ if name in ("outd", "gind") else vm for name in outs),
        scratch_shapes=list(scratch.values()),
        compiler_params=pltpu.CompilerParams(
            collective_id=0, has_side_effects=True, vmem_limit_bytes=66 * 1024 * 1024
        ),
        cost_estimate=pl.CostEstimate(flops=30 * 10**9, bytes_accessed=10**7, transcendentals=10**7),
    )(*ins.values())
    return dict(zip(outs, got))


def local(
    dp, tensor,
    block_input, cotangent, class_ids, scale_ids, class_table, w_ada, b_ada, query_key_value_weight,
    qv_bias, q_gain, output_projection, up_weight, hidden_bias, down_weight, projection_bias,
):
    seqs, quarter, width = block_input.shape
    length = scale_ids.shape[1]
    assert seqs == 2 and tensor == 4
    rows = -(-quarter // 16) * 16
    head = q_gain.shape[1] * dp
    hidden = up_weight.shape[1] * tensor
    dm = Dims(dp, tensor, rows, width, head, hidden)
    T, R, hq, fu, NC, M = dm.T, dm.R, dm.hq, dm.fu, dm.NC, dm.M
    total = class_ids.shape[0]
    di, zi = lax.axis_index("dp"), lax.axis_index("tensor")
    core = di % 2

    pad_rows = ((0, 0), (0, 0), (0, rows - quarter))
    sid = jnp.pad(scale_ids.astype(F32).reshape(2, T, quarter), pad_rows, constant_values=127.0).reshape(2, M)
    sid = jnp.pad(sid, ((0, 6), (0, 0)))
    my_rows = class_table.shape[0]
    my_ids = di * my_rows + jnp.arange(my_rows, dtype=jnp.int32)

    if dm.inside:
        place = jnp.arange(dp, dtype=jnp.int32) == di

        def spread(w):
            return jnp.where(place[:, None], w[..., None, :], 0).reshape(w.shape[:-2] + (-1,)).astype(F32)

        def pad_lanes(w):
            return jnp.pad(w, ((0, 0), (0, width - w.shape[1])))

        hot = (class_ids[:, None] == my_ids[None, :]).astype(B16)
        cond = jnp.dot(hot, class_table, preferred_element_type=F32).reshape(NC, -1)
        tiny = [spread(hidden_bias)[None], spread(qv_bias), spread(q_gain)[None]]
        tiny = jnp.concatenate([pad_lanes(w) for w in tiny], axis=0)
        m1 = jnp.concatenate([jnp.pad(cond, ((0, 8 - NC), (0, 0))), jnp.pad(tiny, ((0, 4), (0, 0)))], axis=0)
        badd = jnp.concatenate([b_ada, projection_bias], axis=0).astype(F32).reshape(1, -1)
        extra = {"m1": m1, "wada": jnp.moveaxis(w_ada, 1, 0), "badd": badd}
    else:
        hot = (class_ids[:, None] == my_ids[None, :]).astype(B16)
        cond = lax.psum(jnp.dot(hot, class_table, preferred_element_type=F32), "dp")
        silu, silu_back = jax.vjp(jax.nn.silu, cond)
        silu_low = silu.astype(B16)
        parts = jnp.einsum("sc,cjd->sjd", silu_low, w_ada, preferred_element_type=F32)
        parts = parts.reshape((NC, T) + parts.shape[1:])
        mine = lax.psum_scatter(parts, "tensor", scatter_dimension=1, tiled=True)[:, 0] + b_ada.astype(F32)
        spread = lax.all_to_all(jnp.repeat(mine, 2, axis=0), "dp", 0, 0, tiled=True)
        modulation = jnp.moveaxis(spread, 0, 1).reshape(6, width)

        pieces = [qv_bias, q_gain, hidden_bias, projection_bias]
        flat = jnp.concatenate([p.reshape(-1) for p in pieces])
        everyone = lax.all_gather(lax.all_gather(flat, "tensor"), "dp")
        cut, at = [], 0
        for p in pieces:
            cut.append(everyone[:, :, at : at + p.size].reshape((dp, T) + p.shape).astype(F32))
            at += p.size
        qv_all = cut[0].transpose(2, 1, 3, 0, 4).reshape(2, T, 2, hq)[:, :, core]
        gain_all = cut[1].transpose(1, 2, 0, 3).reshape(T, 2, hq)[:, core]
        hidden_all = cut[2].transpose(1, 2, 0, 3).reshape(T, 2, fu)[:, core]
        out_bias = cut[3][:, 0].transpose(1, 0, 2).reshape(2, width)
        mods = jnp.concatenate([modulation, out_bias], axis=0)
        hp = jnp.stack([qv_all[0], qv_all[1], gain_all, 1.0 / gain_all], axis=1)
        hp = jnp.concatenate([hp, jnp.zeros_like(hp)], axis=1)
        hb = jnp.broadcast_to(hidden_all[:, None], (T, 8, fu))

        extra = {"mods": mods, "hp": hp, "hb": hb}

    weights = {"wqkv": query_key_value_weight, "wup": up_weight, "wproj": output_projection, "wdown": down_weight}
    pad = ((0, 0), (0, rows - quarter), (0, 0))
    xb = jnp.pad(block_input.astype(B16), pad)
    dyb = jnp.pad(cotangent.astype(B16), pad)

    got = block_call(dm, weights, xb, dyb, sid, extra)
    outd, gind = got["outd"], got["gind"]

    outermost = Layout(major_to_minor=(0, 1, 2))

    def added(base, step):
        step = with_layout_constraint(jnp.swapaxes(step, 0, 1), outermost)
        out = with_layout_constraint(jnp.swapaxes(base, 0, 1) + step[:quarter].astype(F32), outermost)
        return jnp.swapaxes(out, 0, 1)

    block_output, input_grad = added(block_input, outd), added(cotangent, gind)

    w_qkv_grad, w_proj_grad, w_fc1_grad, w_fc2_grad = (got[name] for name in ("g_qkv", "g_proj", "g_up", "g_down"))

    if dm.inside:
        silu, silu_back = jax.vjp(jax.nn.silu, got["cond"])
        dmod = got["dmod"][:6].astype(B16)
        b_ada_grad = jnp.sum(dmod.astype(F32), axis=1)
        w_ada_grad = jnp.einsum("sc,jsd->cjd", silu.astype(B16), dmod, preferred_element_type=F32)
        (d_cond,) = silu_back(got["dsil"])
        ids = jnp.pad(class_ids.reshape(NC, T).T, ((0, 0), (0, 8 - NC)), constant_values=-1).reshape(-1)
        hot = ids[:, None] == my_ids[None, :]
        pk = got["pk"]

        def own(w, n):
            return lax.dynamic_slice_in_dim(w, di * n, n, w.ndim - 1)

        heads = own(jnp.swapaxes(pk[:, :3, :hq], 0, 1).reshape(3, -1, head), head // dp)
        qv_bias_grad, q_gain_grad = heads[:2], heads[2]
        b_fc1_grad = own(pk[:, 0, hq : hq + fu].reshape(hidden_bias.shape[0], -1), hidden_bias.shape[1])
        b_out_grad = lax.dynamic_slice(pk, (0, 6, hq + fu + di * R), (1, 2, R))[0]
    else:
        sums, hsum, fsum = got["sums"], got["hsum"], got["fsum"]
        dmod = sums[:6].reshape(6, dp, R).astype(B16)
        dmod = lax.all_to_all(jnp.moveaxis(dmod, 1, 0), "dp", 0, 0, tiled=True)
        dmod = lax.all_gather(dmod[::2], "tensor", axis=1)
        dmod = dmod.reshape((total, 6, R))
        b_ada_grad = jnp.sum(dmod.astype(F32), axis=0)
        w_ada_grad = jnp.einsum("sc,sjd->cjd", silu_low, dmod, preferred_element_type=F32)
        d_silu = lax.psum(jnp.einsum("sjd,cjd->sc", dmod, w_ada, preferred_element_type=F32), "dp")
        (d_cond,) = silu_back(d_silu)

        vec = jnp.concatenate([hsum[:, :3].reshape(-1), fsum[:, 0].reshape(-1), sums[6:].reshape(-1) * 0.5])
        nh, nf = T * 3 * hq, T * fu
        place_ = jnp.arange(2, dtype=jnp.int32) == core
        by_core = jnp.where(place_[:, None], vec[None, : nh + nf], 0.0).reshape(-1)
        vec = lax.psum(jnp.concatenate([by_core, vec[nh + nf :]]), ("dp", "tensor"))
        by_core = vec[: 2 * (nh + nf)].reshape(2, nh + nf)
        heads = by_core[:, :nh].reshape(2, T, 3, hq)
        heads = lax.dynamic_index_in_dim(heads, zi, 1, keepdims=False)
        heads = jnp.moveaxis(heads, 0, 1).reshape(3, -1, head)
        step = head // dp
        heads = lax.dynamic_slice_in_dim(heads, di * step, step, 2)
        qv_bias_grad, q_gain_grad = heads[:2], heads[2]
        fc1 = lax.dynamic_index_in_dim(by_core[:, nh:].reshape(2, T, fu), zi, 1, keepdims=False)
        fc1 = fc1.reshape(-1, hidden_bias.shape[1] * dp)
        step = hidden_bias.shape[1]
        b_fc1_grad = lax.dynamic_slice_in_dim(fc1, di * step, step, 1)
        b_out_grad = lax.dynamic_slice_in_dim(vec[2 * (nh + nf) :].reshape(2, width), di * R, R, 1)

    table_grad = jnp.dot(hot.astype(F32).T, d_cond, precision=lax.Precision.HIGHEST, preferred_element_type=F32)

    return (
        block_output, input_grad, table_grad, w_ada_grad, b_ada_grad, w_qkv_grad, qv_bias_grad, q_gain_grad,
        w_proj_grad, w_fc1_grad, b_fc1_grad, w_fc2_grad, b_out_grad,
    )


def solution(mesh):
    dp, tensor = mesh.shape["dp"], mesh.shape["tensor"]
    return jax.shard_map(
        functools.partial(local, dp, tensor),
        mesh=mesh,
        in_specs=(
            P("dp", "tensor", None),
            P("dp", "tensor", None),
            P(),
            P("dp", None),
            P("dp", "tensor"),
            P("tensor", None, "dp"),
            P(None, "dp"),
            P(None, "dp", "tensor"),
            P(None, "tensor", "dp"),
            P("tensor", "dp"),
            P("tensor", "dp"),
            P("dp", "tensor"),
            P("tensor", "dp"),
            P("tensor", "dp"),
            P(None, "dp"),
        ),
        out_specs=(
            P("dp", "tensor", None),
            P("dp", "tensor", None),
            P("dp", "tensor"),
            P("tensor", None, "dp"),
            P(None, "dp"),
            P(None, "dp", "tensor"),
            P(None, "tensor", "dp"),
            P("tensor", "dp"),
            P("tensor", "dp"),
            P("dp", "tensor"),
            P("tensor", "dp"),
            P("tensor", "dp"),
            P(None, "dp"),
        ),
        check_vma=False,
    )
```
